32 devices in a mesh: dp: 8 (over z, y), bal: 4 (over x, core).
Axes of the slice: x: 2, y: 2, z: 4, core: 2. Of those that a mesh axis runs over, the one named last changes fastest.
Arguments:
- tokens: bfloat16 [16384, 768], P(('dp', 'bal')), may hold values from -6 to 6
- segment_ids: int32 [32, 512], P(('dp', 'bal')), may hold values from 0 to 3, never falling along the last dimension, each value on 1 to 256 neighbouring positions
- mlm_labels: int32 [16384], P(('dp', 'bal')), may hold values from 0 to 30521
- mask_order: int32 [32, 512], P(('dp', 'bal')), may hold values from 0 to 511, each once within a row
- mask_count: int32 [32], P(('dp', 'bal')), may hold values from 14 to 64, as said below
- qkv_weight: bfloat16 [768, 2304], P(('dp', 'bal')), may hold values from -0.21875 to 0.21875
- query_bias: float32 [768], replicated, may hold values from -3 to 3
- value_bias: float32 [768], replicated, may hold values from -3 to 3
- out_weight: bfloat16 [768, 768], P(('dp', 'bal')), may hold values from -0.875 to 0.875
- out_bias: float32 [768], replicated, may hold values from -2 to 2
- attn_gain: float32 [768], replicated, may hold values from 0.25 to 1.75
- attn_shift: float32 [768], replicated, may hold values from -2 to 2
- up_weight: bfloat16 [768, 3072], P(('dp', 'bal')), may hold values from -0.21875 to 0.21875
- up_bias: float32 [3072], replicated, may hold values from -3 to 3
- down_weight: bfloat16 [3072, 768], P(('dp', 'bal')), may hold values from -0.109375 to 0.109375
- down_bias: float32 [768], replicated, may hold values from -2 to 2
- ffn_gain: float32 [768], replicated, may hold values from 0.25 to 1.75
- ffn_shift: float32 [768], replicated, may hold values from -2 to 2
- head_weight: bfloat16 [768, 768], P(('dp', 'bal')), may hold values from -1 to 1
- head_bias: float32 [768], replicated, may hold values from -3 to 3
- head_gain: float32 [768], replicated, may hold values from 0.25 to 1.75
- head_shift: float32 [768], replicated, may hold values from -2 to 2
- decoder: bfloat16 [768, 30522], P(('dp', 'bal')), may hold values from -0.21875 to 0.21875
- decoder_bias: float32 [30522], replicated, may hold values from -2.5 to 2.5
Outputs:
- layer_out: bfloat16 [16384, 768], P(('dp', 'bal'))
- loss: float32 [], replicated
- tokens_grad: float32 [16384, 768], P(('dp', 'bal'))
- qkv_grad: float32 [768, 2304], P(('dp', 'bal'))
- query_bias_grad: float32 [768], replicated
- value_bias_grad: float32 [768], replicated
- out_grad: float32 [768, 768], P(('dp', 'bal'))
- out_bias_grad: float32 [768], replicated
- attn_gain_grad: float32 [768], replicated
- attn_shift_grad: float32 [768], replicated
- up_grad: float32 [768, 3072], P(('dp', 'bal'))
- up_bias_grad: float32 [3072], replicated
- down_grad: float32 [3072, 768], P(('dp', 'bal'))
- down_bias_grad: float32 [768], replicated
- ffn_gain_grad: float32 [768], replicated
- ffn_shift_grad: float32 [768], replicated
- head_grad: float32 [768, 768], P(('dp', 'bal'))
- head_bias_grad: float32 [768], replicated
- head_gain_grad: float32 [768], replicated
- head_shift_grad: float32 [768], replicated
- decoder_grad: float32 [768, 30522], P(('dp', 'bal'))
- decoder_bias_grad: float32 [30522], replicated
The draws below stay inside these ranges and needn't reach their ends.
Inputs may be any that keep to these rules, and one draw needn't show every extreme that they name: `mask_count`: the 4 counts of one index of dp (consecutive entries) sum to exactly 128; one of them is 64.
All inputs are finite; a program needn't handle non-finite values.
Results may differ from the reference program's by a relative error of at most 0.035.
Values may be sent and summed in bfloat16 or wider, within the bound.
No kernel may reach another device: no remote copies, remote signals or barrier semaphores. Data moves between devices by JAX's collectives and lax.ppermute only.
A program may use at most 384 MiB of HBM per device.

```python
import math
import jax
import jax.numpy as jnp
import numpy as np
from jax import lax

D = 768
HEADS = 12
HDIM = 64
FF = 3072
VOCAB = 30522
SEQ = 512
HEAD_DEV = 32
GROUPS = 8
BALANCE = 4
TOK_DEV = 512
ROWS = 32
TOKENS = 16384
MASK_DEV = 64
DEVICES = 32


def draw_mask_count(key, part):
    key = jax.random.fold_in(key, 7)
    others = BALANCE - 1
    baseline = (BALANCE - 2) * HEAD_DEV // others
    remainder = (BALANCE - 2) * HEAD_DEV - others * baseline
    move_key, order_key = jax.random.split(key)
    transfers = jax.random.randint(move_key, (GROUPS, others), 0, baseline // 3 + 1)
    fixed_first = (jnp.arange(others) == 0).astype(jnp.int32) * (baseline // 3)
    is_free = (jnp.arange(others) >= 2).astype(jnp.int32)
    transfers = transfers * is_free[None, :] + fixed_first[None, :]
    shared = baseline + transfers - jnp.roll(transfers, -1, axis=1)
    shared = shared + (jnp.arange(others) == 0).astype(jnp.int32) * remainder
    device_loads = jnp.concatenate([jnp.full((GROUPS, 1), 2 * HEAD_DEV, jnp.int32), shared.astype(jnp.int32)], axis=1)
    scores = jax.random.randint(order_key, (GROUPS, BALANCE), 0, 1 << 20) * BALANCE + jnp.arange(BALANCE)
    shuffle = jnp.argsort(scores, axis=1, stable=True)
    return jnp.take_along_axis(device_loads, shuffle, axis=1).reshape(GROUPS * BALANCE).astype(jnp.int32)


def draw_head_weight(key, part):
    key = jax.random.fold_in(key, 11)
    base_key, row_key, col_key, spot_key = jax.random.split(key, 4)
    base_part = jnp.clip(jax.random.normal(base_key, (D, D), jnp.float32), -3.0, 3.0)
    factor_rows = jnp.clip(jax.random.normal(row_key, (D,), jnp.float32), -3.0, 3.0)
    factor_cols = jnp.clip(jax.random.normal(col_key, (D,), jnp.float32), -3.0, 3.0)
    strength = 2.0
    spot_draw = jax.random.randint(spot_key, (3,), 0, D // 2)
    position_ids = jnp.arange(D)
    upper_row = spot_draw[0]
    lower_row = D // 2 + spot_draw[1]
    spot_col = spot_draw[2]
    factor_rows = jnp.where(position_ids == upper_row, 4.0, jnp.where(position_ids == lower_row, -4.0, factor_rows))
    factor_cols = jnp.where(position_ids == spot_col, 4.0, factor_cols)
    weight = (base_part + strength * factor_rows[:, None] * factor_cols[None, :]) * D ** (-0.5)
    return jnp.clip(weight, -1.0, 1.0).astype(jnp.bfloat16)


def with_ends(array, key, smallest, largest):
    spot = [jax.random.randint(jax.random.fold_in(key, axis), (), 0, length) for axis, length in enumerate(array.shape)]
    main_axis = array.shape.index(max(array.shape))
    neighbour = spot[:main_axis] + [(spot[main_axis] + 1) % array.shape[main_axis]] + spot[main_axis + 1:]
    return array.at[tuple(spot)].set(smallest).at[tuple(neighbour)].set(largest)


def level_of(own_key, shape, cuts, low, largest):
    gain = 1.0
    for dim, parts in cuts:
        steps = jax.random.uniform(jax.random.fold_in(jax.random.fold_in(own_key, 6), dim), (parts,), jnp.float32, low / len(cuts), largest / len(cuts))
        gain = gain * jnp.repeat(jnp.exp(steps), shape[dim] // parts).reshape((-1,) + (1,) * (len(shape) - 1 - dim))
    return gain


def rank_bounds(number_of, skew):
    portions = [(1 << 20) // math.isqrt(standing ** skew) + 1 for standing in range(1, number_of + 1)]
    scale = 1 + sum(portions) // (1 << 30)
    return np.cumsum(np.array([max(1, weight // scale) for weight in portions]))


def skewed_ids(rng, extent, number_of, skew):
    table = rank_bounds(number_of, skew)
    ticket = jax.random.randint(jax.random.fold_in(rng, 1), extent, 0, int(table[number_of - 1]))
    rank = jnp.searchsorted(jnp.asarray(table, jnp.int32), ticket, side="right")
    return jax.random.permutation(jax.random.fold_in(rng, 2), number_of)[rank].astype(jnp.int32)


def length_profile(count, total, reach, skew):
    portions = [(1 << 20) // math.isqrt(grade ** skew) + 1 for grade in range(2, count + 1)]
    surplus, holding = total - reach - (count - 1), [1] * (count - 1)
    while surplus > 0:
        free = [i for i in range(count - 1) if holding[i] < reach]
        pool, left = sum([portions[i] for i in free]), surplus
        for i in free:
            more = min(reach - holding[i], max(1, left * portions[i] // pool), surplus)
            holding[i] = holding[i] + more
            surplus = surplus - more
    return np.array([reach] + holding)


def uneven(stream_key, amount, total, most, lean):
    if amount == 2:
        one = jax.random.randint(stream_key, (), max(1, total - most), min(most, total - 1) + 1)
        return jnp.stack([one, total - one])
    sizes = jnp.asarray(length_profile(amount, total, most, lean), jnp.int32)
    couples = (amount - 1) // 2
    source_of, sink = sizes[1:1 + 2 * couples:2], sizes[2:2 + 2 * couples:2]
    slack = jnp.minimum(source_of - 1, most - sink)
    shifted = jax.random.randint(jax.random.fold_in(stream_key, 1), (couples,), 0, 1 << 20) % (slack + 1)
    sizes = sizes.at[1:1 + 2 * couples:2].set(source_of - shifted).at[2:2 + 2 * couples:2].set(sink + shifted)
    return sizes[jax.random.permutation(jax.random.fold_in(stream_key, 2), amount)]


def centred(own_key, shape, width, most, cuts=(), kind=jnp.bfloat16):
    gain = level_of(own_key, shape, cuts, -0.22, 0.18) if cuts else 1.0
    values = jax.random.normal(own_key, shape, jnp.float32) * width * gain
    return jnp.minimum(jnp.maximum(values, -most), most).astype(kind)


def setup_inputs(seed: int = 0) -> dict:
    key_list = jax.random.split(jax.random.key(seed), 25)
    return {
        "tokens": centred(key_list[0], (TOKENS, D), 1.0, 6.0, ((0, 32),)),
        "segment_ids": jax.vmap(lambda own: jnp.searchsorted(jnp.cumsum(uneven(own, 4, SEQ, SEQ // 2, 2)), jnp.arange(SEQ), side="right"))(jax.random.split(key_list[1], ROWS)).reshape((ROWS, SEQ)).astype(jnp.int32),
        "mlm_labels": with_ends(skewed_ids(key_list[2], (TOKENS,), VOCAB, 1), jax.random.fold_in(key_list[2], 3), 0, VOCAB - 1).astype(jnp.int32),
        "mask_order": jax.vmap(lambda own: jax.random.permutation(own, TOK_DEV))(jax.random.split(key_list[3], DEVICES)).reshape((DEVICES, TOK_DEV)).astype(jnp.int32),
        "mask_count": draw_mask_count(jax.random.fold_in(key_list[24], 71), 0),
        "qkv_weight": centred(key_list[5], (D, 3 * D), D ** -0.5, 0.21875, ((0, 32),)),
        "query_bias": centred(key_list[6], (D,), 0.5, 3.0, (), jnp.float32),
        "value_bias": centred(key_list[7], (D,), 0.5, 3.0, (), jnp.float32),
        "out_weight": centred(key_list[8], (D, D), (D // 16) ** -0.5, 0.875, ((0, 32),)),
        "out_bias": centred(key_list[9], (D,), 0.3, 2.0, (), jnp.float32),
        "attn_gain": jnp.clip(1.0 + 0.15 * jax.random.normal(key_list[10], (D,), jnp.float32), 0.25, 1.75),
        "attn_shift": centred(key_list[11], (D,), 0.3, 2.0, (), jnp.float32),
        "up_weight": centred(key_list[12], (D, FF), D ** -0.5, 0.21875, ((0, 32),)),
        "up_bias": centred(key_list[13], (FF,), 0.5, 3.0, (), jnp.float32),
        "down_weight": centred(key_list[14], (FF, D), FF ** -0.5, 0.109375, ((0, 32),)),
        "down_bias": centred(key_list[15], (D,), 0.3, 2.0, (), jnp.float32),
        "ffn_gain": jnp.clip(1.0 + 0.15 * jax.random.normal(key_list[16], (D,), jnp.float32), 0.25, 1.75),
        "ffn_shift": centred(key_list[17], (D,), 0.3, 2.0, (), jnp.float32),
        "head_weight": draw_head_weight(jax.random.fold_in(key_list[24], 71), 0),
        "head_bias": centred(key_list[19], (D,), 0.5, 3.0, (), jnp.float32),
        "head_gain": jnp.clip(1.0 + 0.15 * jax.random.normal(key_list[20], (D,), jnp.float32), 0.25, 1.75),
        "head_shift": centred(key_list[21], (D,), 0.3, 2.0, (), jnp.float32),
        "decoder": centred(key_list[22], (D, VOCAB), D ** -0.5, 0.21875, ((0, 32),)),
        "decoder_bias": centred(key_list[23], (VOCAB,), 0.5, 2.5, (), jnp.float32),
    }


PRECISE = lax.Precision.HIGHEST
EPSILON = 1e-06

@jax.custom_vjp
def low(v):
    return lax.optimization_barrier(v.astype(jnp.bfloat16)).astype(jnp.float32)

@jax.custom_vjp
def low_back(v):
    return v

def low_keep(v):
    return (low(v), None)

def low_pass(kept, grad):
    return (grad,)

def back_keep(v):
    return (v, None)

def back_low(kept, grad):
    return (low(grad),)
low.defvjp(low_keep, low_pass)
low_back.defvjp(back_keep, back_low)

def matmul(left_mat, right_mat):
    return jnp.dot(left_mat, right_mat, precision=PRECISE, preferred_element_type=jnp.float32)

def layer_norm(hidden, gain_vec, shift_vec):
    average = lax.optimization_barrier(jnp.mean(hidden, axis=-1, keepdims=True))
    centered = hidden - average
    variance = lax.optimization_barrier(jnp.mean(centered * centered, axis=-1, keepdims=True))
    return centered * lax.rsqrt(variance + EPSILON) * gain_vec + shift_vec

def gelu_exact(values):
    return jax.nn.gelu(values, approximate=False)

def attend_rows(qkv_rows, seg_rows):
    groups = qkv_rows.shape[0]
    seqlen = qkv_rows.shape[1]
    split_heads = qkv_rows.reshape(groups, seqlen, 3, HEADS, HDIM)
    queries = split_heads[:, :, 0]
    key_rows = split_heads[:, :, 1]
    value_rows = split_heads[:, :, 2]
    scores = low_back(jnp.einsum('gqhd,gkhd->ghqk', queries, key_rows, precision=PRECISE) * HDIM ** (-0.5))
    same_seg = seg_rows[:, None, :, None] == seg_rows[:, None, None, :]
    masked = jnp.where(same_seg, scores, -1e+30)
    row_peak = lax.optimization_barrier(jnp.max(masked, axis=-1, keepdims=True))
    exp_scores = jnp.exp(masked - row_peak)
    attn_probs = exp_scores / lax.optimization_barrier(jnp.sum(exp_scores, axis=-1, keepdims=True))
    context = jnp.einsum('ghqk,gkhd->gqhd', low(attn_probs), value_rows, precision=PRECISE)
    return context.reshape(groups * seqlen, HEADS * HDIM)

def layer_group(layer_params, x_rows, seg_rows):
    qkv_weight, query_bias, value_bias, out_weight, out_bias, attn_gain, attn_shift, up_weight, up_bias, down_weight, down_bias, ffn_gain, ffn_shift = layer_params
    groups, seqlen, model_width = x_rows.shape
    flat_rows = x_rows.reshape(groups * seqlen, model_width)
    merged_bias = jnp.concatenate([query_bias, jnp.zeros_like(query_bias), value_bias])
    qkv_rows = low(low_back(matmul(flat_rows, qkv_weight) + merged_bias))
    context = low(low_back(attend_rows(qkv_rows.reshape(groups, seqlen, 3 * model_width), seg_rows)))
    attn_sum = low_back(matmul(context, out_weight) + out_bias)
    normed_one = low(layer_norm(flat_rows + attn_sum, attn_gain, attn_shift))
    up_rows = low_back(matmul(normed_one, up_weight) + up_bias)
    hidden = low(gelu_exact(up_rows))
    down_rows = low_back(matmul(hidden, down_weight) + down_bias)
    output = layer_norm(normed_one + down_rows, ffn_gain, ffn_shift)
    return output.reshape(groups, seqlen, model_width)

def run_layer(layer_params, tokens_in, segment_ids):
    groups = tokens_in.shape[0] // (8 * SEQ)
    x_groups = tokens_in.reshape(groups, 8, SEQ, D)
    seg_groups = segment_ids.reshape(groups, 8, SEQ)

    def scan_step(carried, pieces):
        return (carried, layer_group(layer_params, pieces[0], pieces[1]))
    unused, outputs = lax.scan(jax.checkpoint(scan_step), jnp.float32(0.0), (x_groups, seg_groups))
    return outputs.reshape(groups * 8 * SEQ, D)

def head_loss(head_params, head_in, label_rows, valid_rows):
    head_weight, head_bias, head_gain, head_shift, decoder, decoder_bias = head_params
    inner_rows = low_back(matmul(head_in, head_weight) + head_bias)
    head_normed = low(layer_norm(gelu_exact(inner_rows), head_gain, head_shift))
    logits = low_back(matmul(head_normed, decoder) + decoder_bias)
    row_peak = lax.optimization_barrier(jnp.max(logits, axis=1, keepdims=True))
    log_total = row_peak[:, 0] + jnp.log(lax.optimization_barrier(jnp.sum(jnp.exp(logits - row_peak), axis=1)))
    target = jnp.take_along_axis(logits, label_rows[:, None], axis=1)[:, 0]
    return jnp.sum(jnp.where(valid_rows, log_total - target, 0.0))

def forward(tokens_in, layer_params, head_params, segment_ids, mlm_labels, mask_order, mask_count):
    output = run_layer(layer_params, tokens_in, segment_ids)
    layer_out = low(low_back(output))
    listed = (jnp.arange(DEVICES, dtype=jnp.int32)[:, None] * TOK_DEV + mask_order[:, :MASK_DEV]).astype(jnp.int32)
    listed_flat = listed.reshape(DEVICES * MASK_DEV)
    head_in = jnp.take(layer_out, listed_flat, axis=0).reshape(DEVICES, MASK_DEV, D)
    label_rows = jnp.take(mlm_labels, listed_flat).reshape(DEVICES, MASK_DEV)
    valid_rows = jnp.arange(MASK_DEV, dtype=jnp.int32)[None, :] < mask_count[:, None]

    def head_step(pieces):
        return head_loss(head_params, pieces[0], pieces[1], pieces[2])
    totals = lax.map(jax.checkpoint(head_step), (head_in, label_rows, valid_rows))
    return (jnp.sum(totals) / (DEVICES * HEAD_DEV), layer_out)

def reference(tokens, segment_ids, mlm_labels, mask_order, mask_count, qkv_weight, query_bias, value_bias, out_weight, out_bias, attn_gain, attn_shift, up_weight, up_bias, down_weight, down_bias, ffn_gain, ffn_shift, head_weight, head_bias, head_gain, head_shift, decoder, decoder_bias):
    layer_params = tuple((member.astype(jnp.float32) for member in (qkv_weight, query_bias, value_bias, out_weight, out_bias, attn_gain, attn_shift, up_weight, up_bias, down_weight, down_bias, ffn_gain, ffn_shift)))
    head_params = tuple((member.astype(jnp.float32) for member in (head_weight, head_bias, head_gain, head_shift, decoder, decoder_bias)))
    tokens_in = tokens.astype(jnp.float32)

    def objective(tokens_arg, layer_arg, head_arg):
        return forward(tokens_arg, layer_arg, head_arg, segment_ids, mlm_labels, mask_order, mask_count)
    loss, pullback, layer_out = jax.vjp(objective, tokens_in, layer_params, head_params, has_aux=True)
    tokens_grad, layer_grads, head_grads = pullback(jnp.ones_like(loss))
    return (layer_out.astype(jnp.bfloat16), loss, tokens_grad, layer_grads[0], layer_grads[1], layer_grads[2], layer_grads[3], layer_grads[4], layer_grads[5], layer_grads[6], layer_grads[7], layer_grads[8], layer_grads[9], layer_grads[10], layer_grads[11], layer_grads[12], head_grads[0], head_grads[1], head_grads[2], head_grads[3], head_grads[4], head_grads[5])
```

```python
import jax
import jax.numpy as jnp
from jax import lax
from jax.sharding import PartitionSpec as P

HEADS = 12
HDIM = 64
HEAD_DEV = 32
MASK_DEV = 64


EPSILON = 1e-06
MASK_FILL = -1e30
AXES = ("dp", "bal")
LOW = jnp.bfloat16


def gelu_exact(values):
    return jax.nn.gelu(values, approximate=False)


def product(left_mat, right_mat):
    return jnp.dot(left_mat, right_mat, preferred_element_type=jnp.float32)


def product_tn(left_mat, right_mat):
    return lax.dot_general(
        left_mat, right_mat, (((0,), (0,)), ((), ())), preferred_element_type=jnp.float32
    )


def product_nt(left_mat, right_mat):
    return lax.dot_general(
        left_mat, right_mat, (((1,), (1,)), ((), ())), preferred_element_type=jnp.float32
    )


def pick_exact(onehot, rows):
    return jnp.dot(onehot, rows, precision=lax.Precision.HIGHEST)


def norm_parts(hidden):
    average = jnp.mean(hidden, axis=-1, keepdims=True)
    centered = hidden - average
    inv_std = lax.rsqrt(jnp.mean(centered * centered, axis=-1, keepdims=True) + EPSILON)
    return centered * inv_std, inv_std


def norm_back(normal, inv_std, gain_vec, grad):
    scaled = grad * gain_vec
    first = jnp.mean(scaled, axis=-1, keepdims=True)
    second = jnp.mean(scaled * normal, axis=-1, keepdims=True)
    return (
        inv_std * (scaled - first - normal * second),
        jnp.sum(grad * normal, axis=0),
        jnp.sum(grad, axis=0),
    )


class Grid:
    def __init__(self, dp_size, bal_size):
        self.high = 4 if dp_size % 4 == 0 else 1
        self.low = dp_size // self.high
        self.wide = bal_size // 2
        self.sizes = (self.high, self.low, self.wide, 2)
        self.count = dp_size * bal_size
        dp_place, bal_place = lax.axis_index("dp"), lax.axis_index("bal")
        self.place = (
            dp_place // self.low,
            dp_place % self.low,
            bal_place // 2,
            bal_place % 2,
        )
        self.crossed = self.low == self.wide

    def index(self, spot):
        high, low, wide, core = spot
        return ((high * self.low + low) * self.wide + wide) * 2 + core

    def spots(self):
        for high in range(self.high):
            for low in range(self.low):
                for wide in range(self.wide):
                    for core in range(2):
                        yield (high, low, wide, core)

    def shift(self, value, axis_of, step):
        pairs = []
        for spot in self.spots():
            axis = axis_of[spot[3]]
            target = list(spot)
            target[axis] = (spot[axis] + step) % self.sizes[axis]
            pairs.append((self.index(spot), self.index(target)))
        return lax.ppermute(value, AXES, pairs)

    def own(self, axis_of):
        first, second = self.place[axis_of[0]], self.place[axis_of[1]]
        return first if axis_of[0] == axis_of[1] else jnp.where(self.place[3] == 0, first, second)

    def orders(self):
        return ((1, 2), (2, 1)) if self.crossed else ((1, 1), (2, 2))

    def gather_stage(self, value, axis_of):
        size = self.sizes[axis_of[0]]
        me = self.own(axis_of)
        parts = [value] + [self.shift(value, axis_of, step) for step in range(1, size)]
        rel = (me - jnp.arange(size)) % size
        rel = rel.reshape((size,) + (1,) * value.ndim)
        out = parts[-1][None]
        for step in range(size - 2, -1, -1):
            out = jnp.where(rel == step, parts[step][None], out)
        return out

    def scatter_stage(self, value, axis_of, axis):
        size = self.sizes[axis_of[0]]
        me = self.own(axis_of)

        def piece(step):
            return lax.dynamic_index_in_dim(value, (me + step) % size, axis, keepdims=False)

        total = piece(0).astype(jnp.float32)
        for step in range(1, size):
            total = total + self.shift(piece(step), axis_of, step).astype(jnp.float32)
        return total.astype(value.dtype)

    def gather(self, rows):
        height, width = rows.shape
        half = width // 2
        core = self.place[3]
        keep = lax.dynamic_slice_in_dim(rows, core * half, half, 1)
        give = lax.dynamic_slice_in_dim(rows, (1 - core) * half, half, 1)
        taken = self.shift(give, (3, 3), 1)
        is_own = (jnp.arange(2) == core)[:, None, None]
        part = jnp.where(is_own, keep[None], taken[None])
        part = self.gather_stage(part, (0, 0))
        first, second = self.orders()
        part = self.gather_stage(part, first)
        part = self.gather_stage(part, second)
        straight = part.transpose(2, 1, 0, 3, 4, 5)
        if self.crossed:
            turned = part.transpose(2, 0, 1, 3, 4, 5)
            straight = jnp.where(core == 0, straight, turned)
        mine = straight.reshape(self.count * height, half)
        other = self.shift(mine, (3, 3), 1)
        return jnp.concatenate(
            [jnp.where(core == 0, mine, other), jnp.where(core == 0, other, mine)], axis=1
        )

    def scatter(self, terms):
        total_rows, width = terms.shape
        height = total_rows // self.count
        half = width // 2
        core = self.place[3]
        keep = lax.dynamic_slice_in_dim(terms, core * half, half, 1)
        give = lax.dynamic_slice_in_dim(terms, (1 - core) * half, half, 1)
        taken = self.shift(give, (3, 3), 1)
        part = (keep.astype(jnp.float32) + taken.astype(jnp.float32)).astype(terms.dtype)
        part = part.reshape(self.high, self.low, self.wide, 2, height, half)
        first, second = self.orders()
        if self.crossed:
            part = jnp.where(core == 0, part, part.transpose(0, 2, 1, 3, 4, 5))
        part = self.scatter_stage(part, second, 2)
        part = self.scatter_stage(part, first, 1)
        part = self.scatter_stage(part, (0, 0), 0)
        mine = lax.dynamic_index_in_dim(part, core, 0, keepdims=False)
        away = lax.dynamic_index_in_dim(part, 1 - core, 0, keepdims=False)
        other = self.shift(away, (3, 3), 1)
        return jnp.concatenate(
            [jnp.where(core == 0, mine, other), jnp.where(core == 0, other, mine)], axis=1
        )

    def gather_group(self, rows):
        part = self.gather_stage(rows, (2, 2))
        part = self.gather_stage(part, (3, 3))
        part = part.transpose(1, 0, 2, 3)
        return part.reshape(self.wide * 2 * rows.shape[0], rows.shape[1])

    def total(self, value):
        for axis in (3, 2, 1, 0):
            size = self.sizes[axis]
            moved = [self.shift(value, (axis, axis), step) for step in range(1, size)]
            for piece in moved:
                value = value + piece
        return value


def heads_of(rows):
    return rows.reshape(rows.shape[0], HEADS, HDIM)


def attention_probs(queries, key_rows, query_seg, key_seg):
    scores = jnp.einsum(
        "qhd,khd->hqk", queries, key_rows, preferred_element_type=jnp.float32
    ) * HDIM ** (-0.5)
    same_seg = query_seg[:, None] == key_seg[None, :]
    masked = jnp.where(same_seg[None], scores, MASK_FILL)
    row_peak = jnp.max(masked, axis=-1, keepdims=True)
    exp_scores = jnp.exp(masked - row_peak)
    return exp_scores / jnp.sum(exp_scores, axis=-1, keepdims=True)


def per_device(
    tokens,
    segment_ids,
    mlm_labels,
    mask_order,
    mask_count,
    qkv_weight,
    query_bias,
    value_bias,
    out_weight,
    out_bias,
    attn_gain,
    attn_shift,
    up_weight,
    up_bias,
    down_weight,
    down_bias,
    ffn_gain,
    ffn_shift,
    head_weight,
    head_bias,
    head_gain,
    head_shift,
    decoder,
    decoder_bias,
):
    model_width = tokens.shape[1]
    tok_rows = tokens.shape[0]
    vocab_size = decoder.shape[1]
    bal_size = lax.axis_size("bal")
    dp_size = lax.axis_size("dp")
    bal_place = lax.axis_index("bal")
    dp_place = lax.axis_index("dp")
    grid = Grid(dp_size, bal_size)
    device_count = dp_size * bal_size
    my_place = dp_place * bal_size + bal_place
    group_slots = HEAD_DEV * bal_size
    slot_count = HEAD_DEV * device_count
    inv_count = 1.0 / slot_count
    part_vocab = -(-(-(-vocab_size // device_count)) // 128) * 128
    seg_row = segment_ids[0]

    listed = mask_order[0, :MASK_DEV]
    pick_mat = listed[:, None] == jnp.arange(tok_rows)[None, :]
    listed_ids = jnp.sum(jnp.where(pick_mat, mlm_labels[None, :], 0), axis=1)
    listed_seg = jnp.sum(jnp.where(pick_mat, seg_row[None, :], 0), axis=1)
    info = jnp.concatenate([listed_ids, mask_count, jnp.zeros((63,), jnp.int32)])
    info = jnp.broadcast_to(info[None, None, :], (device_count, 1, 2 * MASK_DEV))
    info = lax.all_to_all(info, AXES, split_axis=0, concat_axis=0, tiled=True)
    info = info.reshape(dp_size, bal_size, 2 * MASK_DEV)
    counts = info[:, :, MASK_DEV]
    starts = jnp.cumsum(counts, axis=1) - counts
    steps = jnp.arange(MASK_DEV)
    slot_of = jnp.where(steps < counts[..., None], starts[..., None] + steps, -1)
    slot_of = slot_of.reshape(dp_size, 1, bal_size * MASK_DEV)
    ids_flat = info[:, :, :MASK_DEV].reshape(dp_size, 1, bal_size * MASK_DEV)
    slot_ids = jnp.arange(group_slots)[None, :, None]
    labels = jnp.sum(jnp.where(slot_of == slot_ids, ids_flat, 0), axis=2).reshape(slot_count)
    group_slot_of = lax.dynamic_index_in_dim(slot_of, dp_place, 0, keepdims=False)
    my_slots = bal_place * HEAD_DEV + jnp.arange(HEAD_DEV)
    to_head = (group_slot_of == my_slots[:, None]).astype(LOW)
    own_slot_of = lax.dynamic_slice_in_dim(group_slot_of[0], bal_place * MASK_DEV, MASK_DEV)
    from_head = (own_slot_of[:, None] == jnp.arange(group_slots)[None, :]).astype(LOW)

    qkv_full = grid.gather(qkv_weight)
    both = grid.gather(jnp.concatenate([out_weight, head_weight], axis=1))
    out_full, head_full = both[:, :model_width], both[:, model_width:]
    up_full = grid.gather(up_weight)
    down_full = grid.gather(down_weight)
    padded = jnp.pad(decoder, ((0, 0), (0, part_vocab * device_count - vocab_size)))
    padded = padded.reshape(decoder.shape[0], device_count, part_vocab).transpose(1, 0, 2)
    words = lax.all_to_all(padded, AXES, split_axis=0, concat_axis=0, tiled=True)
    words = words.reshape(model_width, part_vocab)
    padded_bias = jnp.pad(decoder_bias, (0, part_vocab * device_count - vocab_size))
    words_bias = lax.dynamic_slice_in_dim(padded_bias, my_place * part_vocab, part_vocab)

    merged_bias = jnp.concatenate([query_bias, jnp.zeros_like(query_bias), value_bias])
    qkv_rows = (product(tokens, qkv_full) + merged_bias).astype(LOW)
    queries, key_rows, value_rows = (
        heads_of(qkv_rows[:, i * model_width : (i + 1) * model_width]) for i in range(3)
    )
    attn_probs = attention_probs(queries, key_rows, seg_row, seg_row).astype(LOW)
    context = jnp.einsum("hqk,khd->qhd", attn_probs, value_rows, preferred_element_type=jnp.float32)
    context = context.reshape(tok_rows, model_width).astype(LOW)
    resid_one = tokens.astype(jnp.float32) + product(context, out_full) + out_bias
    normed_one = (norm_parts(resid_one)[0] * attn_gain + attn_shift).astype(LOW)
    up_rows = product(normed_one, up_full) + up_bias
    hidden = gelu_exact(up_rows).astype(LOW)
    resid_two = normed_one.astype(jnp.float32) + product(hidden, down_full) + down_bias
    layer_out = (norm_parts(resid_two)[0] * ffn_gain + ffn_shift).astype(LOW)

    pick_low = pick_mat.astype(LOW)
    pick_full = pick_mat.astype(jnp.float32)
    listed_rows = product(pick_low, layer_out).astype(LOW)
    group_rows = grid.gather_group(listed_rows)
    head_in = product(to_head, group_rows).astype(LOW)
    inner_rows = product(head_in, head_full) + head_bias
    head_act, act_back = jax.vjp(gelu_exact, inner_rows)
    head_normal, head_inv = norm_parts(head_act)
    head_normed = (head_normal * head_gain + head_shift).astype(LOW)
    all_normed = grid.gather(head_normed)
    logits = product(all_normed, words) + words_bias
    vocab_ids = my_place * part_vocab + jnp.arange(part_vocab)
    logits = jnp.where(vocab_ids[None, :] < vocab_size, logits, MASK_FILL)
    part_peak = jnp.max(logits, axis=1)
    part_log = part_peak + jnp.log(jnp.sum(jnp.exp(logits - part_peak[:, None]), axis=1))
    spread = jnp.broadcast_to(part_log[None], (device_count, slot_count))
    all_logs = lax.all_to_all(spread, AXES, split_axis=0, concat_axis=0, tiled=True)
    peak = jnp.max(all_logs, axis=0)
    log_total = peak + jnp.log(jnp.sum(jnp.exp(all_logs - peak), axis=0))
    is_label = vocab_ids[None, :] == labels[:, None]
    target_part = jnp.sum(jnp.where(is_label, logits, 0.0))
    loss_part = jnp.where(my_place == 0, jnp.sum(log_total), 0.0) - target_part
    dlogits = (
        (jnp.exp(logits - log_total[:, None]) - is_label.astype(jnp.float32)) * inv_count
    ).astype(LOW)
    dhead_normed = grid.scatter(product_nt(dlogits, words).astype(LOW)).astype(jnp.float32)
    words_grad = product_tn(all_normed, dlogits).astype(LOW)
    words_bias_grad = jnp.sum(dlogits, axis=0, dtype=jnp.float32)
    dhead_act, head_gain_part, head_shift_part = norm_back(
        head_normal, head_inv, head_gain, dhead_normed
    )
    dinner = act_back(dhead_act)[0].astype(LOW)
    head_bias_part = jnp.sum(dinner, axis=0, dtype=jnp.float32)
    head_term = product_tn(head_in, dinner)
    dhead_in = product_nt(dinner, head_full).astype(LOW)
    dlayer_out = product(from_head, grid.gather_group(dhead_in))

    low_rows = product(pick_low, jnp.concatenate([normed_one, context, qkv_rows], axis=1)).astype(LOW)
    normed_s = low_rows[:, :model_width]
    context_s = low_rows[:, model_width : 2 * model_width]
    queries_s = heads_of(low_rows[:, 2 * model_width : 3 * model_width])
    resid_one_s = pick_exact(pick_full, resid_one)
    resid_two_s = pick_exact(pick_full, resid_two)
    normal_two, inv_two = norm_parts(resid_two_s)
    dresid_two, ffn_gain_part, ffn_shift_part = norm_back(normal_two, inv_two, ffn_gain, dlayer_out)
    ddown_rows = dresid_two.astype(LOW)
    up_s = product(normed_s, up_full) + up_bias
    hidden_s, gelu_back = jax.vjp(gelu_exact, up_s)
    down_term = product_tn(hidden_s.astype(LOW), ddown_rows)
    down_bias_part = jnp.sum(ddown_rows, axis=0, dtype=jnp.float32)
    dup_rows = gelu_back(product_nt(ddown_rows, down_full))[0].astype(LOW)
    up_term = product_tn(normed_s, dup_rows)
    up_bias_part = jnp.sum(dup_rows, axis=0, dtype=jnp.float32)
    dnormed_one = dresid_two + product_nt(dup_rows, up_full)
    normal_one, inv_one = norm_parts(resid_one_s)
    dresid_one, attn_gain_part, attn_shift_part = norm_back(
        normal_one, inv_one, attn_gain, dnormed_one
    )
    dattn_sum = dresid_one.astype(LOW)
    out_term = product_tn(context_s, dattn_sum)
    out_bias_part = jnp.sum(dattn_sum, axis=0, dtype=jnp.float32)
    dcontext = heads_of(product_nt(dattn_sum, out_full).astype(LOW))
    probs_s = attention_probs(queries_s, key_rows, listed_seg, seg_row)
    dprobs = jnp.einsum("qhd,khd->hqk", dcontext, value_rows, preferred_element_type=jnp.float32)
    dscores = probs_s * (dprobs - jnp.sum(probs_s * dprobs, axis=-1, keepdims=True))
    dscores = dscores.astype(LOW)
    score_scale = HDIM ** (-0.5)
    dqueries_s = (
        jnp.einsum("hqk,khd->qhd", dscores, key_rows, preferred_element_type=jnp.float32)
        * score_scale
    )
    dkey_rows = (
        jnp.einsum("hqk,qhd->khd", dscores, queries_s, preferred_element_type=jnp.float32)
        * score_scale
    )
    dvalues = jnp.einsum(
        "hqk,qhd->khd", probs_s.astype(LOW), dcontext, preferred_element_type=jnp.float32
    )
    dqueries_s = dqueries_s.reshape(MASK_DEV, model_width).astype(LOW)
    dkey_rows = dkey_rows.reshape(tok_rows, model_width).astype(LOW)
    dvalues = dvalues.reshape(tok_rows, model_width).astype(LOW)
    dqueries = product_tn(pick_low, dqueries_s).astype(LOW)
    dqkv_rows = jnp.concatenate([dqueries, dkey_rows, dvalues], axis=1)
    qkv_term = product_tn(tokens, dqkv_rows)
    query_part = jnp.sum(dqueries_s, axis=0, dtype=jnp.float32)
    value_part = jnp.sum(dvalues, axis=0, dtype=jnp.float32)
    tokens_grad = pick_exact(pick_full.T, dresid_one) + product_nt(dqkv_rows, qkv_full)

    words_back = lax.all_to_all(
        words_grad.reshape(device_count, decoder.shape[0], part_vocab),
        AXES,
        split_axis=0,
        concat_axis=0,
        tiled=True,
    )
    decoder_grad = words_back.transpose(1, 0, 2).reshape(decoder.shape[0], -1)
    decoder_grad = decoder_grad[:, :vocab_size].astype(jnp.float32)
    decoder_bias_grad = grid.gather(words_bias_grad[None]).reshape(-1)[:vocab_size]
    down_grad = grid.scatter(down_term.astype(LOW)).astype(jnp.float32)
    up_grad = grid.scatter(up_term.astype(LOW)).astype(jnp.float32)
    both_term = jnp.concatenate([out_term, head_term], axis=1)
    both_grad = grid.scatter(both_term.astype(LOW)).astype(jnp.float32)
    qkv_grad = grid.scatter(qkv_term.astype(LOW)).astype(jnp.float32)
    small = [
        query_part,
        value_part,
        out_bias_part,
        attn_gain_part,
        attn_shift_part,
        up_bias_part,
        down_bias_part,
        ffn_gain_part,
        ffn_shift_part,
        head_bias_part,
        head_gain_part,
        head_shift_part,
        jnp.full((128,), loss_part),
    ]
    packed = grid.total(jnp.concatenate(small))
    sums = []
    for piece in small:
        sums.append(packed[: piece.shape[0]])
        packed = packed[piece.shape[0] :]
    return (
        layer_out,
        sums[12][0] * inv_count,
        tokens_grad,
        qkv_grad,
        sums[0],
        sums[1],
        both_grad[:, :model_width],
        sums[2],
        sums[3],
        sums[4],
        up_grad,
        sums[5],
        down_grad,
        sums[6],
        sums[7],
        sums[8],
        both_grad[:, model_width:],
        sums[9],
        sums[10],
        sums[11],
        decoder_grad,
        decoder_bias_grad,
    )


def solution(mesh):
    cut, rows = P(("dp", "bal"), None), P(("dp", "bal"))
    whole = P()
    return jax.shard_map(
        per_device,
        mesh=mesh,
        in_specs=(
            cut, cut, rows, cut, rows, cut, whole, whole, cut, whole, whole, whole,
            cut, whole, cut, whole, whole, whole, cut, whole, whole, whole, cut, whole,
        ),
        out_specs=(
            cut, whole, cut, cut, whole, whole, cut, whole, whole, whole, cut,
            whole, cut, whole, whole, whole, cut, whole, whole, whole, cut, whole,
        ),
        check_vma=False,
    )
```

```python
import functools

import jax
import jax.numpy as jnp
from jax import lax
from jax.experimental import pallas as pl
from jax.experimental.pallas import tpu as pltpu
from jax.sharding import PartitionSpec as P

HDIM = 64
HEAD_DEV = 32
MASK_DEV = 64


EPSILON = 1e-06
MASK_FILL = -1e30
AXES = ("dp", "bal")
LOW = jnp.bfloat16


def gelu_exact(values):
    return jax.nn.gelu(values, approximate=False)


def product(left_mat, right_mat):
    return jnp.dot(left_mat, right_mat, preferred_element_type=jnp.float32)


def product_tn(left_mat, right_mat):
    return lax.dot_general(
        left_mat, right_mat, (((0,), (0,)), ((), ())), preferred_element_type=jnp.float32
    )


def product_nt(left_mat, right_mat):
    return lax.dot_general(
        left_mat, right_mat, (((1,), (1,)), ((), ())), preferred_element_type=jnp.float32
    )


def norm_parts(hidden):
    average = jnp.mean(hidden, axis=-1, keepdims=True)
    centered = hidden - average
    inv_std = lax.rsqrt(jnp.mean(centered * centered, axis=-1, keepdims=True) + EPSILON)
    return centered * inv_std, inv_std


def norm_back(normal, inv_std, gain_vec, grad):
    scaled = grad * gain_vec
    first = jnp.mean(scaled, axis=-1, keepdims=True)
    second = jnp.mean(scaled * normal, axis=-1, keepdims=True)
    return (
        inv_std * (scaled - first - normal * second),
        jnp.sum(grad * normal, axis=0),
        jnp.sum(grad, axis=0),
    )


class Grid:
    def __init__(self, dp_size, bal_size):
        self.high = 4 if dp_size % 4 == 0 else 1
        self.low = dp_size // self.high
        self.wide = bal_size // 2
        self.sizes = (self.high, self.low, self.wide, 2)
        self.count = dp_size * bal_size
        dp_place, bal_place = lax.axis_index("dp"), lax.axis_index("bal")
        self.place = (
            dp_place // self.low,
            dp_place % self.low,
            bal_place // 2,
            bal_place % 2,
        )
        self.crossed = self.low == self.wide

    def index(self, spot):
        high, low, wide, core = spot
        return ((high * self.low + low) * self.wide + wide) * 2 + core

    def spots(self):
        for high in range(self.high):
            for low in range(self.low):
                for wide in range(self.wide):
                    for core in range(2):
                        yield (high, low, wide, core)

    def shift(self, value, axis_of, step):
        pairs = []
        for spot in self.spots():
            axis = axis_of[spot[3]]
            target = list(spot)
            target[axis] = (spot[axis] + step) % self.sizes[axis]
            pairs.append((self.index(spot), self.index(target)))
        return lax.ppermute(value, AXES, pairs)

    def own(self, axis_of):
        first, second = self.place[axis_of[0]], self.place[axis_of[1]]
        return first if axis_of[0] == axis_of[1] else jnp.where(self.place[3] == 0, first, second)

    def orders(self):
        return ((1, 2), (2, 1)) if self.crossed else ((1, 1), (2, 2))

    def gather_stage(self, value, axis_of):
        size = self.sizes[axis_of[0]]
        me = self.own(axis_of)
        parts = [value] + [self.shift(value, axis_of, step) for step in range(1, size)]

        def join(hold):
            rel = (me + hold - jnp.arange(size)) % size
            rel = rel.reshape((size,) + (1,) * value.ndim)
            out = parts[-1][None]
            for step in range(size - 2, -1, -1):
                out = jnp.where(rel == step, parts[step][None], out)
            return out

        return join

    def halves(self, first, second):
        is_first = self.place[3] == 0
        return jnp.where(is_first, first, second), jnp.where(is_first, second, first)

    def gather_steps(self, height):
        core = self.place[3]
        first, second = self.orders()

        def start(pair):
            keep, give = pair
            taken = self.shift(give, (3, 3), 1)

            def join(hold):
                is_own = (jnp.arange(2) == core + hold)[:, None, None]
                return jnp.where(is_own, keep[None], taken[None])

            return join

        def third(part):
            other = self.gather_stage(part, second)

            def straight(hold):
                joined = other(hold)
                out = joined.transpose(2, 1, 0, 3, 4, 5)
                if self.crossed:
                    turned = joined.transpose(2, 0, 1, 3, 4, 5)
                    out = jnp.where(core == 0, out, turned)
                return out.reshape(self.count * height, part.shape[-1])

            return straight

        def last(mine):
            other = self.shift(mine, (3, 3), 1)
            return lambda hold: (mine, other)

        return [
            start,
            lambda part: self.gather_stage(part, (0, 0)),
            lambda part: self.gather_stage(part, first),
            third,
            last,
        ]

    def scatter_steps(self, height, taken=None):
        core = self.place[3]
        first, second = self.orders()

        def total(pieces, hold=0):
            out = jnp.asarray(hold).astype(jnp.float32)
            for piece in pieces:
                out = out + piece.astype(jnp.float32)
            return out.astype(LOW)

        def start(pair):
            keep, give = pair
            came = self.shift(give, (3, 3), 1) if taken is None else taken
            shape = (self.high, self.low, self.wide, 2, height, keep.shape[1])
            return lambda hold: ([keep.reshape(shape), came.reshape(shape)], hold)

        def stage(axis_of, piece, hold):
            size = self.sizes[axis_of[0]]
            moved = [self.shift(total(piece(step), hold), axis_of, step) for step in range(1, size)]
            return lambda hold: (piece(0) + moved, hold)

        def cut(given, axis_of, axis):
            parts, hold = given
            size, me = self.sizes[axis_of[0]], self.own(axis_of)

            def piece(step):
                spot = (me + step) % size
                return [lax.dynamic_index_in_dim(part, spot, axis, keepdims=False) for part in parts]

            return stage(axis_of, piece, hold)

        def one(given):
            parts, hold = given
            if not self.crossed:
                return cut(given, second, 2)

            def piece(step):
                def of(part):
                    wide = (self.place[2] + step) % self.wide
                    low = (self.place[1] + step) % self.low
                    return jnp.where(
                        core == 0,
                        lax.dynamic_index_in_dim(part, wide, 2, keepdims=False),
                        lax.dynamic_index_in_dim(part, low, 1, keepdims=False),
                    )

                return [of(part) for part in parts]

            return stage(second, piece, hold)

        def last(given):
            parts, hold = given
            mine = total([lax.dynamic_index_in_dim(part, core, 0, keepdims=False) for part in parts])
            away = total(
                [lax.dynamic_index_in_dim(part, 1 - core, 0, keepdims=False) for part in parts], hold
            )
            other = self.shift(away, (3, 3), 1)
            return lambda hold: (mine, other)

        return [
            start,
            one,
            lambda given: cut(given, first, 1),
            lambda given: cut(given, (0, 0), 0),
            last,
        ]

    def gather_group(self, rows):
        parts = []
        for wide in range(self.wide):
            for core in range(2):
                if wide == 0 and core == 0:
                    parts.append(rows)
                    continue
                pairs = []
                for spot in self.spots():
                    target = (spot[0], spot[1], (spot[2] + wide) % self.wide, (spot[3] + core) % 2)
                    pairs.append((self.index(spot), self.index(target)))
                parts.append(lax.ppermute(rows, AXES, pairs))
        bal_size = self.wide * 2
        wide_from = (self.place[2] - jnp.arange(bal_size) // 2) % self.wide
        core_from = (self.place[3] - jnp.arange(bal_size) % 2) % 2
        rel = (wide_from * 2 + core_from)[:, None, None]
        out = parts[-1][None]
        for step in range(bal_size - 2, -1, -1):
            out = jnp.where(rel == step, parts[step][None], out)
        return out.reshape(bal_size * rows.shape[0], rows.shape[1])

    def total_steps(self):
        def stage(axis):
            def run(part):
                moved = [self.shift(part, (axis, axis), step) for step in range(1, self.sizes[axis])]

                def join(hold):
                    out = part + jnp.asarray(hold).astype(part.dtype)
                    for piece in moved:
                        out = out + piece
                    return out

                return join

            return run

        return [stage(axis) for axis in (3, 2, 1, 0)]


class Transfer:
    def __init__(self, part, steps):
        self.part = part
        self.steps = list(steps)
        self.join = self.steps.pop(0)(part)

    def step(self, *others):
        self.part = self.join(sum((nothing(other) for other in others), 0))
        self.join = self.steps.pop(0)(self.part)

    def finish(self, *others):
        while self.steps:
            self.step(*others)
            others = ()
        self.part = self.join(sum((nothing(other) for other in others), 0))
        return self.part


def nothing(value):
    hold = 0
    for piece in jax.tree.leaves(value):
        if piece.ndim:
            spot = piece[(0,) * piece.ndim]
            hold = hold + (spot != spot).astype(jnp.int32)
    return hold


def once(value, *others):
    for other in others:
        value = value + nothing(other).astype(value.dtype)
    return value


def erf_fast(value):
    value = jnp.clip(value, -3.832506856900711, 3.832506856900711)
    square = value * value
    top = jnp.float32(0.00022905065861350646)
    for number in (0.0034082910107109506, 0.050955695062380861, 0.18520832239976145, 1.128379143519084):
        top = top * square + number
    low = jnp.float32(-1.1791602954361697e-7)
    for number in (
        0.000023547966471313185,
        0.0010179625278914885,
        0.014070470171167667,
        0.11098505178285362,
        0.49746925110067538,
        1.0,
    ):
        low = low * square + number
    return value * top / low


def gelu_fast(value):
    return 0.5 * value * (1.0 + erf_fast(value * 0.7071067811865476))


def gelu_slope(value):
    bell = jnp.exp(value * value * -0.5) * 0.3989422804014327
    return 0.5 * (1.0 + erf_fast(value * 0.7071067811865476)) + value * bell


def call_after(kernel, others, in_specs, **settings):
    others = jax.tree.leaves(others)

    def run(*refs):
        kernel(*refs[len(others) :])

    call = pl.pallas_call(
        run, in_specs=[pl.BlockSpec(memory_space=pl.ANY)] * len(others) + in_specs, **settings
    )
    return lambda *operands: call(*others, *operands)


def full_block(*shape):
    return pl.BlockSpec(shape, lambda step: (0,) * len(shape))


def feed_forward_kernel(
    context_ref,
    tokens_ref,
    out_ref,
    vectors_ref,
    up_first_ref,
    up_second_ref,
    up_bias_ref,
    down_first_ref,
    down_second_ref,
    layer_ref,
    normed_ref,
    one_ref,
    total_ref,
):
    step = pl.program_id(0)
    half = up_first_ref.shape[0]

    @pl.when(step == 0)
    def _():
        attn = jnp.dot(context_ref[...], out_ref[...], preferred_element_type=jnp.float32)
        resid = tokens_ref[...].astype(jnp.float32) + attn + vectors_ref[0:1, :]
        one_ref[...] = resid
        normed = norm_parts(resid)[0] * vectors_ref[1:2, :] + vectors_ref[2:3, :]
        normed = normed.astype(LOW)
        normed_ref[...] = normed
        total_ref[...] = normed.astype(jnp.float32) + vectors_ref[3:4, :]

    normed = normed_ref[...]
    up = product(normed[:, :half], up_first_ref[...]) + product(normed[:, half:], up_second_ref[...])
    hidden = gelu_fast(up + up_bias_ref[...]).astype(LOW)
    total_ref[...] += product(hidden[:, :half], down_first_ref[...]) + product(
        hidden[:, half:], down_second_ref[...]
    )

    @pl.when(step == pl.num_programs(0) - 1)
    def _():
        layer = norm_parts(total_ref[...])[0] * vectors_ref[4:5, :] + vectors_ref[5:6, :]
        layer_ref[...] = layer.astype(LOW)


def weight_blocks(width, steps):
    def cut(row, first):
        return pl.BlockSpec((width // 2, width), lambda step: (row, first + step))

    return [
        cut(0, 0),
        cut(1, 0),
        pl.BlockSpec((1, width), lambda step: (0, step)),
        cut(0, steps),
        cut(1, steps),
    ]


def feed_forward(context, tokens, out_full, vectors, packed, up_bias, others=()):
    rows, width = tokens.shape
    steps = packed.shape[1] // (2 * width)
    block = full_block(rows, width)
    return call_after(
        feed_forward_kernel,
        others,
        [block, block, full_block(width, width), full_block(8, width)] + weight_blocks(width, steps),
        grid=(steps,),
        out_specs=[block, block, block, block],
        out_shape=[
            jax.ShapeDtypeStruct((rows, width), LOW),
            jax.ShapeDtypeStruct((rows, width), LOW),
            jax.ShapeDtypeStruct((rows, width), jnp.float32),
            jax.ShapeDtypeStruct((rows, width), jnp.float32),
        ],
        compiler_params=pltpu.CompilerParams(vmem_limit_bytes=24 * 1024 * 1024),
        cost_estimate=pl.CostEstimate(
            flops=4 * rows * width * width * steps,
            bytes_accessed=4 * width * width * steps,
            transcendentals=rows * width * steps,
        ),
    )(context, tokens, out_full, vectors, packed, packed, up_bias[None, :], packed, packed)


def feed_back_kernel(
    grad_ref,
    one_ref,
    two_ref,
    normed_ref,
    vectors_ref,
    up_first_ref,
    up_second_ref,
    up_bias_ref,
    down_first_ref,
    down_second_ref,
    ddown_ref,
    done_ref,
    up_sum_ref,
    sums_ref,
    total_ref,
):
    step = pl.program_id(0)

    def norm_grad(resid, gain, grad, row):
        normal, inv_std = norm_parts(resid)
        dresid, gain_part, shift_part = norm_back(normal, inv_std, gain, grad)
        sums_ref[row : row + 1, :] = gain_part[None]
        sums_ref[row + 1 : row + 2, :] = shift_part[None]
        sums_ref[row + 2 : row + 3, :] = jnp.sum(
            dresid.astype(LOW).astype(jnp.float32), axis=0, keepdims=True
        )
        return dresid

    @pl.when(step == 0)
    def _():
        sums_ref[...] = jnp.zeros_like(sums_ref)
        dtwo = norm_grad(two_ref[...], vectors_ref[4:5, :], grad_ref[...].astype(jnp.float32), 0)
        total_ref[...] = dtwo
        ddown_ref[...] = dtwo.astype(LOW)

    half = up_first_ref.shape[0]
    normed, ddown = normed_ref[...], ddown_ref[...]
    up = product(normed[:, :half], up_first_ref[...]) + product(normed[:, half:], up_second_ref[...])
    dhidden = jnp.concatenate(
        [product_nt(ddown, down_first_ref[...]), product_nt(ddown, down_second_ref[...])], axis=1
    )
    dup = (gelu_slope(up + up_bias_ref[...]) * dhidden).astype(LOW)
    up_sum_ref[...] = jnp.sum(dup.astype(jnp.float32), axis=0, keepdims=True)
    total_ref[:, :half] += product_nt(dup, up_first_ref[...])
    total_ref[:, half:] += product_nt(dup, up_second_ref[...])

    @pl.when(step == pl.num_programs(0) - 1)
    def _():
        done_ref[...] = norm_grad(one_ref[...], vectors_ref[1:2, :], total_ref[...], 3).astype(LOW)


def feed_back(grad, resid_one, resid_two, normed, vectors, packed, up_bias):
    rows, width = normed.shape
    steps = packed.shape[1] // (2 * width)
    block = full_block(rows, width)
    return pl.pallas_call(
        feed_back_kernel,
        grid=(steps,),
        in_specs=[
            block,
            block,
            block,
            block,
            full_block(8, width),
            *weight_blocks(width, steps),
        ],
        out_specs=[
            block,
            block,
            pl.BlockSpec((1, width), lambda step: (0, step)),
            full_block(8, width),
        ],
        out_shape=[
            jax.ShapeDtypeStruct((rows, width), LOW),
            jax.ShapeDtypeStruct((rows, width), LOW),
            jax.ShapeDtypeStruct((1, width * steps), jnp.float32),
            jax.ShapeDtypeStruct((8, width), jnp.float32),
        ],
        scratch_shapes=[pltpu.VMEM((rows, width), jnp.float32)],
        compiler_params=pltpu.CompilerParams(vmem_limit_bytes=24 * 1024 * 1024),
        cost_estimate=pl.CostEstimate(
            flops=6 * rows * width * width * steps,
            bytes_accessed=4 * width * width * steps,
            transcendentals=rows * width * steps,
        ),
    )(grad, resid_one, resid_two, normed, vectors, packed, packed, up_bias[None, :], packed, packed)


def attention_kernel(
    tokens_ref, weight_ref, bias_ref, seg_column_ref, seg_ref, qkv_ref, context_ref
):
    width = context_ref.shape[1]
    rows = tokens_ref.shape[0]
    qkv = jnp.dot(tokens_ref[...], weight_ref[...], preferred_element_type=jnp.float32)
    qkv_ref[...] = (qkv + bias_ref[...]).astype(LOW)
    block = rows // 2
    for head in range(width // HDIM):
        lanes = [slice(i * width + head * HDIM, i * width + (head + 1) * HDIM) for i in range(3)]
        key, value = qkv_ref[:, lanes[1]], qkv_ref[:, lanes[2]]
        for part in range(2):
            spot = slice(part * block, (part + 1) * block)
            query = qkv_ref[spot, lanes[0]] * jnp.asarray(HDIM ** (-0.5), LOW)
            scores = lax.dot_general(
                query, key, (((1,), (1,)), ((), ())), preferred_element_type=jnp.float32
            )
            scores = jnp.where(seg_column_ref[spot, :] == seg_ref[...], scores, MASK_FILL)
            exp_scores = jnp.exp(scores - jnp.max(scores, axis=-1, keepdims=True))
            probs = exp_scores * (1.0 / jnp.sum(exp_scores, axis=-1, keepdims=True))
            context_ref[spot, lanes[0]] = jnp.dot(
                probs.astype(LOW), value, preferred_element_type=jnp.float32
            ).astype(LOW)


def attention(tokens, weight, bias, seg_row, others=()):
    rows = tokens.shape[0]
    width = bias.shape[1] // 3
    return call_after(
        attention_kernel,
        others,
        [
            full_block(rows, tokens.shape[1]),
            full_block(tokens.shape[1], 3 * width),
            full_block(1, 3 * width),
            full_block(rows, 1),
            full_block(1, rows),
        ],
        grid=(1,),
        out_specs=[full_block(rows, 3 * width), full_block(rows, width)],
        out_shape=[
            jax.ShapeDtypeStruct((rows, 3 * width), LOW),
            jax.ShapeDtypeStruct((rows, width), LOW),
        ],
        compiler_params=pltpu.CompilerParams(vmem_limit_bytes=24 * 1024 * 1024),
        cost_estimate=pl.CostEstimate(
            flops=2 * rows * width * (3 * tokens.shape[1] + 2 * rows),
            bytes_accessed=2 * rows * tokens.shape[1] + 2 * weight.size,
            transcendentals=rows * rows * width // HDIM,
        ),
    )(tokens, weight, bias, seg_row[:, None], seg_row[None, :])


def attention_back_kernel(
    scale,
    queries_ref,
    qkv_in_ref,
    grad_ref,
    listed_seg_ref,
    seg_ref,
    pick_ref,
    dqkv_ref,
    sums_ref,
    dqueries_ref,
):
    width = queries_ref.shape[1]
    same_seg = listed_seg_ref[...] == seg_ref[...]

    def dot(left, right, left_dim, right_dim):
        return lax.dot_general(
            left,
            right,
            (((left_dim,), (right_dim,)), ((), ())),
            preferred_element_type=jnp.float32,
        )

    for head in range(width // HDIM):
        lanes = slice(head * HDIM, (head + 1) * HDIM)
        query = queries_ref[:, lanes]
        key = qkv_in_ref[:, width + head * HDIM : width + (head + 1) * HDIM]
        value = qkv_in_ref[:, 2 * width + head * HDIM : 2 * width + (head + 1) * HDIM]
        grad = grad_ref[:, lanes]
        scores = jnp.where(same_seg, dot(query, key, 1, 1) * scale, MASK_FILL)
        exp_scores = jnp.exp(scores - jnp.max(scores, axis=-1, keepdims=True))
        probs = exp_scores / jnp.sum(exp_scores, axis=-1, keepdims=True)
        dprobs = dot(grad, value, 1, 1)
        dscores = probs * (dprobs - jnp.sum(probs * dprobs, axis=-1, keepdims=True))
        dscores = dscores.astype(LOW)
        dqueries_ref[:, lanes] = (dot(dscores, key, 1, 0) * scale).astype(LOW)
        dqkv_ref[:, width + head * HDIM : width + (head + 1) * HDIM] = (
            dot(dscores, query, 0, 0) * scale
        ).astype(LOW)
        dqkv_ref[:, 2 * width + head * HDIM : 2 * width + (head + 1) * HDIM] = dot(
            probs.astype(LOW), grad, 0, 0
        ).astype(LOW)
    dqueries = dqueries_ref[...]
    dqkv_ref[:, :width] = dot(pick_ref[...], dqueries, 0, 0).astype(LOW)
    sums_ref[...] = jnp.zeros_like(sums_ref)
    sums_ref[0:1, :] = jnp.sum(dqueries.astype(jnp.float32), axis=0, keepdims=True)
    sums_ref[1:2, :] = jnp.sum(
        dqkv_ref[:, 2 * width :].astype(jnp.float32), axis=0, keepdims=True
    )


def attention_back(queries, parts, grad, listed_seg, seg_row, pick, others=()):
    listed, width = queries.shape
    rows = parts.shape[0]
    return call_after(
        functools.partial(attention_back_kernel, HDIM ** (-0.5)),
        others,
        [pl.BlockSpec(memory_space=pltpu.VMEM)] * 6,
        out_shape=[
            jax.ShapeDtypeStruct((rows, 3 * width), LOW),
            jax.ShapeDtypeStruct((8, width), jnp.float32),
        ],
        scratch_shapes=[pltpu.VMEM((listed, width), LOW)],
        compiler_params=pltpu.CompilerParams(vmem_limit_bytes=24 * 1024 * 1024),
        cost_estimate=pl.CostEstimate(
            flops=10 * listed * rows * width,
            bytes_accessed=10 * rows * width,
            transcendentals=listed * rows * width // HDIM,
        ),
    )(queries, parts, grad, listed_seg[:, None], seg_row[None, :], pick)


def heads_of(rows):
    return rows.reshape(rows.shape[0], rows.shape[1] // HDIM, HDIM)


def attention_probs(queries, key_rows, query_seg, key_seg):
    scores = jnp.einsum(
        "qhd,khd->hqk", queries, key_rows, preferred_element_type=jnp.float32
    ) * HDIM ** (-0.5)
    same_seg = query_seg[:, None] == key_seg[None, :]
    masked = jnp.where(same_seg[None], scores, MASK_FILL)
    row_peak = jnp.max(masked, axis=-1, keepdims=True)
    exp_scores = jnp.exp(masked - row_peak)
    return exp_scores / jnp.sum(exp_scores, axis=-1, keepdims=True)


def per_device(
    tokens,
    segment_ids,
    mlm_labels,
    mask_order,
    mask_count,
    qkv_weight,
    query_bias,
    value_bias,
    out_weight,
    out_bias,
    attn_gain,
    attn_shift,
    up_weight,
    up_bias,
    down_weight,
    down_bias,
    ffn_gain,
    ffn_shift,
    head_weight,
    head_bias,
    head_gain,
    head_shift,
    decoder,
    decoder_bias,
):
    model_width = tokens.shape[1]
    tok_rows = tokens.shape[0]
    vocab_size = decoder.shape[1]
    bal_size = lax.axis_size("bal")
    dp_size = lax.axis_size("dp")
    bal_place = lax.axis_index("bal")
    dp_place = lax.axis_index("dp")
    grid = Grid(dp_size, bal_size)
    device_count = dp_size * bal_size
    my_place = dp_place * bal_size + bal_place
    group_slots = HEAD_DEV * bal_size
    slot_count = HEAD_DEV * device_count
    inv_count = 1.0 / slot_count
    part_vocab = -(-(-(-vocab_size // device_count)) // 128) * 128
    seg_row = segment_ids[0]

    listed = mask_order[0, :MASK_DEV]
    pick_mat = listed[:, None] == jnp.arange(tok_rows)[None, :]
    pick_low = pick_mat.astype(LOW)

    def pick(rows):
        return product(pick_low, rows).astype(LOW)

    listed_ids = jnp.sum(jnp.where(pick_mat, mlm_labels[None, :], 0), axis=1)
    listed_seg = jnp.sum(jnp.where(pick_mat, seg_row[None, :], 0), axis=1)

    shard_rows = qkv_weight.shape[0]
    my_units = down_weight.shape[0]
    units = my_units * device_count
    ratio = my_units // shard_rows
    half = model_width // 2

    def unit_order(rows):
        split = rows.reshape(rows.shape[0], device_count, ratio, shard_rows)
        return split.transpose(0, 2, 1, 3).reshape(rows.shape[0], units)

    down_wide = down_weight.reshape(ratio, shard_rows, model_width).transpose(1, 0, 2)
    down_wide = down_wide.reshape(shard_rows, ratio * model_width)
    packed = lax.all_gather(
        jnp.concatenate([unit_order(up_weight), down_wide], axis=1), AXES, axis=0, tiled=True
    )
    up_offsets = unit_order(up_bias[None])[0]
    my_columns = up_weight.reshape(shard_rows, device_count, my_units).transpose(1, 0, 2)
    my_offsets = lax.dynamic_slice_in_dim(up_bias, my_place * my_units, my_units)

    def by_heads(rows):
        split = rows.reshape(rows.shape[0], 3, 2, half)
        return grid.halves(
            split[:, :, 0].reshape(rows.shape[0], 3 * half),
            split[:, :, 1].reshape(rows.shape[0], 3 * half),
        )

    def with_half(rows, half_rows):
        return [jnp.concatenate(pair, axis=1) for pair in zip(rows, half_rows)]

    info = jnp.concatenate([listed_ids, mask_count, jnp.zeros((63,), jnp.int32)])
    info = grid.gather_group(info[None])
    weights_run = Transfer(
        with_half(by_heads(qkv_weight), grid.halves(out_weight, head_weight)),
        grid.gather_steps(shard_rows),
    )
    qkv_width = 3 * half
    weights_run.step()
    weights_run.step(info)
    weights_run.step()
    weights_run.step()
    weights_run.finish()
    all_mine, all_other = weights_run.part
    out_full, head_full = grid.halves(all_mine[:, qkv_width:], all_other[:, qkv_width:])

    counts = info[:, MASK_DEV]
    starts = jnp.cumsum(counts) - counts
    steps = jnp.arange(MASK_DEV)
    slot_of = jnp.where(steps[None] < counts[:, None], starts[:, None] + steps[None], -1)
    own_slot_of = lax.dynamic_index_in_dim(slot_of, bal_place, 0, keepdims=False)
    slot_of = slot_of.reshape(1, bal_size * MASK_DEV)
    my_slots = bal_place * HEAD_DEV + jnp.arange(HEAD_DEV)
    is_mine = slot_of == my_slots[:, None]
    to_head = is_mine.astype(LOW)
    from_head = (own_slot_of[:, None] == jnp.arange(group_slots)[None, :]).astype(LOW)
    my_labels = jnp.sum(jnp.where(is_mine, info[:, :MASK_DEV].reshape(1, -1), 0), axis=1)
    tokens_s = pick(tokens)

    padded = jnp.pad(decoder, ((0, 0), (0, part_vocab * device_count - vocab_size)))
    padded = padded.reshape(decoder.shape[0], device_count, part_vocab).transpose(1, 0, 2)
    bias_mine, bias_other = by_heads(
        jnp.concatenate([query_bias, jnp.zeros_like(query_bias), value_bias])[None]
    )
    parts_mine, context_mine = attention(
        tokens, all_mine, bias_mine, seg_row, [to_head, from_head, tokens_s, padded]
    )
    parts_other, context_other = attention(tokens, all_other, bias_other, seg_row, [context_mine])
    context = jnp.concatenate(grid.halves(context_mine, context_other), axis=1)
    words = lax.all_to_all(padded, AXES, split_axis=0, concat_axis=0, tiled=True)

    picked = [tokens_s, *grid.halves(pick(context_mine), pick(context_other))]
    group_rows = grid.gather_group(jnp.concatenate(picked, axis=1))
    queries_mine, queries_other = pick(parts_mine[:, :half]), pick(parts_other[:, :half])
    my_columns = lax.all_to_all(my_columns, AXES, split_axis=0, concat_axis=0, tiled=True)
    my_columns = my_columns.reshape(model_width, my_units)
    slot_rows = product(to_head, group_rows).astype(LOW)
    tokens_own, context_own = slot_rows[:, :model_width], slot_rows[:, model_width:]
    vectors = jnp.stack(
        [out_bias, attn_gain, attn_shift, down_bias, ffn_gain, ffn_shift, out_bias, out_bias]
    )
    head_in, normed_own, resid_one, resid_two = feed_forward(
        context_own, tokens_own, out_full, vectors, packed, up_offsets, [my_columns, words, queries_mine, queries_other]
    )

    inner_rows = product(head_in, head_full) + head_bias
    head_act, act_back = jax.vjp(gelu_exact, inner_rows)
    head_normal, head_inv = norm_parts(head_act)
    head_normed = (head_normal * head_gain + head_shift).astype(LOW)
    head_run = Transfer(
        grid.halves(head_normed[:, :half], head_normed[:, half:]), grid.gather_steps(HEAD_DEV)
    )
    part_rows = tok_rows // 2
    layer_parts = []

    def layer_part(*others):
        spot = slice(len(layer_parts) * part_rows, (len(layer_parts) + 1) * part_rows)
        part = feed_forward(
            context[spot], tokens[spot], out_full, vectors, packed, up_offsets, others
        )
        layer_parts.append(part[0])
        return part[0]

    head_run.step()
    head_run.step()
    head_run.step()
    head_run.step()
    normed_mine, normed_other = head_run.finish()
    words = words.reshape(model_width, part_vocab)
    words_mine, words_other = grid.halves(words[:half], words[half:])
    padded_bias = jnp.pad(decoder_bias, (0, part_vocab * device_count - vocab_size))
    words_bias = lax.dynamic_slice_in_dim(padded_bias, my_place * part_vocab, part_vocab)
    logits = product(normed_mine, words_mine) + product(normed_other, words_other) + words_bias
    vocab_ids = my_place * part_vocab + jnp.arange(part_vocab)
    logits = jnp.where(vocab_ids[None, :] < vocab_size, logits, MASK_FILL)
    part_peak = jnp.max(logits, axis=1)
    part_log = part_peak + jnp.log(jnp.sum(jnp.exp(logits - part_peak[:, None]), axis=1))
    spread = jnp.concatenate(
        [part_log, my_labels.astype(jnp.float32), jnp.zeros((128 - HEAD_DEV,), jnp.float32)]
    )
    spread = jnp.broadcast_to(spread[None, None], (device_count, 1, slot_count + 128))
    spread = lax.all_to_all(spread, AXES, split_axis=0, concat_axis=0, tiled=True)
    spread = once(spread[:, 0], layer_part(part_log))
    all_logs = spread[:, :slot_count]
    labels = spread[:, slot_count : slot_count + HEAD_DEV].reshape(slot_count).astype(jnp.int32)
    peak = jnp.max(all_logs, axis=0)
    log_total = peak + jnp.log(jnp.sum(jnp.exp(all_logs - peak), axis=0))
    is_label = vocab_ids[None, :] == labels[:, None]
    dlogits = (
        (jnp.exp(logits - log_total[:, None]) - is_label.astype(jnp.float32)) * inv_count
    ).astype(LOW)
    dhead_other = product_nt(dlogits, words_other).astype(LOW)
    dhead_mine = product_nt(dlogits, words_mine).astype(LOW)
    head_run = Transfer((dhead_mine, dhead_other), grid.scatter_steps(HEAD_DEV))
    words_grad = jnp.concatenate(
        grid.halves(product_tn(normed_mine, dlogits), product_tn(normed_other, dlogits))
    ).astype(LOW)
    head_run.step()
    head_run.step(words_grad)
    head_run.step()
    head_run.step()
    words_bias_grad = jnp.sum(dlogits, axis=0, dtype=jnp.float32)
    target_part = jnp.sum(jnp.where(is_label, logits, 0.0))
    loss_part = jnp.where(my_place == 0, jnp.sum(log_total), 0.0) - target_part
    dhead_normed = jnp.concatenate(grid.halves(*head_run.finish()), axis=1).astype(jnp.float32)
    dhead_act, head_gain_part, head_shift_part = norm_back(
        head_normal, head_inv, head_gain, dhead_normed
    )
    dinner = act_back(dhead_act)[0].astype(LOW)
    head_bias_part = jnp.sum(dinner, axis=0, dtype=jnp.float32)
    dhead_in = product_nt(dinner, head_full).astype(LOW)

    ddown_own, dresid_own, up_sums, own_sums = feed_back(
        dhead_in, resid_one, resid_two, normed_own, vectors, packed, up_offsets
    )
    group_grads = grid.gather_group(dresid_own)
    factors = lax.all_gather(
        jnp.concatenate([normed_own, ddown_own], axis=1), AXES, axis=0, tiled=True
    )
    out_term = product_tn(context_own, dresid_own).astype(LOW)
    head_term = product_tn(head_in, dinner).astype(LOW)
    both_mine, both_other = grid.halves(out_term, head_term)
    dresid_one = product(from_head, group_grads).astype(LOW)
    dcontext = product_nt(dresid_one, out_full).astype(LOW)
    dcontext_mine, dcontext_other = grid.halves(dcontext[:, :half], dcontext[:, half:])
    dqkv_other, sums_other = attention_back(
        queries_other,
        parts_other,
        dcontext_other,
        listed_seg,
        seg_row,
        pick_low,
    )
    other_term = product_tn(tokens, dqkv_other).astype(LOW)
    other_term = jnp.concatenate([other_term, both_other], axis=1)
    other_taken = grid.shift(other_term, (3, 3), 1)
    dqkv_mine, sums_mine = attention_back(
        queries_mine,
        parts_mine,
        dcontext_mine,
        listed_seg,
        seg_row,
        pick_low,
        [other_term],
    )
    mine_term = product_tn(tokens, dqkv_mine).astype(LOW)
    mine_term = jnp.concatenate([mine_term, both_mine], axis=1)
    weights_run = Transfer((mine_term, None), grid.scatter_steps(shard_rows, other_taken))
    words_grad = once(words_grad, mine_term)
    words_back = lax.all_to_all(
        words_grad.reshape(device_count, decoder.shape[0], part_vocab),
        AXES,
        split_axis=0,
        concat_axis=0,
        tiled=True,
    )
    weights_run.step()

    qkv_sums = jnp.concatenate(grid.halves(sums_mine, sums_other), axis=1)
    small = jnp.stack(
        [
            qkv_sums[0],
            qkv_sums[1],
            own_sums[5],
            own_sums[3],
            own_sums[4],
            own_sums[2],
            own_sums[0],
            own_sums[1],
            head_bias_part,
            head_gain_part,
            head_shift_part,
            jnp.full((model_width,), loss_part),
        ]
        + jnp.split(up_sums[0], ratio)
    )
    small = jnp.pad(small, ((0, 0), (0, 1024 - model_width)))
    is_here = jnp.arange(device_count) == my_place
    vocab_sums = jnp.where(is_here[:, None], words_bias_grad[None], 0.0).reshape(-1, 1024)
    small_run = Transfer(jnp.concatenate([small, vocab_sums]), grid.total_steps())
    small_run.step()
    weights_run.step(small_run.part, layer_part(mine_term))
    small_run.step()
    tokens_grad = product_tn(pick_low, dresid_one) + product_nt(dqkv_other, all_other[:, :qkv_width])
    tokens_grad = once(tokens_grad, layer_parts[-1]) + product_nt(dqkv_mine, all_mine[:, :qkv_width])

    rows_all, ddown_all = factors[:, :model_width], factors[:, model_width:]
    hidden, act_back = jax.vjp(gelu_exact, product(rows_all, my_columns) + my_offsets)
    dup_all = act_back(product_nt(ddown_all, down_weight))[0].astype(LOW)
    up_term = product_tn(rows_all, dup_all).astype(LOW).reshape(device_count, shard_rows, my_units)
    weights_run.step(small_run.part, tokens_grad)
    small_run.step()
    up_back = lax.all_to_all(up_term, AXES, split_axis=0, concat_axis=0, tiled=True)
    down_grad = product_tn(hidden.astype(LOW), ddown_all)
    up_grad = up_back.transpose(1, 0, 2).reshape(shard_rows, units).astype(jnp.float32)

    weights_run.step(up_term, small_run.part)
    mine, other = weights_run.finish()
    sums = small_run.finish()
    decoder_bias_grad = sums[12 + ratio :].reshape(-1)[:vocab_size]
    sums = sums[: 12 + ratio, :model_width]
    up_sums = sums[12:].reshape(ratio, device_count, shard_rows).transpose(1, 0, 2).reshape(-1)
    first, second = grid.halves(mine[:, :qkv_width], other[:, :qkv_width])
    qkv_grad = jnp.stack(
        [first.reshape(shard_rows, 3, half), second.reshape(shard_rows, 3, half)], axis=2
    )
    qkv_grad = qkv_grad.reshape(shard_rows, 3 * model_width).astype(jnp.float32)
    out_grad, head_grad = grid.halves(mine[:, qkv_width:], other[:, qkv_width:])
    decoder_grad = words_back.transpose(1, 0, 2).reshape(decoder.shape[0], -1)
    decoder_grad = decoder_grad[:, :vocab_size].astype(jnp.float32)
    return (
        jnp.concatenate(layer_parts),
        sums[11, 0] * inv_count,
        tokens_grad,
        qkv_grad,
        sums[0],
        sums[1],
        out_grad.astype(jnp.float32),
        sums[2],
        sums[3],
        sums[4],
        up_grad,
        up_sums,
        down_grad,
        sums[5],
        sums[6],
        sums[7],
        head_grad.astype(jnp.float32),
        sums[8],
        sums[9],
        sums[10],
        decoder_grad,
        decoder_bias_grad,
    )


def solution(mesh):
    cut, rows = P(("dp", "bal"), None), P(("dp", "bal"))
    whole = P()
    return jax.shard_map(
        per_device,
        mesh=mesh,
        in_specs=(
            cut, cut, rows, cut, rows, cut, whole, whole, cut, whole, whole, whole,
            cut, whole, cut, whole, whole, whole, cut, whole, whole, whole, cut, whole,
        ),
        out_specs=(
            cut, whole, cut, cut, whole, whole, cut, whole, whole, whole, cut,
            whole, cut, whole, whole, whole, cut, whole, whole, whole, cut, whole,
        ),
        check_vma=False,
    )
```

```python
import functools

import jax
import jax.numpy as jnp
import numpy as np
from jax import lax
from jax.experimental import pallas as pl
from jax.experimental.pallas import tpu as pltpu
from jax.sharding import PartitionSpec as P

HDIM = 64
HEAD_DEV = 32
MASK_DEV = 64


EPSILON = 1e-06
MASK_FILL = -1e30
AXES = ("dp", "bal")
LOW = jnp.bfloat16


def gelu_exact(values):
    return jax.nn.gelu(values, approximate=False)


def product(left_mat, right_mat):
    return jnp.dot(left_mat, right_mat, preferred_element_type=jnp.float32)


def product_tn(left_mat, right_mat):
    return lax.dot_general(
        left_mat, right_mat, (((0,), (0,)), ((), ())), preferred_element_type=jnp.float32
    )


def product_nt(left_mat, right_mat):
    return lax.dot_general(
        left_mat, right_mat, (((1,), (1,)), ((), ())), preferred_element_type=jnp.float32
    )


def norm_parts(hidden):
    average = jnp.mean(hidden, axis=-1, keepdims=True)
    centered = hidden - average
    inv_std = lax.rsqrt(jnp.mean(centered * centered, axis=-1, keepdims=True) + EPSILON)
    return centered * inv_std, inv_std


def norm_back(normal, inv_std, gain_vec, grad):
    scaled = grad * gain_vec
    first = jnp.mean(scaled, axis=-1, keepdims=True)
    second = jnp.mean(scaled * normal, axis=-1, keepdims=True)
    return (
        inv_std * (scaled - first - normal * second),
        jnp.sum(grad * normal, axis=0),
        jnp.sum(grad, axis=0),
    )


class Grid:
    def __init__(self, dp_size, bal_size):
        self.high = 4 if dp_size % 4 == 0 else 1
        self.low = dp_size // self.high
        self.wide = bal_size // 2
        self.sizes = (self.high, self.low, self.wide, 2)
        self.count = dp_size * bal_size
        dp_place, bal_place = lax.axis_index("dp"), lax.axis_index("bal")
        self.place = (
            dp_place // self.low,
            dp_place % self.low,
            bal_place // 2,
            bal_place % 2,
        )
        self.crossed = self.low == self.wide

    def index(self, spot):
        high, low, wide, core = spot
        return ((high * self.low + low) * self.wide + wide) * 2 + core

    def spots(self):
        for high in range(self.high):
            for low in range(self.low):
                for wide in range(self.wide):
                    for core in range(2):
                        yield (high, low, wide, core)

    def shift(self, value, axis_of, step):
        pairs = []
        for spot in self.spots():
            axis = axis_of[spot[3]]
            target = list(spot)
            target[axis] = (spot[axis] + step) % self.sizes[axis]
            pairs.append((self.index(spot), self.index(target)))
        self.sent = value
        return lax.ppermute(value, AXES, pairs)

    def own(self, axis_of):
        first, second = self.place[axis_of[0]], self.place[axis_of[1]]
        return first if axis_of[0] == axis_of[1] else jnp.where(self.place[3] == 0, first, second)

    def orders(self):
        return ((1, 2), (2, 1)) if self.crossed else ((1, 1), (2, 2))

    def gather_stage(self, value, axis_of):
        size = self.sizes[axis_of[0]]
        me = self.own(axis_of)
        parts = [value] + [self.shift(value, axis_of, step) for step in range(1, size)]

        def join(hold):
            rel = (me + hold - jnp.arange(size)) % size
            rel = rel.reshape((size,) + (1,) * value.ndim)
            out = parts[-1][None]
            for step in range(size - 2, -1, -1):
                out = jnp.where(rel == step, parts[step][None], out)
            return out

        return join

    def halves(self, first, second, hold=0):
        is_first = self.place[3] + hold == 0
        return lax.select(is_first, first, second), lax.select(is_first, second, first)

    def gather_steps(self, height):
        core = self.place[3]
        first, second = self.orders()

        def start(pair):
            keep, give = pair
            taken = self.shift(give, (3, 3), 1)

            def join(hold):
                is_own = (jnp.arange(2) == core + hold)[:, None, None]
                return jnp.where(is_own, keep[None], taken[None])

            return join

        def third(part):
            other = self.gather_stage(part, second)

            def straight(hold):
                joined = other(hold)
                out = joined.transpose(2, 1, 0, 3, 4, 5)
                if self.crossed:
                    turned = joined.transpose(2, 0, 1, 3, 4, 5)
                    out = lax.select(core == 0, out, turned)
                return out.reshape(self.count * height, part.shape[-1])

            return straight

        def last(mine):
            other = self.shift(mine, (3, 3), 1)
            return lambda hold: (mine, other)

        return [
            start,
            lambda part: self.gather_stage(part, (0, 0)),
            lambda part: self.gather_stage(part, first),
            third,
            last,
        ]

    def scatter_steps(self, height, taken=None):
        core = self.place[3]
        first, second = self.orders()

        def total(pieces, hold=0):
            out = jnp.asarray(hold).astype(jnp.float32)
            for piece in pieces:
                out = out + piece.astype(jnp.float32)
            return out.astype(LOW)

        def start(pair):
            keep, give = pair
            came = self.shift(give, (3, 3), 1) if taken is None else taken
            shape = (self.high, self.low, self.wide, 2, height, keep.shape[1])
            return lambda hold: ([keep.reshape(shape), came.reshape(shape)], hold)

        def stage(axis_of, piece, hold):
            size = self.sizes[axis_of[0]]
            moved = [self.shift(total(piece(step), hold), axis_of, step) for step in range(1, size)]
            return lambda hold: (piece(0) + moved, hold)

        def cut(given, axis_of, axis):
            parts, hold = given
            size, me = self.sizes[axis_of[0]], self.own(axis_of)

            def piece(step):
                spot = (me + step) % size
                return [lax.dynamic_index_in_dim(part, spot, axis, keepdims=False) for part in parts]

            return stage(axis_of, piece, hold)

        def one(given):
            parts, hold = given
            if not self.crossed:
                return cut(given, second, 2)
            size, me = self.wide, self.own(second)
            flat = [part.reshape(self.high, size * size, *part.shape[3:]) for part in parts]

            def piece(step, along):
                spot = (me + step) % size
                spot = jnp.where(core == 0, along * size + spot, spot * size + along)
                return [lax.dynamic_index_in_dim(part, spot, 1, keepdims=False) for part in flat]

            moved = [
                [self.shift(total(piece(step, along), hold), second, step) for step in range(1, size)]
                for along in range(size)
            ]
            return lambda hold: ([piece(0, along) + moved[along] for along in range(size)], hold)

        def two(given):
            if not self.crossed:
                return cut(given, first, 1)
            columns, hold = given
            size, me = self.low, self.own(first)

            def piece(step):
                spot = (me + step) % size
                out = columns[-1]
                for along in range(size - 2, -1, -1):
                    out = [lax.select(spot == along, *pair) for pair in zip(columns[along], out)]
                return out

            return stage(first, piece, hold)

        def last(given):
            parts, hold = given
            mine = total([lax.dynamic_index_in_dim(part, core, 0, keepdims=False) for part in parts])
            away = total(
                [lax.dynamic_index_in_dim(part, 1 - core, 0, keepdims=False) for part in parts], hold
            )
            other = self.shift(away, (3, 3), 1)
            return lambda hold: (mine, other)

        return [
            start,
            one,
            two,
            lambda given: cut(given, (0, 0), 0),
            last,
        ]

    def group(self):
        return [
            (self.place[2] - wide) % self.wide * 2 + (self.place[3] - core) % 2
            for wide in range(self.wide)
            for core in range(2)
        ]

    def gather_group(self, rows):
        parts = []
        for wide in range(self.wide):
            for core in range(2):
                if wide == 0 and core == 0:
                    parts.append(rows)
                    continue
                pairs = []
                for spot in self.spots():
                    target = (spot[0], spot[1], (spot[2] + wide) % self.wide, (spot[3] + core) % 2)
                    pairs.append((self.index(spot), self.index(target)))
                parts.append(lax.ppermute(rows, AXES, pairs))
        return parts


class Transfer:
    def __init__(self, part, steps):
        self.part = part
        self.steps = list(steps)
        self.join = self.steps.pop(0)(part)

    def step(self, *others):
        self.part = self.join(sum((nothing(other) for other in others), 0))
        self.join = self.steps.pop(0)(self.part)

    def finish(self, *others):
        while self.steps:
            self.step(*others)
            others = ()
        self.part = self.join(sum((nothing(other) for other in others), 0))
        return self.part


def nothing(value):
    hold = 0
    for piece in jax.tree.leaves(value):
        if piece.ndim:
            spot = piece[(0,) * piece.ndim]
            is_float = jnp.issubdtype(spot.dtype, jnp.floating)
            hold = hold + (spot != spot if is_float else spot < -1).astype(jnp.int32)
    return hold


def once(value, *others):
    for other in others:
        value = value + nothing(other).astype(value.dtype)
    return value


def erf_fast(value):
    value = jnp.clip(value, -3.832506856900711, 3.832506856900711)
    square = value * value
    top = jnp.float32(0.00022905065861350646)
    for number in (0.0034082910107109506, 0.050955695062380861, 0.18520832239976145, 1.128379143519084):
        top = top * square + number
    low = jnp.float32(-1.1791602954361697e-7)
    for number in (
        0.000023547966471313185,
        0.0010179625278914885,
        0.014070470171167667,
        0.11098505178285362,
        0.49746925110067538,
        1.0,
    ):
        low = low * square + number
    return value * top / low


def gelu_fast(value):
    return 0.5 * value * (1.0 + erf_fast(value * 0.7071067811865476))


def gelu_slope(value):
    bell = jnp.exp(value * value * -0.5) * 0.3989422804014327
    return 0.5 * (1.0 + erf_fast(value * 0.7071067811865476)) + value * bell


def call_after(kernel, others, in_specs, **settings):
    others = jax.tree.leaves(others)

    def run(*refs):
        kernel(*refs[len(others) :])

    call = pl.pallas_call(
        run, in_specs=[pl.BlockSpec(memory_space=pl.ANY)] * len(others) + in_specs, **settings
    )
    return lambda *operands: call(*others, *operands)


def load_weights(packed_ref, weights_ref, sems):
    count, _, width = weights_ref.shape
    copies = []
    order = [part * (count // 2) + block for block in range(count // 2) for part in range(2)]
    for block in order:
        source = packed_ref.at[:, block * width : (block + 1) * width]
        copies.append((block, pltpu.make_async_copy(source, weights_ref.at[block], sems.at[block])))
        copies[-1][1].start()
    return dict(copies)


def feed_forward_kernel(
    spot_out,
    context_ref,
    tokens_ref,
    out_ref,
    vectors_ref,
    up_bias_ref,
    packed_ref,
    layer_ref,
    normed_ref,
    one_ref,
    total_ref,
    weights_ref,
    sems,
):
    copies = load_weights(packed_ref, weights_ref, sems)
    blocks = len(copies) // 2
    width = tokens_ref.shape[1]
    resid = tokens_ref[spot_out, :].astype(jnp.float32)
    resid = resid + product(context_ref[spot_out, :], out_ref[...])
    resid = resid + vectors_ref[0:1, :]
    one_ref[...] = resid
    normed = norm_parts(resid)[0] * vectors_ref[1:2, :] + vectors_ref[2:3, :]
    normed = normed.astype(LOW)
    normed_ref[...] = normed
    total_ref[...] = normed.astype(jnp.float32) + vectors_ref[3:4, :]
    rows = total_ref.shape[0]
    parts = max(1, rows // 128)
    for block in range(blocks):
        copies[block].wait()
        copies[blocks + block].wait()
        bias = up_bias_ref[:, block * width : (block + 1) * width]
        for part in range(parts):
            spot = slice(part * (rows // parts), (part + 1) * (rows // parts))
            up = product(normed_ref[spot, :], weights_ref[block])
            hidden = gelu_fast(up + bias).astype(LOW)
            total_ref[spot, :] += product(hidden, weights_ref[blocks + block])
    layer = norm_parts(total_ref[...])[0] * vectors_ref[4:5, :] + vectors_ref[5:6, :]
    layer_ref[spot_out, :] = layer.astype(LOW)


def square_scratch(packed, width):
    count = packed.shape[1] // width
    return [pltpu.VMEM((count, width, width), LOW), pltpu.SemaphoreType.DMA((count,))]


def feed_forward_more_kernel(spot, into_ref, *refs):
    layer_ref = refs[6]
    layer_ref[: spot.start, :] = into_ref[: spot.start, :]
    feed_forward_kernel(spot, *refs)


def feed_forward(context, tokens, out_full, vectors, packed, up_bias, others, room, part=0, parts=1, into=None):
    rows, width = tokens.shape[0] // parts, tokens.shape[1]
    units = packed.shape[1] // 2
    spot = slice(part * rows, (part + 1) * rows)
    more = () if into is None else (into,)
    kernel = functools.partial(feed_forward_kernel, spot)
    if more:
        kernel = functools.partial(feed_forward_more_kernel, spot)
    others = jax.tree.leaves(others)
    return call_after(
        kernel,
        others,
        [pl.BlockSpec(memory_space=pltpu.VMEM)] * (5 + len(more))
        + [pl.BlockSpec(memory_space=pltpu.HBM)],
        out_shape=[
            jax.ShapeDtypeStruct((parts * rows, width), LOW),
            jax.ShapeDtypeStruct((rows, width), LOW),
            jax.ShapeDtypeStruct((rows, width), jnp.float32),
            jax.ShapeDtypeStruct((rows, width), jnp.float32),
        ],
        scratch_shapes=square_scratch(packed, width),
        compiler_params=pltpu.CompilerParams(vmem_limit_bytes=room * 1024 * 1024),
        cost_estimate=pl.CostEstimate(
            flops=4 * rows * width * units,
            bytes_accessed=4 * width * units,
            transcendentals=rows * units,
        ),
    )(*more, context, tokens, out_full, vectors, up_bias[None, :], packed)


def feed_back_kernel(
    grad_ref,
    one_ref,
    two_ref,
    normed_ref,
    vectors_ref,
    more_ref,
    up_bias_ref,
    packed_ref,
    send_ref,
    done_ref,
    total_ref,
    sums_ref,
    weights_ref,
    sems,
):
    copies = load_weights(packed_ref, weights_ref, sems)
    blocks = len(copies) // 2
    width = normed_ref.shape[1]
    sums_ref[...] = jnp.zeros_like(sums_ref)
    sums_ref[0:6, :] = more_ref[0:6, :]

    def norm_grad(resid, gain, grad, row):
        normal, inv_std = norm_parts(resid)
        dresid, gain_part, shift_part = norm_back(normal, inv_std, gain, grad)
        sums_ref[row : row + 1, :] = gain_part[None]
        sums_ref[row + 1 : row + 2, :] = shift_part[None]
        sums_ref[row + 2 : row + 3, :] = jnp.sum(
            dresid.astype(LOW).astype(jnp.float32), axis=0, keepdims=True
        )
        return dresid

    dtwo = norm_grad(two_ref[...], vectors_ref[4:5, :], grad_ref[...].astype(jnp.float32), 6)
    total_ref[...] = dtwo
    ddown = dtwo.astype(LOW)
    send_ref[:, :width] = ddown
    for block in range(blocks):
        copies[block].wait()
        copies[blocks + block].wait()
        spot = slice(block * width, (block + 1) * width)
        up = product(normed_ref[...], weights_ref[block]) + up_bias_ref[:, spot]
        dup = (gelu_slope(up) * product_nt(ddown, weights_ref[blocks + block])).astype(LOW)
        sums_ref[12 + block : 13 + block, :] = jnp.sum(
            dup.astype(jnp.float32), axis=0, keepdims=True
        )
        total_ref[...] += product_nt(dup, weights_ref[block])
    done_ref[...] = norm_grad(one_ref[...], vectors_ref[1:2, :], total_ref[...], 9).astype(LOW)
    half = width // 2
    send_ref[:16, width:] = sums_ref[:, :half].astype(LOW)
    send_ref[16:, width:] = sums_ref[:, half:].astype(LOW)


def feed_back(grad, resid_one, resid_two, normed, vectors, more, packed, up_bias, others):
    rows, width = normed.shape
    units = packed.shape[1] // 2
    return call_after(
        feed_back_kernel,
        others,
        [pl.BlockSpec(memory_space=pltpu.VMEM)] * 7
        + [pl.BlockSpec(memory_space=pltpu.HBM)],
        out_shape=[
            jax.ShapeDtypeStruct((rows, width + width // 2), LOW),
            jax.ShapeDtypeStruct((rows, width), LOW),
        ],
        scratch_shapes=[
            pltpu.VMEM((rows, width), jnp.float32),
            pltpu.VMEM((16, width), jnp.float32),
        ]
        + square_scratch(packed, width),
        compiler_params=pltpu.CompilerParams(vmem_limit_bytes=24 * 1024 * 1024),
        cost_estimate=pl.CostEstimate(
            flops=6 * rows * width * units,
            bytes_accessed=4 * width * units,
            transcendentals=rows * units,
        ),
    )(grad, resid_one, resid_two, normed, vectors, more, up_bias[None, :], packed)


def attention_kernel(
    tokens_ref, weight_ref, bias_ref, seg_column_ref, seg_ref, qkv_ref, context_ref
):
    width = context_ref.shape[1]
    rows = tokens_ref.shape[0]
    qkv = product(tokens_ref[...], weight_ref[:, : 3 * width])
    qkv_ref[...] = (qkv + bias_ref[...]).astype(LOW)
    block = rows // 2
    for head in range(width // HDIM):
        lanes = [slice(i * width + head * HDIM, i * width + (head + 1) * HDIM) for i in range(3)]
        key, value = qkv_ref[:, lanes[1]], qkv_ref[:, lanes[2]]
        for part in range(2):
            spot = slice(part * block, (part + 1) * block)
            query = qkv_ref[spot, lanes[0]] * jnp.asarray(HDIM ** (-0.5), LOW)
            scores = lax.dot_general(
                query, key, (((1,), (1,)), ((), ())), preferred_element_type=jnp.float32
            )
            scores = jnp.where(seg_column_ref[spot, :] == seg_ref[...], scores, MASK_FILL)
            exp_scores = jnp.exp(scores - jnp.max(scores, axis=-1, keepdims=True))
            probs = exp_scores * (1.0 / jnp.sum(exp_scores, axis=-1, keepdims=True))
            context_ref[spot, lanes[0]] = jnp.dot(
                probs.astype(LOW), value, preferred_element_type=jnp.float32
            ).astype(LOW)


def attention(tokens, weight, bias, seg_row, others=()):
    rows = tokens.shape[0]
    width = bias.shape[1] // 3
    return call_after(
        attention_kernel,
        others,
        [pl.BlockSpec(memory_space=pltpu.VMEM)] * 5,
        out_shape=[
            jax.ShapeDtypeStruct((rows, 3 * width), LOW),
            jax.ShapeDtypeStruct((rows, width), LOW),
        ],
        compiler_params=pltpu.CompilerParams(vmem_limit_bytes=24 * 1024 * 1024),
        cost_estimate=pl.CostEstimate(
            flops=2 * rows * width * (3 * tokens.shape[1] + 2 * rows),
            bytes_accessed=2 * rows * tokens.shape[1] + 2 * weight.size,
            transcendentals=rows * rows * width // HDIM,
        ),
    )(tokens, weight, bias, seg_row[:, None], seg_row[None, :])


def attention_back_kernel(
    scale, queries_ref, first_ref, second_ref, grad_ref, listed_seg_ref, seg_ref, pick_ref, turned_ref,
    beside_ref, first_grad_ref, first_term_ref, second_grad_ref, second_term_ref, sums_ref, dqueries_ref,
):
    same_seg = listed_seg_ref[...] == seg_ref[...]
    width = first_ref.shape[1] // 3
    sums_ref[...] = jnp.zeros_like(sums_ref)

    def dot(left, right, left_dim, right_dim):
        return lax.dot_general(
            left,
            right,
            (((left_dim,), (right_dim,)), ((), ())),
            preferred_element_type=jnp.float32,
        )

    halves = (
        (0, first_ref, first_grad_ref, first_term_ref),
        (1, second_ref, second_grad_ref, second_term_ref),
    )
    for half, qkv_ref, dqkv_ref, term_ref in halves:
        for head in range(width // HDIM):
            lanes = slice(half * width + head * HDIM, half * width + (head + 1) * HDIM)
            keys = slice(width + head * HDIM, width + (head + 1) * HDIM)
            values = slice(2 * width + head * HDIM, 2 * width + (head + 1) * HDIM)
            query, grad = queries_ref[:, lanes], grad_ref[:, lanes]
            key, value = qkv_ref[:, keys], qkv_ref[:, values]
            scores = jnp.where(same_seg, dot(query, key, 1, 1) * scale, MASK_FILL)
            exp_scores = jnp.exp(scores - jnp.max(scores, axis=-1, keepdims=True))
            probs = exp_scores / jnp.sum(exp_scores, axis=-1, keepdims=True)
            dprobs = dot(grad, value, 1, 1)
            dscores = probs * (dprobs - jnp.sum(probs * dprobs, axis=-1, keepdims=True))
            dscores = dscores.astype(LOW)
            dqueries_ref[:, lanes] = (dot(dscores, key, 1, 0) * scale).astype(LOW)
            dqkv_ref[:, keys] = (dot(dscores, query, 0, 0) * scale).astype(LOW)
            dqkv_ref[:, values] = dot(probs.astype(LOW), grad, 0, 0).astype(LOW)
        lanes = slice(half * width, (half + 1) * width)
        dqkv_ref[:, :width] = dot(pick_ref[...], dqueries_ref[:, lanes], 0, 0).astype(LOW)
        term_ref[:, : 3 * width] = product(turned_ref[...], dqkv_ref[...]).astype(LOW)
        term_ref[:, 3 * width :] = beside_ref[:, 2 * half * width : 2 * (half + 1) * width]
        sums_ref[0:1, lanes] = jnp.sum(
            dqueries_ref[:, lanes].astype(jnp.float32), axis=0, keepdims=True
        )
        sums_ref[1:2, lanes] = jnp.sum(
            dqkv_ref[:, 2 * width :].astype(jnp.float32), axis=0, keepdims=True
        )


def attention_back(queries, first, second, grad, listed_seg, seg_row, pick, turned, beside, others):
    listed = queries.shape[0]
    rows, width = first.shape
    term = (turned.shape[0], width + beside.shape[1] // 2)
    return call_after(
        functools.partial(attention_back_kernel, HDIM ** (-0.5)),
        others,
        [pl.BlockSpec(memory_space=pltpu.VMEM)] * 9,
        out_shape=[
            jax.ShapeDtypeStruct((rows, width), LOW),
            jax.ShapeDtypeStruct(term, LOW),
            jax.ShapeDtypeStruct((rows, width), LOW),
            jax.ShapeDtypeStruct(term, LOW),
            jax.ShapeDtypeStruct((8, queries.shape[1]), jnp.float32),
        ],
        scratch_shapes=[pltpu.VMEM(queries.shape, LOW)],
        compiler_params=pltpu.CompilerParams(vmem_limit_bytes=32 * 1024 * 1024),
        cost_estimate=pl.CostEstimate(
            flops=20 * listed * rows * width // 3 + 4 * turned.size * width,
            bytes_accessed=20 * rows * width // 3,
            transcendentals=2 * listed * rows * width // (3 * HDIM),
        ),
    )(queries, first, second, grad, listed_seg[:, None], seg_row[None, :], pick, turned, beside)


def heads_of(rows):
    return rows.reshape(rows.shape[0], rows.shape[1] // HDIM, HDIM)


def attention_probs(queries, key_rows, query_seg, key_seg):
    scores = jnp.einsum(
        "qhd,khd->hqk", queries, key_rows, preferred_element_type=jnp.float32
    ) * HDIM ** (-0.5)
    same_seg = query_seg[:, None] == key_seg[None, :]
    masked = jnp.where(same_seg[None], scores, MASK_FILL)
    row_peak = jnp.max(masked, axis=-1, keepdims=True)
    exp_scores = jnp.exp(masked - row_peak)
    return exp_scores / jnp.sum(exp_scores, axis=-1, keepdims=True)


def per_device(
    tokens,
    segment_ids,
    mlm_labels,
    mask_order,
    mask_count,
    qkv_weight,
    query_bias,
    value_bias,
    out_weight,
    out_bias,
    attn_gain,
    attn_shift,
    up_weight,
    up_bias,
    down_weight,
    down_bias,
    ffn_gain,
    ffn_shift,
    head_weight,
    head_bias,
    head_gain,
    head_shift,
    decoder,
    decoder_bias,
):
    model_width = tokens.shape[1]
    tok_rows = tokens.shape[0]
    vocab_size = decoder.shape[1]
    bal_size = lax.axis_size("bal")
    dp_size = lax.axis_size("dp")
    bal_place = lax.axis_index("bal")
    dp_place = lax.axis_index("dp")
    grid = Grid(dp_size, bal_size)
    device_count = dp_size * bal_size
    my_place = dp_place * bal_size + bal_place
    slot_count = HEAD_DEV * device_count
    inv_count = 1.0 / slot_count
    part_vocab = -(-(-(-vocab_size // device_count)) // 128) * 128
    seg_row = segment_ids[0]

    listed = mask_order[0, :MASK_DEV]
    pick_mat = listed[:, None] == jnp.arange(tok_rows)[None, :]
    pick_low = pick_mat.astype(LOW)

    def pick(rows):
        return product(pick_low, rows).astype(LOW)

    listed_ids = jnp.sum(jnp.where(pick_mat, mlm_labels[None, :], 0), axis=1)
    listed_seg = jnp.sum(jnp.where(pick_mat, seg_row[None, :], 0), axis=1)

    shard_rows = qkv_weight.shape[0]
    my_units = down_weight.shape[0]
    units = my_units * device_count
    ratio = my_units // shard_rows
    half = model_width // 2

    def unit_order(rows):
        split = rows.reshape(rows.shape[0], device_count, ratio, shard_rows)
        return split.transpose(0, 2, 1, 3).reshape(rows.shape[0], units)

    down_wide = down_weight.reshape(ratio, shard_rows, model_width).transpose(1, 0, 2)
    down_wide = down_wide.reshape(shard_rows, ratio * model_width)
    packed = lax.all_gather(
        jnp.concatenate([unit_order(up_weight), down_wide], axis=1), AXES, axis=0, tiled=True
    )
    up_offsets = unit_order(up_bias[None])[0]
    my_offsets = lax.dynamic_slice_in_dim(up_bias, my_place * my_units, my_units)

    def by_heads(rows):
        split = rows.reshape(rows.shape[0], 3, 2, half)
        return grid.halves(
            split[:, :, 0].reshape(rows.shape[0], 3 * half),
            split[:, :, 1].reshape(rows.shape[0], 3 * half),
        )

    def with_half(rows, half_rows):
        return [jnp.concatenate(pair, axis=1) for pair in zip(rows, half_rows)]

    weights_run = Transfer(
        with_half(by_heads(qkv_weight), grid.halves(out_weight, head_weight)),
        grid.gather_steps(shard_rows),
    )
    qkv_width = 3 * half
    weights_run.step()
    weights_run.step()
    weights_run.step()
    info = jnp.concatenate([listed_ids, mask_count, jnp.zeros((63,), jnp.int32)])
    info = grid.gather_group(info[None])
    weights_run.step()
    all_mine, all_other = weights_run.finish()
    out_full, head_full = grid.halves(all_mine[:, qkv_width:], all_other[:, qkv_width:])

    info = jnp.concatenate(info)
    group = jnp.stack(grid.group())
    counts = info[:, MASK_DEV]
    before = group[None, :] < group[:, None]
    starts = jnp.sum(jnp.where(before, counts[None, :], 0), axis=1)
    steps = jnp.arange(MASK_DEV)
    slot_of = jnp.where(steps[None] < counts[:, None], starts[:, None] + steps[None], -1)
    my_slots = bal_place * HEAD_DEV + jnp.arange(HEAD_DEV)
    is_mine = slot_of[None] == my_slots[:, None, None]
    my_labels = jnp.sum(jnp.where(is_mine, info[None, :, :MASK_DEV], 0), axis=(1, 2))
    to_head = is_mine.astype(LOW)
    group_slots = group[:, None] * HEAD_DEV + jnp.arange(HEAD_DEV)[None, :]
    from_head = (slot_of[0][:, None, None] == group_slots[None]).astype(LOW)

    def choose(choice, parts):
        total = product(choice[:, 0], parts[0])
        for index, part in enumerate(parts[1:], 1):
            total = total + product(choice[:, index], part)
        return total.astype(LOW)

    tokens_s = pick(tokens)

    padded = jnp.pad(decoder, ((0, 0), (0, part_vocab * device_count - vocab_size)))
    padded = padded.reshape(decoder.shape[0], device_count, part_vocab).transpose(1, 0, 2)
    bias_mine, bias_other = by_heads(
        jnp.concatenate([query_bias, jnp.zeros_like(query_bias), value_bias])[None]
    )
    parts_mine, context_mine = attention(
        tokens, all_mine, bias_mine, seg_row, [padded]
    )
    parts_other, context_other = attention(tokens, all_other, bias_other, seg_row, [context_mine])
    context = jnp.concatenate(grid.halves(context_mine, context_other), axis=1)
    words = lax.all_to_all(padded, AXES, split_axis=0, concat_axis=0, tiled=True)

    picked = [tokens_s, *grid.halves(pick(context_mine), pick(context_other))]
    group_rows = grid.gather_group(jnp.concatenate(picked, axis=1))
    listed_queries = jnp.concatenate(
        [pick(parts_mine[:, :half]), pick(parts_other[:, :half])], axis=1
    )
    slot_rows = choose(to_head, group_rows)
    tokens_own, context_own = slot_rows[:, :model_width], slot_rows[:, model_width:]
    vectors = jnp.stack(
        [out_bias, attn_gain, attn_shift, down_bias, ffn_gain, ffn_shift, out_bias, out_bias]
    )
    window = min(256, model_width)
    begin = jnp.minimum(my_place * shard_rows // 128 * 128, model_width - window)
    lanes = jnp.arange(window)[:, None] + begin - my_place * shard_rows
    unit_ids = np.arange(my_units)
    my_columns = jnp.zeros((model_width, my_units), jnp.float32)
    for block in range(ratio):
        piece = lax.dynamic_slice_in_dim(packed, block * model_width + begin, window, 1)
        wanted = np.where(unit_ids // shard_rows == block, unit_ids % shard_rows, -model_width)
        is_unit = lanes == jnp.asarray(wanted, jnp.int32)[None, :]
        my_columns = my_columns + product(piece, is_unit.astype(LOW))
    my_columns = my_columns.astype(LOW)


    def layer_part(part, others, room, into=None):
        return feed_forward(
            context, tokens, out_full, vectors, packed, up_offsets, others, room, part, 2, into
        )[0]

    head_in, normed_own, resid_one, resid_two = feed_forward(
        context_own, tokens_own, out_full, vectors, packed, up_offsets, [listed_queries], 24
    )

    rows_all = lax.all_gather(normed_own, AXES, axis=0, tiled=True)
    up_all = product(rows_all, my_columns) + my_offsets

    inner_rows = product(head_in, head_full) + head_bias
    head_act, act_back = jax.vjp(gelu_exact, inner_rows)
    head_normal, head_inv = norm_parts(head_act)
    head_normed = (head_normal * head_gain + head_shift).astype(LOW)
    head_run = Transfer(
        grid.halves(head_normed[:, :half], head_normed[:, half:]), grid.gather_steps(HEAD_DEV)
    )
    head_run.step(lax.dynamic_slice(words, (nothing(head_in), 0, 0), (1, 1, 1)))
    head_run.step()
    head_run.step()
    head_run.step()
    normed_mine, normed_other = head_run.finish()
    words = words.reshape(model_width, part_vocab)
    words_mine, words_other = grid.halves(words[:half], words[half:])
    padded_bias = jnp.pad(decoder_bias, (0, part_vocab * device_count - vocab_size))
    words_bias = lax.dynamic_slice_in_dim(padded_bias, my_place * part_vocab, part_vocab)
    logits = product(normed_mine, words_mine) + product(normed_other, words_other) + words_bias
    vocab_ids = my_place * part_vocab + jnp.arange(part_vocab)
    logits = jnp.where(vocab_ids[None, :] < vocab_size, logits, MASK_FILL)
    part_peak = jnp.max(logits, axis=1)
    part_log = part_peak + jnp.log(jnp.sum(jnp.exp(logits - part_peak[:, None]), axis=1))
    spread = jnp.concatenate(
        [part_log, my_labels.astype(jnp.float32), jnp.zeros((128 - HEAD_DEV,), jnp.float32)]
    )
    spread = jnp.broadcast_to(spread[None, None], (device_count, 1, slot_count + 128))
    spread = lax.all_to_all(spread, AXES, split_axis=0, concat_axis=0, tiled=True)
    spread = spread[:, 0]
    all_logs = spread[:, :slot_count]
    labels = spread[:, slot_count : slot_count + HEAD_DEV].reshape(slot_count).astype(jnp.int32)
    peak = jnp.max(all_logs, axis=0)
    log_total = peak + jnp.log(jnp.sum(jnp.exp(all_logs - peak), axis=0))
    is_label = vocab_ids[None, :] == labels[:, None]
    dlogits = (
        (jnp.exp(logits - log_total[:, None]) - is_label.astype(jnp.float32)) * inv_count
    ).astype(LOW)
    dhead_other = product_nt(dlogits, words_other).astype(LOW)
    dhead_mine = product_nt(dlogits, words_mine).astype(LOW)
    head_run = Transfer((dhead_mine, dhead_other), grid.scatter_steps(HEAD_DEV))
    words_terms = [product_tn(rows, dlogits).astype(LOW) for rows in (normed_mine, normed_other)]
    head_run.step()
    head_run.step()
    head_run.step()
    head_run.step()
    words_bias_grad = jnp.sum(dlogits, axis=0, dtype=jnp.float32)
    target_part = jnp.sum(jnp.where(is_label, logits, 0.0))
    loss_part = jnp.where(my_place == 0, jnp.sum(log_total), 0.0) - target_part
    dhead_normed = jnp.concatenate(grid.halves(*head_run.finish()), axis=1).astype(jnp.float32)
    dhead_act, head_gain_part, head_shift_part = norm_back(
        head_normal, head_inv, head_gain, dhead_normed
    )
    dinner = act_back(dhead_act)[0].astype(LOW)
    head_bias_part = jnp.sum(dinner, axis=0, dtype=jnp.float32)
    dhead_in = product_nt(dinner, head_full).astype(LOW)

    words_grad = jnp.concatenate(grid.halves(*words_terms, nothing(dhead_in))).astype(LOW)
    words_back = lax.all_to_all(
        words_grad.reshape(device_count, decoder.shape[0], part_vocab),
        AXES,
        split_axis=0,
        concat_axis=0,
        tiled=True,
    )

    loss_high = loss_part.astype(LOW).astype(jnp.float32)
    vocab_rows = jnp.pad(words_bias_grad, (0, 2 * model_width - part_vocab))
    more = jnp.stack(
        [
            head_bias_part,
            head_gain_part,
            head_shift_part,
            jnp.where(jnp.arange(model_width) < half, loss_high, loss_part - loss_high),
            vocab_rows[:model_width],
            vocab_rows[model_width:],
            head_bias_part,
            head_bias_part,
        ]
    )
    send, dresid_own = feed_back(
        dhead_in, resid_one, resid_two, normed_own, vectors, more, packed, up_offsets, [up_all]
    )
    group_grads = grid.gather_group(dresid_own)
    factors = lax.all_gather(send, AXES, axis=0, tiled=True)

    def two_parts(rows):
        high = rows.astype(LOW)
        return jnp.concatenate([high, (rows - high.astype(jnp.float32)).astype(LOW)])

    out_term = product_tn(context_own, dresid_own).astype(LOW)
    head_term = product_tn(head_in, dinner).astype(LOW)
    beside = jnp.concatenate(grid.halves(out_term, head_term), axis=1)
    dresid_one = choose(from_head, group_grads)
    dcontext = product_nt(dresid_one, out_full).astype(LOW)
    dcontext = jnp.concatenate(grid.halves(dcontext[:, :half], dcontext[:, half:]), axis=1)
    dqkv_mine, mine_term, dqkv_other, other_term, qkv_sums = attention_back(
        listed_queries,
        parts_mine,
        parts_other,
        dcontext,
        listed_seg,
        seg_row,
        pick_low,
        tokens.T,
        beside,
        [],
    )
    other_taken = grid.shift(other_term, (3, 3), 1)
    weights_run = Transfer((mine_term, None), grid.scatter_steps(shard_rows, other_taken))
    weights_run.step(words_back)
    first_part = layer_part(0, [grid.sent], 24)
    weights_run.step()
    second_part = layer_part(1, [grid.sent], 24, first_part)
    qkv_sums = grid.halves(qkv_sums[:2, :half], qkv_sums[:2, half:])
    qkv_sums = two_parts(jnp.concatenate(qkv_sums, axis=1))

    ddown_all = factors[:, :model_width]
    hidden, act_back = jax.vjp(gelu_exact, up_all)
    dup_all = act_back(product_nt(ddown_all, down_weight))[0].astype(LOW)
    up_term = product_tn(rows_all, dup_all).astype(LOW).reshape(device_count, shard_rows, my_units)
    weights_run.step()
    qkv_sums = qkv_sums.reshape(-1, my_units)
    qkv_sums = jnp.broadcast_to(qkv_sums[None], (device_count, *qkv_sums.shape))
    up_back = lax.all_to_all(
        jnp.concatenate([up_term, qkv_sums], axis=1), AXES, split_axis=0, concat_axis=0, tiled=True
    )
    down_grad = product_tn(hidden.astype(LOW), ddown_all)
    up_grad = up_back[:, :shard_rows].transpose(1, 0, 2).reshape(shard_rows, units)
    up_grad = up_grad.astype(jnp.float32)
    qkv_sums = jnp.sum(up_back[:, shard_rows:].astype(jnp.float32), axis=0)
    qkv_sums = jnp.sum(qkv_sums.reshape(2, 2, model_width), axis=0)

    tokens_grad = product_tn(pick_low, once(dresid_one, weights_run.part[0][-1]))
    tokens_grad = tokens_grad + product_nt(dqkv_other, all_other[:, :qkv_width])
    tokens_grad = tokens_grad + product_nt(dqkv_mine, all_mine[:, :qkv_width])
    weights_run.step()
    words_back = once(words_back, weights_run.part[0][-1])
    mine, other = weights_run.finish()
    sums = factors[:, model_width:].astype(jnp.float32).reshape(device_count, 2, 16, half)
    sums = jnp.concatenate([sums[:, 0], sums[:, 1]], axis=2)
    decoder_bias_grad = sums[:, 4:6].reshape(device_count, 2 * model_width)[:, :part_vocab]
    decoder_bias_grad = decoder_bias_grad.reshape(-1)[:vocab_size]
    sums = jnp.sum(sums, axis=0)
    up_sums = sums[12:].reshape(ratio, device_count, shard_rows).transpose(1, 0, 2).reshape(-1)
    first, second = grid.halves(mine[:, :qkv_width], other[:, :qkv_width])
    qkv_grad = jnp.stack(
        [first.reshape(shard_rows, 3, half), second.reshape(shard_rows, 3, half)], axis=2
    )
    qkv_grad = qkv_grad.reshape(shard_rows, 3 * model_width).astype(jnp.float32)
    out_grad, head_grad = grid.halves(mine[:, qkv_width:], other[:, qkv_width:])
    decoder_grad = words_back.transpose(1, 0, 2).reshape(decoder.shape[0], -1)
    decoder_grad = decoder_grad[:, :vocab_size].astype(jnp.float32)
    return (
        second_part,
        (sums[3, 0] + sums[3, half]) * inv_count,
        tokens_grad,
        qkv_grad,
        qkv_sums[0],
        qkv_sums[1],
        out_grad.astype(jnp.float32),
        sums[11],
        sums[9],
        sums[10],
        up_grad,
        up_sums,
        down_grad,
        sums[8],
        sums[6],
        sums[7],
        head_grad.astype(jnp.float32),
        sums[0],
        sums[1],
        sums[2],
        decoder_grad,
        decoder_bias_grad,
    )


def solution(mesh):
    cut, rows = P(("dp", "bal"), None), P(("dp", "bal"))
    whole = P()
    return jax.shard_map(
        per_device,
        mesh=mesh,
        in_specs=(
            cut, cut, rows, cut, rows, cut, whole, whole, cut, whole, whole, whole,
            cut, whole, cut, whole, whole, whole, cut, whole, whole, whole, cut, whole,
        ),
        out_specs=(
            cut, whole, cut, cut, whole, whole, cut, whole, whole, whole, cut,
            whole, cut, whole, whole, whole, cut, whole, whole, whole, cut, whole,
        ),
        check_vma=False,
    )
```

```python
import functools

import jax
import jax.numpy as jnp
import numpy as np
from jax import lax
from jax.experimental import pallas as pl
from jax.experimental.pallas import tpu as pltpu
from jax.sharding import PartitionSpec as P

HDIM = 64
HEAD_DEV = 32
MASK_DEV = 64


EPSILON = 1e-06
MASK_FILL = -1e30
AXES = ("dp", "bal")
LOW = jnp.bfloat16


def gelu_exact(values):
    return jax.nn.gelu(values, approximate=False)


def product(left_mat, right_mat):
    return jnp.dot(left_mat, right_mat, preferred_element_type=jnp.float32)


def product_tn(left_mat, right_mat):
    return lax.dot_general(
        left_mat, right_mat, (((0,), (0,)), ((), ())), preferred_element_type=jnp.float32
    )


def product_nt(left_mat, right_mat):
    return lax.dot_general(
        left_mat, right_mat, (((1,), (1,)), ((), ())), preferred_element_type=jnp.float32
    )


def norm_parts(hidden):
    average = jnp.mean(hidden, axis=-1, keepdims=True)
    centered = hidden - average
    inv_std = lax.rsqrt(jnp.mean(centered * centered, axis=-1, keepdims=True) + EPSILON)
    return centered * inv_std, inv_std


def norm_back(normal, inv_std, gain_vec, grad):
    scaled = grad * gain_vec
    first = jnp.mean(scaled, axis=-1, keepdims=True)
    second = jnp.mean(scaled * normal, axis=-1, keepdims=True)
    return (
        inv_std * (scaled - first - normal * second),
        jnp.sum(grad * normal, axis=0),
        jnp.sum(grad, axis=0),
    )


class Grid:
    def __init__(self, dp_size, bal_size):
        self.high = 4 if dp_size % 4 == 0 else 1
        self.low = dp_size // self.high
        self.wide = bal_size // 2
        self.sizes = (self.high, self.low, self.wide, 2)
        self.count = dp_size * bal_size
        dp_place, bal_place = lax.axis_index("dp"), lax.axis_index("bal")
        self.place = (
            dp_place // self.low,
            dp_place % self.low,
            bal_place // 2,
            bal_place % 2,
        )
        self.crossed = self.low == self.wide

    def index(self, spot):
        high, low, wide, core = spot
        return ((high * self.low + low) * self.wide + wide) * 2 + core

    def spots(self):
        for high in range(self.high):
            for low in range(self.low):
                for wide in range(self.wide):
                    for core in range(2):
                        yield (high, low, wide, core)

    def shift(self, value, axis_of, step):
        pairs = []
        for spot in self.spots():
            axis = axis_of[spot[3]]
            target = list(spot)
            target[axis] = (spot[axis] + step) % self.sizes[axis]
            pairs.append((self.index(spot), self.index(target)))
        self.sent = value
        return lax.ppermute(value, AXES, pairs)

    def own(self, axis_of):
        first, second = self.place[axis_of[0]], self.place[axis_of[1]]
        return first if axis_of[0] == axis_of[1] else jnp.where(self.place[3] == 0, first, second)

    def orders(self):
        return ((1, 2), (2, 1)) if self.crossed else ((1, 1), (2, 2))

    def gather_stage(self, value, axis_of):
        size = self.sizes[axis_of[0]]
        me = self.own(axis_of)
        parts = [value] + [self.shift(value, axis_of, step) for step in range(1, size)]

        def join(hold):
            rel = (me + hold - jnp.arange(size)) % size
            rel = rel.reshape((size,) + (1,) * value.ndim)
            out = parts[-1][None]
            for step in range(size - 2, -1, -1):
                out = jnp.where(rel == step, parts[step][None], out)
            return out

        return join

    def halves(self, first, second, hold=0):
        is_first = self.place[3] + hold == 0
        return lax.select(is_first, first, second), lax.select(is_first, second, first)

    def gather_steps(self, height):
        core = self.place[3]
        first, second = self.orders()

        def start(pair):
            keep, give = pair
            taken = self.shift(give, (3, 3), 1)

            def join(hold):
                is_own = (jnp.arange(2) == core + hold)[:, None, None]
                return jnp.where(is_own, keep[None], taken[None])

            return join

        def third(part):
            other = self.gather_stage(part, second)

            def straight(hold):
                joined = other(hold)
                out = joined.transpose(2, 1, 0, 3, 4, 5)
                if self.crossed:
                    turned = joined.transpose(2, 0, 1, 3, 4, 5)
                    out = lax.select(core == 0, out, turned)
                out = lax.optimization_barrier(out)
                return out.reshape(self.count * height, part.shape[-1])

            return straight

        def last(mine):
            other = self.shift(mine, (3, 3), 1)
            return lambda hold: (mine, other)

        return [
            start,
            lambda part: self.gather_stage(part, (0, 0)),
            lambda part: self.gather_stage(part, first),
            third,
            last,
        ]

    def scatter_steps(self, height, taken=None):
        core = self.place[3]
        first, second = self.orders()

        def total(pieces, hold=0):
            out = jnp.asarray(hold).astype(jnp.float32)
            for piece in pieces:
                out = out + piece.astype(jnp.float32)
            return out.astype(LOW)

        def start(pair):
            keep, give = pair
            came = self.shift(give, (3, 3), 1) if taken is None else taken
            shape = (self.high, self.low, self.wide, 2, height, keep.shape[1])
            return lambda hold: ([keep.reshape(shape), came.reshape(shape)], hold)

        def stage(axis_of, piece, hold):
            size = self.sizes[axis_of[0]]
            moved = [self.shift(total(piece(step), hold), axis_of, step) for step in range(1, size)]
            return lambda hold: (piece(0) + moved, hold)

        def cut(given, axis_of, axis):
            parts, hold = given
            size, me = self.sizes[axis_of[0]], self.own(axis_of)

            def piece(step):
                spot = (me + step) % size
                return [lax.dynamic_index_in_dim(part, spot, axis, keepdims=False) for part in parts]

            return stage(axis_of, piece, hold)

        def one(given):
            parts, hold = given
            if not self.crossed:
                return cut(given, second, 2)
            size, me = self.wide, self.own(second)
            flat = [part.reshape(self.high, size * size, *part.shape[3:]) for part in parts]

            def piece(step, along):
                spot = (me + step) % size
                spot = jnp.where(core == 0, along * size + spot, spot * size + along)
                return [lax.dynamic_index_in_dim(part, spot, 1, keepdims=False) for part in flat]

            moved = [
                [self.shift(total(piece(step, along), hold), second, step) for step in range(1, size)]
                for along in range(size)
            ]
            return lambda hold: ([piece(0, along) + moved[along] for along in range(size)], hold)

        def two(given):
            if not self.crossed:
                return cut(given, first, 1)
            columns, hold = given
            size, me = self.low, self.own(first)

            def piece(step):
                spot = (me + step) % size
                out = columns[-1]
                for along in range(size - 2, -1, -1):
                    out = [lax.select(spot == along, *pair) for pair in zip(columns[along], out)]
                return out

            return stage(first, piece, hold)

        def last(given):
            parts, hold = given
            mine = total([lax.dynamic_index_in_dim(part, core, 0, keepdims=False) for part in parts])
            away = total(
                [lax.dynamic_index_in_dim(part, 1 - core, 0, keepdims=False) for part in parts], hold
            )
            other = self.shift(away, (3, 3), 1)
            return lambda hold: (mine, other)

        return [
            start,
            one,
            two,
            lambda given: cut(given, (0, 0), 0),
            last,
        ]

    def group(self):
        return [
            (self.place[2] - wide) % self.wide * 2 + (self.place[3] - core) % 2
            for wide in range(self.wide)
            for core in range(2)
        ]

    def gather_group(self, rows):
        parts = []
        for wide in range(self.wide):
            for core in range(2):
                if wide == 0 and core == 0:
                    parts.append(rows)
                    continue
                pairs = []
                for spot in self.spots():
                    target = (spot[0], spot[1], (spot[2] + wide) % self.wide, (spot[3] + core) % 2)
                    pairs.append((self.index(spot), self.index(target)))
                parts.append(lax.ppermute(rows, AXES, pairs))
        return parts


class Transfer:
    def __init__(self, part, steps):
        self.part = part
        self.steps = list(steps)
        self.join = self.steps.pop(0)(part)

    def step(self, *others):
        self.part = self.join(sum((nothing(other) for other in others), 0))
        self.join = self.steps.pop(0)(self.part)

    def finish(self, *others):
        while self.steps:
            self.step(*others)
            others = ()
        self.part = self.join(sum((nothing(other) for other in others), 0))
        return self.part


def nothing(value):
    hold = 0
    for piece in jax.tree.leaves(value):
        if piece.ndim:
            spot = piece[(0,) * piece.ndim]
            is_float = jnp.issubdtype(spot.dtype, jnp.floating)
            hold = hold + (spot != spot if is_float else spot < -1).astype(jnp.int32)
    return hold


def once(value, *others):
    for other in others:
        value = value + nothing(other).astype(value.dtype)
    return value


def erf_fast(value):
    value = jnp.clip(value, -3.832506856900711, 3.832506856900711)
    square = value * value
    top = jnp.float32(0.00022905065861350646)
    for number in (0.0034082910107109506, 0.050955695062380861, 0.18520832239976145, 1.128379143519084):
        top = top * square + number
    low = jnp.float32(-1.1791602954361697e-7)
    for number in (
        0.000023547966471313185,
        0.0010179625278914885,
        0.014070470171167667,
        0.11098505178285362,
        0.49746925110067538,
        1.0,
    ):
        low = low * square + number
    return value * top / low


def gelu_fast(value):
    return 0.5 * value * (1.0 + erf_fast(value * 0.7071067811865476))


def gelu_slope(value):
    bell = jnp.exp(value * value * -0.5) * 0.3989422804014327
    return 0.5 * (1.0 + erf_fast(value * 0.7071067811865476)) + value * bell


def call_after(kernel, others, in_specs, **settings):
    others = jax.tree.leaves(others)

    def run(*refs):
        kernel(*refs[len(others) :])

    call = pl.pallas_call(
        run, in_specs=[pl.BlockSpec(memory_space=pl.ANY)] * len(others) + in_specs, **settings
    )
    return lambda *operands: call(*others, *operands)


def load_weights(packed_ref, weights_ref, sems):
    count, _, width = weights_ref.shape
    copies = []
    order = [part * (count // 2) + block for block in range(count // 2) for part in range(2)]
    for block in order:
        source = packed_ref.at[:, block * width : (block + 1) * width]
        copies.append((block, pltpu.make_async_copy(source, weights_ref.at[block], sems.at[block])))
        copies[-1][1].start()
    return dict(copies)


def feed_forward_kernel(
    spot_out,
    context_ref,
    tokens_ref,
    out_ref,
    vectors_ref,
    up_bias_ref,
    packed_ref,
    layer_ref,
    normed_ref,
    one_ref,
    total_ref,
    weights_ref,
    sems,
):
    copies = load_weights(packed_ref, weights_ref, sems)
    blocks = len(copies) // 2
    width = tokens_ref.shape[1]
    resid = tokens_ref[spot_out, :].astype(jnp.float32)
    resid = resid + product(context_ref[spot_out, :], out_ref[...])
    resid = resid + vectors_ref[0:1, :]
    one_ref[...] = resid
    normed = norm_parts(resid)[0] * vectors_ref[1:2, :] + vectors_ref[2:3, :]
    normed = normed.astype(LOW)
    normed_ref[...] = normed
    total_ref[...] = normed.astype(jnp.float32) + vectors_ref[3:4, :]
    rows = total_ref.shape[0]
    parts = max(1, rows // 128)
    for block in range(blocks):
        copies[block].wait()
        copies[blocks + block].wait()
        bias = up_bias_ref[:, block * width : (block + 1) * width]
        for part in range(parts):
            spot = slice(part * (rows // parts), (part + 1) * (rows // parts))
            up = product(normed_ref[spot, :], weights_ref[block])
            hidden = gelu_fast(up + bias).astype(LOW)
            total_ref[spot, :] += product(hidden, weights_ref[blocks + block])
    layer = norm_parts(total_ref[...])[0] * vectors_ref[4:5, :] + vectors_ref[5:6, :]
    layer_ref[spot_out, :] = layer.astype(LOW)


def square_scratch(packed, width):
    count = packed.shape[1] // width
    return [pltpu.VMEM((count, width, width), LOW), pltpu.SemaphoreType.DMA((count,))]


def feed_forward_more_kernel(spot, into_ref, *refs):
    layer_ref = refs[6]
    layer_ref[: spot.start, :] = into_ref[: spot.start, :]
    feed_forward_kernel(spot, *refs)


def feed_forward(context, tokens, out_full, vectors, packed, up_bias, others, room, part=0, parts=1, into=None):
    rows, width = tokens.shape[0] // parts, tokens.shape[1]
    units = packed.shape[1] // 2
    spot = slice(part * rows, (part + 1) * rows)
    more = () if into is None else (into,)
    kernel = functools.partial(feed_forward_kernel, spot)
    if more:
        kernel = functools.partial(feed_forward_more_kernel, spot)
    others = jax.tree.leaves(others)
    return call_after(
        kernel,
        others,
        [pl.BlockSpec(memory_space=pltpu.VMEM)] * (5 + len(more))
        + [pl.BlockSpec(memory_space=pltpu.HBM)],
        out_shape=[
            jax.ShapeDtypeStruct((parts * rows, width), LOW),
            jax.ShapeDtypeStruct((rows, width), LOW),
            jax.ShapeDtypeStruct((rows, width), jnp.float32),
            jax.ShapeDtypeStruct((rows, width), jnp.float32),
        ],
        scratch_shapes=square_scratch(packed, width),
        compiler_params=pltpu.CompilerParams(vmem_limit_bytes=room * 1024 * 1024),
        cost_estimate=pl.CostEstimate(
            flops=4 * rows * width * units,
            bytes_accessed=4 * width * units,
            transcendentals=rows * units,
        ),
    )(*more, context, tokens, out_full, vectors, up_bias[None, :], packed)


def feed_back_kernel(
    grad_ref,
    one_ref,
    two_ref,
    normed_ref,
    vectors_ref,
    more_ref,
    up_bias_ref,
    packed_ref,
    send_ref,
    done_ref,
    total_ref,
    sums_ref,
    weights_ref,
    sems,
):
    copies = load_weights(packed_ref, weights_ref, sems)
    blocks = len(copies) // 2
    width = normed_ref.shape[1]
    sums_ref[...] = jnp.zeros_like(sums_ref)
    sums_ref[0:6, :] = more_ref[0:6, :]

    def norm_grad(resid, gain, grad, row):
        normal, inv_std = norm_parts(resid)
        dresid, gain_part, shift_part = norm_back(normal, inv_std, gain, grad)
        sums_ref[row : row + 1, :] = gain_part[None]
        sums_ref[row + 1 : row + 2, :] = shift_part[None]
        sums_ref[row + 2 : row + 3, :] = jnp.sum(
            dresid.astype(LOW).astype(jnp.float32), axis=0, keepdims=True
        )
        return dresid

    dtwo = norm_grad(two_ref[...], vectors_ref[4:5, :], grad_ref[...].astype(jnp.float32), 6)
    total_ref[...] = dtwo
    ddown = dtwo.astype(LOW)
    send_ref[:, :width] = ddown
    for block in range(blocks):
        copies[block].wait()
        copies[blocks + block].wait()
        spot = slice(block * width, (block + 1) * width)
        up = product(normed_ref[...], weights_ref[block]) + up_bias_ref[:, spot]
        dup = (gelu_slope(up) * product_nt(ddown, weights_ref[blocks + block])).astype(LOW)
        sums_ref[12 + block : 13 + block, :] = jnp.sum(
            dup.astype(jnp.float32), axis=0, keepdims=True
        )
        total_ref[...] += product_nt(dup, weights_ref[block])
    done_ref[...] = norm_grad(one_ref[...], vectors_ref[1:2, :], total_ref[...], 9).astype(LOW)
    half = width // 2
    send_ref[:16, width:] = sums_ref[:, :half].astype(LOW)
    send_ref[16:, width:] = sums_ref[:, half:].astype(LOW)


def feed_back(grad, resid_one, resid_two, normed, vectors, more, packed, up_bias, others):
    rows, width = normed.shape
    units = packed.shape[1] // 2
    return call_after(
        feed_back_kernel,
        others,
        [pl.BlockSpec(memory_space=pltpu.VMEM)] * 7
        + [pl.BlockSpec(memory_space=pltpu.HBM)],
        out_shape=[
            jax.ShapeDtypeStruct((rows, width + width // 2), LOW),
            jax.ShapeDtypeStruct((rows, width), LOW),
        ],
        scratch_shapes=[
            pltpu.VMEM((rows, width), jnp.float32),
            pltpu.VMEM((16, width), jnp.float32),
        ]
        + square_scratch(packed, width),
        compiler_params=pltpu.CompilerParams(vmem_limit_bytes=24 * 1024 * 1024),
        cost_estimate=pl.CostEstimate(
            flops=6 * rows * width * units,
            bytes_accessed=4 * width * units,
            transcendentals=rows * units,
        ),
    )(grad, resid_one, resid_two, normed, vectors, more, up_bias[None, :], packed)


def segment_rows(seg_ref):
    rows = lax.broadcasted_iota(jnp.int32, (8, seg_ref.shape[1]), 0)
    return (rows == seg_ref[...]).astype(jnp.float32).astype(LOW)


def attention_kernel(tokens_ref, weight_ref, bias_ref, seg_ref, qkv_ref, context_ref):
    width = context_ref.shape[1]
    rows = tokens_ref.shape[0]
    qkv = product(tokens_ref[...], weight_ref[:, : 3 * width])
    qkv_ref[...] = (qkv + bias_ref[...]).astype(LOW)
    block = rows // 2
    segments = segment_rows(seg_ref)
    same_seg = product_tn(segments, segments) > 0.5
    for head in range(width // HDIM):
        lanes = [slice(i * width + head * HDIM, i * width + (head + 1) * HDIM) for i in range(3)]
        key, value = qkv_ref[:, lanes[1]], qkv_ref[:, lanes[2]]
        for part in range(2):
            spot = slice(part * block, (part + 1) * block)
            query = qkv_ref[spot, lanes[0]] * jnp.asarray(HDIM ** (-0.5), LOW)
            scores = lax.dot_general(
                query, key, (((1,), (1,)), ((), ())), preferred_element_type=jnp.float32
            )
            scores = jnp.where(same_seg[spot, :], scores, MASK_FILL)
            exp_scores = jnp.exp(scores - jnp.max(scores, axis=-1, keepdims=True))
            probs = exp_scores * (1.0 / jnp.sum(exp_scores, axis=-1, keepdims=True))
            context_ref[spot, lanes[0]] = jnp.dot(
                probs.astype(LOW), value, preferred_element_type=jnp.float32
            ).astype(LOW)


def attention(tokens, weight, bias, segment_ids, others=()):
    rows = tokens.shape[0]
    width = bias.shape[1] // 3
    return call_after(
        attention_kernel,
        others,
        [pl.BlockSpec(memory_space=pltpu.VMEM)] * 4,
        out_shape=[
            jax.ShapeDtypeStruct((rows, 3 * width), LOW),
            jax.ShapeDtypeStruct((rows, width), LOW),
        ],
        compiler_params=pltpu.CompilerParams(vmem_limit_bytes=24 * 1024 * 1024),
        cost_estimate=pl.CostEstimate(
            flops=2 * rows * width * (3 * tokens.shape[1] + 2 * rows),
            bytes_accessed=2 * rows * tokens.shape[1] + 2 * weight.size,
            transcendentals=rows * rows * width // HDIM,
        ),
    )(tokens, weight, bias, segment_ids)


def attention_back_kernel(
    scale, queries_ref, first_ref, second_ref, grad_ref, seg_ref, pick_ref, turned_ref,
    beside_ref, first_grad_ref, first_term_ref, second_grad_ref, second_term_ref, sums_ref, dqueries_ref,
):
    segments = segment_rows(seg_ref)
    listed = product_nt(segments, pick_ref[...]).astype(LOW)
    same_seg = product_tn(listed, segments) > 0.5
    width = first_ref.shape[1] // 3
    sums_ref[...] = jnp.zeros_like(sums_ref)

    def dot(left, right, left_dim, right_dim):
        return lax.dot_general(
            left,
            right,
            (((left_dim,), (right_dim,)), ((), ())),
            preferred_element_type=jnp.float32,
        )

    halves = (
        (0, first_ref, first_grad_ref, first_term_ref),
        (1, second_ref, second_grad_ref, second_term_ref),
    )
    for half, qkv_ref, dqkv_ref, term_ref in halves:
        for head in range(width // HDIM):
            lanes = slice(half * width + head * HDIM, half * width + (head + 1) * HDIM)
            keys = slice(width + head * HDIM, width + (head + 1) * HDIM)
            values = slice(2 * width + head * HDIM, 2 * width + (head + 1) * HDIM)
            query, grad = queries_ref[:, lanes], grad_ref[:, lanes]
            key, value = qkv_ref[:, keys], qkv_ref[:, values]
            scores = jnp.where(same_seg, dot(query, key, 1, 1) * scale, MASK_FILL)
            exp_scores = jnp.exp(scores - jnp.max(scores, axis=-1, keepdims=True))
            probs = exp_scores / jnp.sum(exp_scores, axis=-1, keepdims=True)
            dprobs = dot(grad, value, 1, 1)
            dscores = probs * (dprobs - jnp.sum(probs * dprobs, axis=-1, keepdims=True))
            dscores = dscores.astype(LOW)
            dqueries_ref[:, lanes] = (dot(dscores, key, 1, 0) * scale).astype(LOW)
            dqkv_ref[:, keys] = (dot(dscores, query, 0, 0) * scale).astype(LOW)
            dqkv_ref[:, values] = dot(probs.astype(LOW), grad, 0, 0).astype(LOW)
        lanes = slice(half * width, (half + 1) * width)
        dqkv_ref[:, :width] = dot(pick_ref[...], dqueries_ref[:, lanes], 0, 0).astype(LOW)
        term_ref[:, : 3 * width] = product(turned_ref[...], dqkv_ref[...]).astype(LOW)
        term_ref[:, 3 * width :] = beside_ref[:, 2 * half * width : 2 * (half + 1) * width]
        sums_ref[0:1, lanes] = jnp.sum(
            dqueries_ref[:, lanes].astype(jnp.float32), axis=0, keepdims=True
        )
        sums_ref[1:2, lanes] = jnp.sum(
            dqkv_ref[:, 2 * width :].astype(jnp.float32), axis=0, keepdims=True
        )


def attention_back(queries, first, second, grad, segment_ids, pick, turned, beside, others):
    listed = queries.shape[0]
    rows, width = first.shape
    term = (turned.shape[0], width + beside.shape[1] // 2)
    return call_after(
        functools.partial(attention_back_kernel, HDIM ** (-0.5)),
        others,
        [pl.BlockSpec(memory_space=pltpu.VMEM)] * 8,
        out_shape=[
            jax.ShapeDtypeStruct((rows, width), LOW),
            jax.ShapeDtypeStruct(term, LOW),
            jax.ShapeDtypeStruct((rows, width), LOW),
            jax.ShapeDtypeStruct(term, LOW),
            jax.ShapeDtypeStruct((8, queries.shape[1]), jnp.float32),
        ],
        scratch_shapes=[pltpu.VMEM(queries.shape, LOW)],
        compiler_params=pltpu.CompilerParams(vmem_limit_bytes=32 * 1024 * 1024),
        cost_estimate=pl.CostEstimate(
            flops=20 * listed * rows * width // 3 + 4 * turned.size * width,
            bytes_accessed=20 * rows * width // 3,
            transcendentals=2 * listed * rows * width // (3 * HDIM),
        ),
    )(queries, first, second, grad, segment_ids, pick, turned, beside)


def turn_row(row):
    return jnp.transpose(jnp.broadcast_to(row, (128, row.shape[1])))[:, 0:1]


def turn_column(column):
    return jnp.transpose(jnp.broadcast_to(column, (column.shape[0], 128)))[0:1, :]


def core_rows(words_ref, core):
    half = words_ref.shape[0] // 2
    mine = words_ref[pl.ds(pl.multiple_of(core * half, 128), half), :]
    other = words_ref[pl.ds(pl.multiple_of((1 - core) * half, 128), half), :]
    return mine, other


def logits_kernel(vocab_size, place_ref, mine_ref, other_ref, words_ref, bias_ref, logits_ref, log_ref):
    words_mine, words_other = core_rows(words_ref, place_ref[0])
    logits = product(mine_ref[...], words_mine) + product(other_ref[...], words_other) + bias_ref[...]
    ids = lax.broadcasted_iota(jnp.int32, logits.shape, 1) + place_ref[1]
    logits = jnp.where(ids < vocab_size, logits, MASK_FILL)
    logits_ref[...] = logits
    peak = jnp.max(logits, axis=1, keepdims=True)
    log_ref[...] = turn_column(
        peak + jnp.log(jnp.sum(jnp.exp(logits - peak), axis=1, keepdims=True))
    )


def dlogits_kernel(
    inv_count, place_ref, logits_ref, log_ref, labels_ref, words_ref, dlogits_ref, mine_ref, other_ref, sums_ref
):
    @pl.when(pl.program_id(0) == 0)
    def _():
        sums_ref[...] = jnp.zeros_like(sums_ref)

    logits = logits_ref[...]
    ids = lax.broadcasted_iota(jnp.int32, logits.shape, 1) + place_ref[1]
    is_label = ids.astype(jnp.float32) == turn_row(labels_ref[...])
    grads = jnp.exp(logits - turn_row(log_ref[...])) - jnp.where(is_label, 1.0, 0.0)
    grads = (grads * inv_count).astype(LOW)
    dlogits_ref[...] = grads
    words_mine, words_other = core_rows(words_ref, place_ref[0])
    other_ref[...] = product_nt(grads, words_other).astype(LOW)
    mine_ref[...] = product_nt(grads, words_mine).astype(LOW)
    sums_ref[0:1, :] += jnp.sum(grads.astype(jnp.float32), axis=0, keepdims=True)
    sums_ref[1:2, :] += jnp.sum(jnp.where(is_label, logits, 0.0), axis=0, keepdims=True)


def words_grad_kernel(place_ref, mine_ref, other_ref, dlogits_ref, grad_ref):
    half = mine_ref.shape[1]
    core = place_ref[0]
    grads = dlogits_ref[...]
    for spot, rows_ref in ((core, mine_ref), (1 - core, other_ref)):
        lanes = pl.ds(pl.multiple_of(spot * half, 128), half)
        grad_ref[lanes, :] = product_tn(rows_ref[...], grads).astype(LOW)


def row_blocks(slots):
    rows = min(256, slots)
    return (
        slots // rows,
        lambda width: pl.BlockSpec((rows, width), lambda step: (step, 0)),
        pl.BlockSpec((1, rows), lambda step: (0, step)),
    )


def whole_block(*shape):
    return pl.BlockSpec(shape, lambda step: (0,) * len(shape))


def part_logits(place, mine, other, words, bias, vocab_size):
    slots, half = mine.shape
    width = words.shape[1]
    steps, rows_of, line = row_blocks(slots)
    return pl.pallas_call(
        functools.partial(logits_kernel, vocab_size),
        grid=(steps,),
        in_specs=[
            pl.BlockSpec(memory_space=pltpu.SMEM),
            rows_of(half),
            rows_of(half),
            whole_block(2 * half, width),
            whole_block(1, width),
        ],
        out_specs=[rows_of(width), line],
        out_shape=[
            jax.ShapeDtypeStruct((slots, width), jnp.float32),
            jax.ShapeDtypeStruct((1, slots), jnp.float32),
        ],
        compiler_params=pltpu.CompilerParams(vmem_limit_bytes=24 * 1024 * 1024),
        cost_estimate=pl.CostEstimate(
            flops=4 * slots * half * width,
            bytes_accessed=4 * slots * width + 4 * half * (slots + width),
            transcendentals=slots * width,
        ),
    )(place, mine, other, words, bias)


def part_dlogits(place, logits, log_total, labels, words, inv_count):
    slots, width = logits.shape
    half = words.shape[0] // 2
    steps, rows_of, line = row_blocks(slots)
    return pl.pallas_call(
        functools.partial(dlogits_kernel, inv_count),
        grid=(steps,),
        in_specs=[
            pl.BlockSpec(memory_space=pltpu.SMEM),
            rows_of(width),
            line,
            line,
            whole_block(2 * half, width),
        ],
        out_specs=[rows_of(width), rows_of(half), rows_of(half), whole_block(8, width)],
        out_shape=[
            jax.ShapeDtypeStruct((slots, width), LOW),
            jax.ShapeDtypeStruct((slots, half), LOW),
            jax.ShapeDtypeStruct((slots, half), LOW),
            jax.ShapeDtypeStruct((8, width), jnp.float32),
        ],
        compiler_params=pltpu.CompilerParams(vmem_limit_bytes=24 * 1024 * 1024),
        cost_estimate=pl.CostEstimate(
            flops=4 * slots * half * width,
            bytes_accessed=6 * slots * width + 4 * half * (slots + width),
            transcendentals=slots * width,
        ),
    )(place, logits, log_total, labels, words)


def part_words_grad(place, mine, other, dlogits):
    slots, half = mine.shape
    width = dlogits.shape[1]
    return pl.pallas_call(
        words_grad_kernel,
        in_specs=[pl.BlockSpec(memory_space=pltpu.SMEM)] + [pl.BlockSpec(memory_space=pltpu.VMEM)] * 3,
        out_shape=jax.ShapeDtypeStruct((2 * half, width), LOW),
        compiler_params=pltpu.CompilerParams(vmem_limit_bytes=32 * 1024 * 1024),
        cost_estimate=pl.CostEstimate(
            flops=4 * slots * half * width,
            bytes_accessed=2 * slots * width + 4 * half * (slots + width),
            transcendentals=0,
        ),
    )(place, mine, other, dlogits)


def heads_of(rows):
    return rows.reshape(rows.shape[0], rows.shape[1] // HDIM, HDIM)


def attention_probs(queries, key_rows, query_seg, key_seg):
    scores = jnp.einsum(
        "qhd,khd->hqk", queries, key_rows, preferred_element_type=jnp.float32
    ) * HDIM ** (-0.5)
    same_seg = query_seg[:, None] == key_seg[None, :]
    masked = jnp.where(same_seg[None], scores, MASK_FILL)
    row_peak = jnp.max(masked, axis=-1, keepdims=True)
    exp_scores = jnp.exp(masked - row_peak)
    return exp_scores / jnp.sum(exp_scores, axis=-1, keepdims=True)


def per_device(
    tokens,
    segment_ids,
    mlm_labels,
    mask_order,
    mask_count,
    qkv_weight,
    query_bias,
    value_bias,
    out_weight,
    out_bias,
    attn_gain,
    attn_shift,
    up_weight,
    up_bias,
    down_weight,
    down_bias,
    ffn_gain,
    ffn_shift,
    head_weight,
    head_bias,
    head_gain,
    head_shift,
    decoder,
    decoder_bias,
):
    model_width = tokens.shape[1]
    tok_rows = tokens.shape[0]
    vocab_size = decoder.shape[1]
    bal_size = lax.axis_size("bal")
    dp_size = lax.axis_size("dp")
    bal_place = lax.axis_index("bal")
    dp_place = lax.axis_index("dp")
    grid = Grid(dp_size, bal_size)
    device_count = dp_size * bal_size
    my_place = dp_place * bal_size + bal_place
    slot_count = HEAD_DEV * device_count
    inv_count = 1.0 / slot_count
    part_vocab = -(-(-(-vocab_size // device_count)) // 128) * 128

    listed = mask_order[0, :MASK_DEV]
    pick_mat = listed[:, None] == jnp.arange(tok_rows)[None, :]
    pick_low = pick_mat.astype(LOW)

    def pick(rows):
        return product(pick_low, rows).astype(LOW)

    listed_ids = jnp.sum(jnp.where(pick_mat, mlm_labels[None, :], 0), axis=1)

    shard_rows = qkv_weight.shape[0]
    my_units = down_weight.shape[0]
    units = my_units * device_count
    ratio = my_units // shard_rows
    half = model_width // 2

    def unit_order(rows):
        split = rows.reshape(rows.shape[0], device_count, ratio, shard_rows)
        return split.transpose(0, 2, 1, 3).reshape(rows.shape[0], units)

    down_wide = down_weight.reshape(ratio, shard_rows, model_width).transpose(1, 0, 2)
    down_wide = down_wide.reshape(shard_rows, ratio * model_width)
    packed = lax.all_gather(
        jnp.concatenate([unit_order(up_weight), down_wide], axis=1), AXES, axis=0, tiled=True
    )
    up_offsets = unit_order(up_bias[None])[0]
    my_offsets = lax.dynamic_slice_in_dim(up_bias, my_place * my_units, my_units)

    def by_heads(rows):
        split = rows.reshape(rows.shape[0], 3, 2, half)
        return grid.halves(
            split[:, :, 0].reshape(rows.shape[0], 3 * half),
            split[:, :, 1].reshape(rows.shape[0], 3 * half),
        )

    info = jnp.concatenate([listed_ids, mask_count, jnp.zeros((63,), jnp.int32)])
    info = grid.gather_group(info[None])
    weights_run = Transfer(by_heads(qkv_weight), grid.gather_steps(shard_rows))
    both_run = Transfer(grid.halves(out_weight, head_weight), grid.gather_steps(shard_rows))
    qkv_width = 3 * half
    weights_run.step()
    weights_run.step()
    weights_run.step()
    all_mine, all_other = weights_run.finish()
    both_run.step()

    info = jnp.concatenate(info)
    group = jnp.stack(grid.group())
    counts = info[:, MASK_DEV]
    before = group[None, :] < group[:, None]
    starts = jnp.sum(jnp.where(before, counts[None, :], 0), axis=1)
    steps = jnp.arange(MASK_DEV)
    slot_of = jnp.where(steps[None] < counts[:, None], starts[:, None] + steps[None], -1)
    my_slots = bal_place * HEAD_DEV + jnp.arange(HEAD_DEV)
    is_mine = slot_of[None] == my_slots[:, None, None]
    my_labels = jnp.sum(jnp.where(is_mine, info[None, :, :MASK_DEV], 0), axis=(1, 2))
    to_head = is_mine.astype(LOW)
    group_slots = group[:, None] * HEAD_DEV + jnp.arange(HEAD_DEV)[None, :]
    from_head = (slot_of[0][:, None, None] == group_slots[None]).astype(LOW)

    def choose(choice, parts):
        total = product(choice[:, 0], parts[0])
        for index, part in enumerate(parts[1:], 1):
            total = total + product(choice[:, index], part)
        return total.astype(LOW)

    tokens_s = pick(tokens)

    bias_mine, bias_other = by_heads(
        jnp.concatenate([query_bias, jnp.zeros_like(query_bias), value_bias])[None]
    )
    parts_mine, context_mine = attention(
        tokens, all_mine, bias_mine, segment_ids, []
    )
    padded = lax.pad(
        decoder,
        nothing(context_mine).astype(LOW),
        ((0, 0, 0), (0, part_vocab * device_count - vocab_size, 0)),
    )
    padded = padded.reshape(decoder.shape[0], device_count, part_vocab).transpose(1, 0, 2)
    parts_other, context_other = attention(tokens, all_other, bias_other, segment_ids, [context_mine])
    both_run.step(context_mine)
    both_run.step()
    both_run.step(context_other)
    out_full, head_full = grid.halves(*both_run.finish())
    context = jnp.concatenate(grid.halves(context_mine, context_other), axis=1)
    words = lax.all_to_all(padded, AXES, split_axis=0, concat_axis=0, tiled=True)

    picked = [tokens_s, *grid.halves(pick(context_mine), pick(context_other))]
    group_rows = grid.gather_group(jnp.concatenate(picked, axis=1))
    listed_queries = jnp.concatenate(
        [pick(parts_mine[:, :half]), pick(parts_other[:, :half])], axis=1
    )
    slot_rows = choose(to_head, group_rows)
    tokens_own, context_own = slot_rows[:, :model_width], slot_rows[:, model_width:]
    vectors = jnp.stack(
        [out_bias, attn_gain, attn_shift, down_bias, ffn_gain, ffn_shift, out_bias, out_bias]
    )
    window = min(256, model_width)
    begin = jnp.minimum(my_place * shard_rows // 128 * 128, model_width - window)
    lanes = jnp.arange(window)[:, None] + begin - my_place * shard_rows
    unit_ids = np.arange(my_units)
    my_columns = jnp.zeros((model_width, my_units), jnp.float32)
    for block in range(ratio):
        piece = lax.dynamic_slice_in_dim(packed, block * model_width + begin, window, 1)
        wanted = np.where(unit_ids // shard_rows == block, unit_ids % shard_rows, -model_width)
        is_unit = lanes == jnp.asarray(wanted, jnp.int32)[None, :]
        my_columns = my_columns + product(piece, is_unit.astype(LOW))
    my_columns = my_columns.astype(LOW)


    def layer_part(part, others, room, into=None):
        return feed_forward(
            context, tokens, out_full, vectors, packed, up_offsets, others, room, part, 2, into
        )[0]

    head_in, normed_own, resid_one, resid_two = feed_forward(
        context_own, tokens_own, out_full, vectors, packed, up_offsets, [listed_queries], 24
    )

    rows_all = lax.all_gather(normed_own, AXES, axis=0, tiled=True)
    up_all = product(rows_all, my_columns) + my_offsets

    inner_rows = product(head_in, head_full) + head_bias
    head_act, act_back = jax.vjp(gelu_exact, inner_rows)
    head_normal, head_inv = norm_parts(head_act)
    head_normed = (head_normal * head_gain + head_shift).astype(LOW)
    head_run = Transfer(
        grid.halves(head_normed[:, :half], head_normed[:, half:]), grid.gather_steps(HEAD_DEV)
    )
    head_run.step(lax.dynamic_slice(words, (nothing(head_in), 0, 0), (1, 1, 1)))
    head_run.step()
    head_run.step()
    head_run.step()
    normed_mine, normed_other = head_run.finish()
    words = words.reshape(model_width, part_vocab)
    padded_bias = jnp.pad(decoder_bias, (0, part_vocab * device_count - vocab_size))
    words_bias = lax.dynamic_slice_in_dim(padded_bias, my_place * part_vocab, part_vocab)
    place = jnp.stack([grid.place[3], my_place * part_vocab]).astype(jnp.int32)
    logits, part_log = part_logits(
        place, normed_mine, normed_other, words, words_bias[None], vocab_size
    )
    spread = jnp.concatenate(
        [part_log[0], my_labels.astype(jnp.float32), jnp.zeros((128 - HEAD_DEV,), jnp.float32)]
    )
    spread = jnp.broadcast_to(spread[None, None], (device_count, 1, slot_count + 128))
    spread = lax.all_to_all(spread, AXES, split_axis=0, concat_axis=0, tiled=True)
    spread = spread[:, 0]
    all_logs = spread[:, :slot_count]
    labels = spread[:, slot_count : slot_count + HEAD_DEV].reshape(1, slot_count)
    peak = jnp.max(all_logs, axis=0)
    log_total = peak + jnp.log(jnp.sum(jnp.exp(all_logs - peak), axis=0))
    dlogits, dhead_mine, dhead_other, logit_sums = part_dlogits(
        place, logits, log_total[None], labels, words, inv_count
    )
    head_run = Transfer((dhead_mine, dhead_other), grid.scatter_steps(HEAD_DEV))
    words_grad = part_words_grad(place, normed_mine, normed_other, dlogits)
    head_run.step()
    head_run.step()
    head_run.step()
    head_run.step()
    words_bias_grad = logit_sums[0]
    target_part = jnp.sum(logit_sums[1])
    loss_part = jnp.where(my_place == 0, jnp.sum(log_total), 0.0) - target_part
    dhead_normed = jnp.concatenate(grid.halves(*head_run.finish()), axis=1).astype(jnp.float32)
    dhead_act, head_gain_part, head_shift_part = norm_back(
        head_normal, head_inv, head_gain, dhead_normed
    )
    dinner = act_back(dhead_act)[0].astype(LOW)
    head_bias_part = jnp.sum(dinner, axis=0, dtype=jnp.float32)
    dhead_in = product_nt(dinner, head_full).astype(LOW)

    words_back = lax.all_to_all(
        words_grad.reshape(device_count, decoder.shape[0], part_vocab),
        AXES,
        split_axis=0,
        concat_axis=0,
        tiled=True,
    )

    loss_high = loss_part.astype(LOW).astype(jnp.float32)
    vocab_rows = jnp.pad(words_bias_grad, (0, 2 * model_width - part_vocab))
    more = jnp.stack(
        [
            head_bias_part,
            head_gain_part,
            head_shift_part,
            jnp.where(jnp.arange(model_width) < half, loss_high, loss_part - loss_high),
            vocab_rows[:model_width],
            vocab_rows[model_width:],
            head_bias_part,
            head_bias_part,
        ]
    )
    send, dresid_own = feed_back(
        dhead_in, resid_one, resid_two, normed_own, vectors, more, packed, up_offsets, [up_all, words_grad]
    )
    group_grads = grid.gather_group(dresid_own)
    factors = lax.all_gather(send, AXES, axis=0, tiled=True)

    def two_parts(rows):
        high = rows.astype(LOW)
        return jnp.concatenate([high, (rows - high.astype(jnp.float32)).astype(LOW)])

    out_term = product_tn(context_own, dresid_own).astype(LOW)
    head_term = product_tn(head_in, dinner).astype(LOW)
    beside = jnp.concatenate(grid.halves(out_term, head_term), axis=1)
    dresid_one = choose(from_head, group_grads)
    dcontext = product_nt(dresid_one, out_full).astype(LOW)
    dcontext = jnp.concatenate(grid.halves(dcontext[:, :half], dcontext[:, half:]), axis=1)
    dqkv_mine, mine_term, dqkv_other, other_term, qkv_sums = attention_back(
        listed_queries,
        parts_mine,
        parts_other,
        dcontext,
        segment_ids,
        pick_low,
        tokens.T,
        beside,
        [],
    )
    other_taken = grid.shift(other_term, (3, 3), 1)
    weights_run = Transfer((mine_term, None), grid.scatter_steps(shard_rows, other_taken))
    weights_run.step(words_back)
    first_part = layer_part(0, [grid.sent], 24)
    weights_run.step(first_part)
    qkv_sums = grid.halves(qkv_sums[:2, :half], qkv_sums[:2, half:])
    qkv_sums = two_parts(jnp.concatenate(qkv_sums, axis=1))

    ddown_all = factors[:, :model_width]
    hidden, act_back = jax.vjp(gelu_exact, up_all)
    dup_all = act_back(product_nt(ddown_all, down_weight))[0].astype(LOW)
    up_term = product_tn(rows_all, dup_all).astype(LOW).reshape(device_count, shard_rows, my_units)
    weights_run.step()
    second_part = layer_part(1, [grid.sent], 24, first_part)
    words_back = once(words_back, grid.sent)
    qkv_sums = qkv_sums.reshape(-1, my_units)
    qkv_sums = jnp.broadcast_to(qkv_sums[None], (device_count, *qkv_sums.shape))
    up_back = lax.all_to_all(
        jnp.concatenate([up_term, qkv_sums], axis=1), AXES, split_axis=0, concat_axis=0, tiled=True
    )
    down_grad = product_tn(hidden.astype(LOW), ddown_all)
    up_grad = up_back[:, :shard_rows].transpose(1, 0, 2).reshape(shard_rows, units)
    up_grad = up_grad.astype(jnp.float32)
    qkv_sums = jnp.sum(up_back[:, shard_rows:].astype(jnp.float32), axis=0)
    qkv_sums = jnp.sum(qkv_sums.reshape(2, 2, model_width), axis=0)

    tokens_grad = product_tn(pick_low, once(dresid_one, weights_run.part[0][-1]))
    tokens_grad = tokens_grad + product_nt(dqkv_other, all_other)
    tokens_grad = tokens_grad + product_nt(dqkv_mine, all_mine)
    weights_run.step()
    mine, other = weights_run.finish()
    sums = factors[:, model_width:].astype(jnp.float32).reshape(device_count, 2, 16, half)
    sums = jnp.concatenate([sums[:, 0], sums[:, 1]], axis=2)
    decoder_bias_grad = sums[:, 4:6].reshape(device_count, 2 * model_width)[:, :part_vocab]
    decoder_bias_grad = decoder_bias_grad.reshape(-1)[:vocab_size]
    sums = jnp.sum(sums, axis=0)
    up_sums = sums[12:].reshape(ratio, device_count, shard_rows).transpose(1, 0, 2).reshape(-1)
    first, second = grid.halves(mine[:, :qkv_width], other[:, :qkv_width])
    qkv_grad = jnp.stack(
        [first.reshape(shard_rows, 3, half), second.reshape(shard_rows, 3, half)], axis=2
    )
    qkv_grad = qkv_grad.reshape(shard_rows, 3 * model_width).astype(jnp.float32)
    out_grad, head_grad = grid.halves(mine[:, qkv_width:], other[:, qkv_width:])
    decoder_grad = words_back.transpose(1, 0, 2).reshape(decoder.shape[0], -1)
    decoder_grad = decoder_grad[:, :vocab_size].astype(jnp.float32)
    return (
        second_part,
        (sums[3, 0] + sums[3, half]) * inv_count,
        tokens_grad,
        qkv_grad,
        qkv_sums[0],
        qkv_sums[1],
        out_grad.astype(jnp.float32),
        sums[11],
        sums[9],
        sums[10],
        up_grad,
        up_sums,
        down_grad,
        sums[8],
        sums[6],
        sums[7],
        head_grad.astype(jnp.float32),
        sums[0],
        sums[1],
        sums[2],
        decoder_grad,
        decoder_bias_grad,
    )


def solution(mesh):
    cut, rows = P(("dp", "bal"), None), P(("dp", "bal"))
    whole = P()
    return jax.shard_map(
        per_device,
        mesh=mesh,
        in_specs=(
            cut, cut, rows, cut, rows, cut, whole, whole, cut, whole, whole, whole,
            cut, whole, cut, whole, whole, whole, cut, whole, whole, whole, cut, whole,
        ),
        out_specs=(
            cut, whole, cut, cut, whole, whole, cut, whole, whole, whole, cut,
            whole, cut, whole, whole, whole, cut, whole, whole, whole, cut, whole,
        ),
        check_vma=False,
    )
```

```python
import functools

import jax
import jax.numpy as jnp
import numpy as np
from jax import lax
from jax.experimental import pallas as pl
from jax.experimental.pallas import tpu as pltpu
from jax.sharding import PartitionSpec as P

HDIM = 64
HEAD_DEV = 32
MASK_DEV = 64


EPSILON = 1e-06
MASK_FILL = -1e30
AXES = ("dp", "bal")
LOW = jnp.bfloat16


def gelu_exact(values):
    return jax.nn.gelu(values, approximate=False)


def product(left_mat, right_mat):
    return jnp.dot(left_mat, right_mat, preferred_element_type=jnp.float32)


def product_tn(left_mat, right_mat):
    return lax.dot_general(
        left_mat, right_mat, (((0,), (0,)), ((), ())), preferred_element_type=jnp.float32
    )


def product_nt(left_mat, right_mat):
    return lax.dot_general(
        left_mat, right_mat, (((1,), (1,)), ((), ())), preferred_element_type=jnp.float32
    )


def norm_parts(hidden):
    average = jnp.mean(hidden, axis=-1, keepdims=True)
    centered = hidden - average
    inv_std = lax.rsqrt(jnp.mean(centered * centered, axis=-1, keepdims=True) + EPSILON)
    return centered * inv_std, inv_std


def norm_back(normal, inv_std, gain_vec, grad):
    scaled = grad * gain_vec
    first = jnp.mean(scaled, axis=-1, keepdims=True)
    second = jnp.mean(scaled * normal, axis=-1, keepdims=True)
    return (
        inv_std * (scaled - first - normal * second),
        jnp.sum(grad * normal, axis=0),
        jnp.sum(grad, axis=0),
    )


class Grid:
    def __init__(self, dp_size, bal_size):
        self.high = 4 if dp_size % 4 == 0 else 1
        self.low = dp_size // self.high
        self.wide = bal_size // 2
        self.sizes = (self.high, self.low, self.wide, 2)
        self.count = dp_size * bal_size
        dp_place, bal_place = lax.axis_index("dp"), lax.axis_index("bal")
        self.place = (
            dp_place // self.low,
            dp_place % self.low,
            bal_place // 2,
            bal_place % 2,
        )
        self.crossed = self.low == self.wide

    def index(self, spot):
        high, low, wide, core = spot
        return ((high * self.low + low) * self.wide + wide) * 2 + core

    def spots(self):
        for high in range(self.high):
            for low in range(self.low):
                for wide in range(self.wide):
                    for core in range(2):
                        yield (high, low, wide, core)

    def shift(self, value, axis_of, step):
        pairs = []
        for spot in self.spots():
            axis = axis_of[spot[3]]
            target = list(spot)
            target[axis] = (spot[axis] + step) % self.sizes[axis]
            pairs.append((self.index(spot), self.index(target)))
        self.sent = value
        return lax.ppermute(value, AXES, pairs)

    def own(self, axis_of):
        first, second = self.place[axis_of[0]], self.place[axis_of[1]]
        return first if axis_of[0] == axis_of[1] else jnp.where(self.place[3] == 0, first, second)

    def orders(self):
        return ((1, 2), (2, 1)) if self.crossed else ((1, 1), (2, 2))

    def gather_stage(self, value, axis_of):
        size = self.sizes[axis_of[0]]
        me = self.own(axis_of)
        parts = [value] + [self.shift(value, axis_of, step) for step in range(1, size)]

        def join(hold):
            rel = (me + hold - jnp.arange(size)) % size
            rel = rel.reshape((size,) + (1,) * value.ndim)
            out = parts[-1][None]
            for step in range(size - 2, -1, -1):
                out = jnp.where(rel == step, parts[step][None], out)
            return out

        return join

    def halves(self, first, second, hold=0):
        is_first = self.place[3] + hold == 0
        return lax.select(is_first, first, second), lax.select(is_first, second, first)

    def gather_steps(self, height):
        core = self.place[3]
        first, second = self.orders()

        def start(pair):
            keep, give = pair
            taken = self.shift(give, (3, 3), 1)

            def join(hold):
                is_own = (jnp.arange(2) == core + hold)[:, None, None]
                return jnp.where(is_own, keep[None], taken[None])

            return join

        def third(part):
            other = self.gather_stage(part, second)

            def straight(hold):
                joined = other(hold)
                out = joined.transpose(2, 1, 0, 3, 4, 5)
                if self.crossed:
                    turned = joined.transpose(2, 0, 1, 3, 4, 5)
                    out = lax.select(core == 0, out, turned)
                out = lax.optimization_barrier(out)
                return out.reshape(self.count * height, part.shape[-1])

            return straight

        def last(mine):
            other = self.shift(mine, (3, 3), 1)
            return lambda hold: (mine, other)

        return [
            start,
            lambda part: self.gather_stage(part, (0, 0)),
            lambda part: self.gather_stage(part, first),
            third,
            last,
        ]

    def scatter_steps(self, height, taken=None):
        core = self.place[3]
        first, second = self.orders()

        def total(pieces, hold=0):
            out = jnp.asarray(hold).astype(jnp.float32)
            for piece in pieces:
                out = out + piece.astype(jnp.float32)
            return out.astype(LOW)

        def start(pair):
            keep, give = pair
            came = self.shift(give, (3, 3), 1) if taken is None else taken
            shape = (self.high, self.low, self.wide, 2, height, keep.shape[1])
            return lambda hold: ([keep.reshape(shape), came.reshape(shape)], hold)

        def stage(axis_of, piece, hold):
            size = self.sizes[axis_of[0]]
            moved = [self.shift(total(piece(step), hold), axis_of, step) for step in range(1, size)]
            return lambda hold: (piece(0) + moved, hold)

        def cut(given, axis_of, axis):
            parts, hold = given
            size, me = self.sizes[axis_of[0]], self.own(axis_of)

            def piece(step):
                spot = (me + step) % size
                return [lax.dynamic_index_in_dim(part, spot, axis, keepdims=False) for part in parts]

            return stage(axis_of, piece, hold)

        def one(given):
            parts, hold = given
            if not self.crossed:
                return cut(given, second, 2)
            size, me = self.wide, self.own(second)
            flat = [part.reshape(self.high, size * size, *part.shape[3:]) for part in parts]

            def piece(step, along):
                spot = (me + step) % size
                spot = jnp.where(core == 0, along * size + spot, spot * size + along)
                return [lax.dynamic_index_in_dim(part, spot, 1, keepdims=False) for part in flat]

            moved = [
                [self.shift(total(piece(step, along), hold), second, step) for step in range(1, size)]
                for along in range(size)
            ]
            return lambda hold: ([piece(0, along) + moved[along] for along in range(size)], hold)

        def two(given):
            if not self.crossed:
                return cut(given, first, 1)
            columns, hold = given
            size, me = self.low, self.own(first)

            def piece(step):
                spot = (me + step) % size
                out = columns[-1]
                for along in range(size - 2, -1, -1):
                    out = [lax.select(spot == along, *pair) for pair in zip(columns[along], out)]
                return out

            return stage(first, piece, hold)

        def last(given):
            parts, hold = given
            mine = total([lax.dynamic_index_in_dim(part, core, 0, keepdims=False) for part in parts])
            away = total(
                [lax.dynamic_index_in_dim(part, 1 - core, 0, keepdims=False) for part in parts], hold
            )
            other = self.shift(away, (3, 3), 1)
            return lambda hold: (mine, other)

        return [
            start,
            one,
            two,
            lambda given: cut(given, (0, 0), 0),
            last,
        ]

    def group(self):
        return [
            (self.place[2] - wide) % self.wide * 2 + (self.place[3] - core) % 2
            for wide in range(self.wide)
            for core in range(2)
        ]

    def gather_group(self, rows):
        parts = []
        for wide in range(self.wide):
            for core in range(2):
                if wide == 0 and core == 0:
                    parts.append(rows)
                    continue
                pairs = []
                for spot in self.spots():
                    target = (spot[0], spot[1], (spot[2] + wide) % self.wide, (spot[3] + core) % 2)
                    pairs.append((self.index(spot), self.index(target)))
                parts.append(lax.ppermute(rows, AXES, pairs))
        return parts


class Transfer:
    def __init__(self, part, steps):
        self.part = part
        self.steps = list(steps)
        self.join = self.steps.pop(0)(part)

    def step(self, *others):
        self.part = self.join(sum((nothing(other) for other in others), 0))
        self.join = self.steps.pop(0)(self.part)

    def finish(self, *others):
        while self.steps:
            self.step(*others)
            others = ()
        self.part = self.join(sum((nothing(other) for other in others), 0))
        return self.part


def nothing(value):
    hold = 0
    for piece in jax.tree.leaves(value):
        if piece.ndim:
            spot = piece[(0,) * piece.ndim]
            is_float = jnp.issubdtype(spot.dtype, jnp.floating)
            hold = hold + (spot != spot if is_float else spot < -1).astype(jnp.int32)
    return hold


def once(value, *others):
    for other in others:
        value = value + nothing(other).astype(value.dtype)
    return value


def erf_fast(value):
    value = jnp.clip(value, -3.832506856900711, 3.832506856900711)
    square = value * value
    top = jnp.float32(0.00022905065861350646)
    for number in (0.0034082910107109506, 0.050955695062380861, 0.18520832239976145, 1.128379143519084):
        top = top * square + number
    low = jnp.float32(-1.1791602954361697e-7)
    for number in (
        0.000023547966471313185,
        0.0010179625278914885,
        0.014070470171167667,
        0.11098505178285362,
        0.49746925110067538,
        1.0,
    ):
        low = low * square + number
    return value * top / low


def gelu_fast(value):
    return 0.5 * value * (1.0 + erf_fast(value * 0.7071067811865476))


def gelu_slope(value):
    bell = jnp.exp(value * value * -0.5) * 0.3989422804014327
    return 0.5 * (1.0 + erf_fast(value * 0.7071067811865476)) + value * bell


def call_after(kernel, others, in_specs, **settings):
    others = jax.tree.leaves(others)

    def run(*refs):
        kernel(*refs[len(others) :])

    call = pl.pallas_call(
        run, in_specs=[pl.BlockSpec(memory_space=pl.ANY)] * len(others) + in_specs, **settings
    )
    return lambda *operands: call(*others, *operands)


def load_weights(packed_ref, weights_ref, sems):
    count, _, width = weights_ref.shape
    copies = []
    order = [part * (count // 2) + block for block in range(count // 2) for part in range(2)]
    for block in order:
        source = packed_ref.at[:, block * width : (block + 1) * width]
        copies.append((block, pltpu.make_async_copy(source, weights_ref.at[block], sems.at[block])))
        copies[-1][1].start()
    return dict(copies)


def feed_forward_kernel(
    spot_out,
    context_ref,
    tokens_ref,
    out_ref,
    vectors_ref,
    up_bias_ref,
    packed_ref,
    layer_ref,
    normed_ref,
    one_ref,
    total_ref,
):
    width = tokens_ref.shape[1]
    blocks = packed_ref.shape[1] // (2 * width)
    resid = tokens_ref[spot_out, :].astype(jnp.float32)
    resid = resid + product(context_ref[spot_out, :], out_ref[...])
    resid = resid + vectors_ref[0:1, :]
    one_ref[...] = resid
    normed = norm_parts(resid)[0] * vectors_ref[1:2, :] + vectors_ref[2:3, :]
    normed = normed.astype(LOW)
    normed_ref[...] = normed
    total_ref[...] = normed.astype(jnp.float32) + vectors_ref[3:4, :]
    rows = total_ref.shape[0]
    parts = max(1, rows // 128)
    for block in range(blocks):
        lanes = slice(block * width, (block + 1) * width)
        down_lanes = slice((blocks + block) * width, (blocks + block + 1) * width)
        bias = up_bias_ref[:, lanes]
        for part in range(parts):
            spot = slice(part * (rows // parts), (part + 1) * (rows // parts))
            up = product(normed_ref[spot, :], packed_ref[:, lanes])
            hidden = gelu_fast(up + bias).astype(LOW)
            total_ref[spot, :] += product(hidden, packed_ref[:, down_lanes])
    layer = norm_parts(total_ref[...])[0] * vectors_ref[4:5, :] + vectors_ref[5:6, :]
    layer_ref[spot_out, :] = layer.astype(LOW)


def square_scratch(packed, width):
    count = packed.shape[1] // width
    return [pltpu.VMEM((count, width, width), LOW), pltpu.SemaphoreType.DMA((count,))]


def feed_forward_more_kernel(spot, into_ref, *refs):
    layer_ref = refs[6]
    layer_ref[: spot.start, :] = into_ref[: spot.start, :]
    feed_forward_kernel(spot, *refs)


def feed_forward(context, tokens, out_full, vectors, packed, up_bias, others, room, part=0, parts=1, into=None):
    rows, width = tokens.shape[0] // parts, tokens.shape[1]
    units = packed.shape[1] // 2
    spot = slice(part * rows, (part + 1) * rows)
    more = () if into is None else (into,)
    kernel = functools.partial(feed_forward_kernel, spot)
    if more:
        kernel = functools.partial(feed_forward_more_kernel, spot)
    others = jax.tree.leaves(others)
    return call_after(
        kernel,
        others,
        [pl.BlockSpec(memory_space=pltpu.VMEM)] * (6 + len(more)),
        out_shape=[
            jax.ShapeDtypeStruct((parts * rows, width), LOW),
            jax.ShapeDtypeStruct((rows, width), LOW),
            jax.ShapeDtypeStruct((rows, width), jnp.float32),
            jax.ShapeDtypeStruct((rows, width), jnp.float32),
        ],
        compiler_params=pltpu.CompilerParams(vmem_limit_bytes=room * 1024 * 1024),
        cost_estimate=pl.CostEstimate(
            flops=4 * rows * width * units,
            bytes_accessed=4 * width * units,
            transcendentals=rows * units,
        ),
    )(*more, context, tokens, out_full, vectors, up_bias[None, :], packed)


def feed_back_kernel(
    grad_ref,
    one_ref,
    two_ref,
    normed_ref,
    vectors_ref,
    more_ref,
    up_bias_ref,
    packed_ref,
    send_ref,
    done_ref,
    total_ref,
    sums_ref,
    weights_ref,
    sems,
):
    copies = load_weights(packed_ref, weights_ref, sems)
    blocks = len(copies) // 2
    width = normed_ref.shape[1]
    sums_ref[...] = jnp.zeros_like(sums_ref)
    sums_ref[0:6, :] = more_ref[0:6, :]

    def norm_grad(resid, gain, grad, row):
        normal, inv_std = norm_parts(resid)
        dresid, gain_part, shift_part = norm_back(normal, inv_std, gain, grad)
        sums_ref[row : row + 1, :] = gain_part[None]
        sums_ref[row + 1 : row + 2, :] = shift_part[None]
        sums_ref[row + 2 : row + 3, :] = jnp.sum(
            dresid.astype(LOW).astype(jnp.float32), axis=0, keepdims=True
        )
        return dresid

    dtwo = norm_grad(two_ref[...], vectors_ref[4:5, :], grad_ref[...].astype(jnp.float32), 6)
    total_ref[...] = dtwo
    ddown = dtwo.astype(LOW)
    send_ref[:, :width] = ddown
    for block in range(blocks):
        copies[block].wait()
        copies[blocks + block].wait()
        spot = slice(block * width, (block + 1) * width)
        up = product(normed_ref[...], weights_ref[block]) + up_bias_ref[:, spot]
        dup = (gelu_slope(up) * product_nt(ddown, weights_ref[blocks + block])).astype(LOW)
        sums_ref[12 + block : 13 + block, :] = jnp.sum(
            dup.astype(jnp.float32), axis=0, keepdims=True
        )
        total_ref[...] += product_nt(dup, weights_ref[block])
    done_ref[...] = norm_grad(one_ref[...], vectors_ref[1:2, :], total_ref[...], 9).astype(LOW)
    half = width // 2
    send_ref[:16, width:] = sums_ref[:, :half].astype(LOW)
    send_ref[16:, width:] = sums_ref[:, half:].astype(LOW)


def feed_back(grad, resid_one, resid_two, normed, vectors, more, packed, up_bias, others):
    rows, width = normed.shape
    units = packed.shape[1] // 2
    return call_after(
        feed_back_kernel,
        others,
        [pl.BlockSpec(memory_space=pltpu.VMEM)] * 7
        + [pl.BlockSpec(memory_space=pltpu.HBM)],
        out_shape=[
            jax.ShapeDtypeStruct((rows, width + width // 2), LOW),
            jax.ShapeDtypeStruct((rows, width), LOW),
        ],
        scratch_shapes=[
            pltpu.VMEM((rows, width), jnp.float32),
            pltpu.VMEM((16, width), jnp.float32),
        ]
        + square_scratch(packed, width),
        compiler_params=pltpu.CompilerParams(vmem_limit_bytes=24 * 1024 * 1024),
        cost_estimate=pl.CostEstimate(
            flops=6 * rows * width * units,
            bytes_accessed=4 * width * units,
            transcendentals=rows * units,
        ),
    )(grad, resid_one, resid_two, normed, vectors, more, up_bias[None, :], packed)


def segment_rows(seg_ref):
    rows = lax.broadcasted_iota(jnp.int32, (8, seg_ref.shape[1]), 0)
    return (rows == seg_ref[...]).astype(jnp.float32).astype(LOW)


def attention_kernel(tokens_ref, weight_ref, bias_ref, seg_ref, qkv_ref, context_ref):
    width = context_ref.shape[1]
    rows = tokens_ref.shape[0]
    qkv = product(tokens_ref[...], weight_ref[:, : 3 * width])
    qkv_ref[...] = (qkv + bias_ref[...]).astype(LOW)
    block = rows // 2
    segments = segment_rows(seg_ref)
    same_seg = product_tn(segments, segments) > 0.5
    for head in range(width // HDIM):
        lanes = [slice(i * width + head * HDIM, i * width + (head + 1) * HDIM) for i in range(3)]
        key, value = qkv_ref[:, lanes[1]], qkv_ref[:, lanes[2]]
        for part in range(2):
            spot = slice(part * block, (part + 1) * block)
            query = qkv_ref[spot, lanes[0]] * jnp.asarray(HDIM ** (-0.5), LOW)
            scores = lax.dot_general(
                query, key, (((1,), (1,)), ((), ())), preferred_element_type=jnp.float32
            )
            scores = jnp.where(same_seg[spot, :], scores, MASK_FILL)
            exp_scores = jnp.exp(scores - jnp.max(scores, axis=-1, keepdims=True))
            probs = exp_scores * (1.0 / jnp.sum(exp_scores, axis=-1, keepdims=True))
            context_ref[spot, lanes[0]] = jnp.dot(
                probs.astype(LOW), value, preferred_element_type=jnp.float32
            ).astype(LOW)


def attention(tokens, weight, bias, segment_ids, others=()):
    rows = tokens.shape[0]
    width = bias.shape[1] // 3
    return call_after(
        attention_kernel,
        others,
        [pl.BlockSpec(memory_space=pltpu.VMEM)] * 4,
        out_shape=[
            jax.ShapeDtypeStruct((rows, 3 * width), LOW),
            jax.ShapeDtypeStruct((rows, width), LOW),
        ],
        compiler_params=pltpu.CompilerParams(vmem_limit_bytes=24 * 1024 * 1024),
        cost_estimate=pl.CostEstimate(
            flops=2 * rows * width * (3 * tokens.shape[1] + 2 * rows),
            bytes_accessed=2 * rows * tokens.shape[1] + 2 * weight.size,
            transcendentals=rows * rows * width // HDIM,
        ),
    )(tokens, weight, bias, segment_ids)


def attention_back_kernel(
    scale, queries_ref, first_ref, second_ref, grad_ref, seg_ref, pick_ref, turned_ref,
    beside_ref, first_grad_ref, first_term_ref, second_grad_ref, second_term_ref, sums_ref, dqueries_ref,
):
    segments = segment_rows(seg_ref)
    listed = product_nt(segments, pick_ref[...]).astype(LOW)
    same_seg = product_tn(listed, segments) > 0.5
    width = first_ref.shape[1] // 3
    sums_ref[...] = jnp.zeros_like(sums_ref)

    def dot(left, right, left_dim, right_dim):
        return lax.dot_general(
            left,
            right,
            (((left_dim,), (right_dim,)), ((), ())),
            preferred_element_type=jnp.float32,
        )

    halves = (
        (0, first_ref, first_grad_ref, first_term_ref),
        (1, second_ref, second_grad_ref, second_term_ref),
    )
    for half, qkv_ref, dqkv_ref, term_ref in halves:
        for head in range(width // HDIM):
            lanes = slice(half * width + head * HDIM, half * width + (head + 1) * HDIM)
            keys = slice(width + head * HDIM, width + (head + 1) * HDIM)
            values = slice(2 * width + head * HDIM, 2 * width + (head + 1) * HDIM)
            query, grad = queries_ref[:, lanes], grad_ref[:, lanes]
            key, value = qkv_ref[:, keys], qkv_ref[:, values]
            scores = jnp.where(same_seg, dot(query, key, 1, 1) * scale, MASK_FILL)
            exp_scores = jnp.exp(scores - jnp.max(scores, axis=-1, keepdims=True))
            probs = exp_scores / jnp.sum(exp_scores, axis=-1, keepdims=True)
            dprobs = dot(grad, value, 1, 1)
            dscores = probs * (dprobs - jnp.sum(probs * dprobs, axis=-1, keepdims=True))
            dscores = dscores.astype(LOW)
            dqueries_ref[:, lanes] = (dot(dscores, key, 1, 0) * scale).astype(LOW)
            dqkv_ref[:, keys] = (dot(dscores, query, 0, 0) * scale).astype(LOW)
            dqkv_ref[:, values] = dot(probs.astype(LOW), grad, 0, 0).astype(LOW)
        lanes = slice(half * width, (half + 1) * width)
        dqkv_ref[:, :width] = dot(pick_ref[...], dqueries_ref[:, lanes], 0, 0).astype(LOW)
        term_ref[:, : 3 * width] = product(turned_ref[...], dqkv_ref[...]).astype(LOW)
        term_ref[:, 3 * width :] = beside_ref[:, 2 * half * width : 2 * (half + 1) * width]
        sums_ref[0:1, lanes] = jnp.sum(
            dqueries_ref[:, lanes].astype(jnp.float32), axis=0, keepdims=True
        )
        sums_ref[1:2, lanes] = jnp.sum(
            dqkv_ref[:, 2 * width :].astype(jnp.float32), axis=0, keepdims=True
        )


def attention_back(queries, first, second, grad, segment_ids, pick, turned, beside, others):
    listed = queries.shape[0]
    rows, width = first.shape
    term = (turned.shape[0], width + beside.shape[1] // 2)
    return call_after(
        functools.partial(attention_back_kernel, HDIM ** (-0.5)),
        others,
        [pl.BlockSpec(memory_space=pltpu.VMEM)] * 8,
        out_shape=[
            jax.ShapeDtypeStruct((rows, width), LOW),
            jax.ShapeDtypeStruct(term, LOW),
            jax.ShapeDtypeStruct((rows, width), LOW),
            jax.ShapeDtypeStruct(term, LOW),
            jax.ShapeDtypeStruct((8, queries.shape[1]), jnp.float32),
        ],
        scratch_shapes=[pltpu.VMEM(queries.shape, LOW)],
        compiler_params=pltpu.CompilerParams(vmem_limit_bytes=32 * 1024 * 1024),
        cost_estimate=pl.CostEstimate(
            flops=20 * listed * rows * width // 3 + 4 * turned.size * width,
            bytes_accessed=20 * rows * width // 3,
            transcendentals=2 * listed * rows * width // (3 * HDIM),
        ),
    )(queries, first, second, grad, segment_ids, pick, turned, beside)


def turn_row(row):
    return jnp.transpose(jnp.broadcast_to(row, (128, row.shape[1])))[:, 0:1]


def turn_column(column):
    return jnp.transpose(jnp.broadcast_to(column, (column.shape[0], 128)))[0:1, :]


def core_rows(words_ref, core):
    half = words_ref.shape[0] // 2
    mine = words_ref[pl.ds(pl.multiple_of(core * half, 128), half), :]
    other = words_ref[pl.ds(pl.multiple_of((1 - core) * half, 128), half), :]
    return mine, other


def logits_kernel(vocab_size, place_ref, mine_ref, other_ref, words_ref, bias_ref, logits_ref, log_ref):
    words_mine, words_other = core_rows(words_ref, place_ref[0])
    logits = product(mine_ref[...], words_mine) + product(other_ref[...], words_other) + bias_ref[...]
    ids = lax.broadcasted_iota(jnp.int32, logits.shape, 1) + place_ref[1]
    logits = jnp.where(ids < vocab_size, logits, MASK_FILL)
    logits_ref[...] = logits
    peak = jnp.max(logits, axis=1, keepdims=True)
    log_ref[...] = turn_column(
        peak + jnp.log(jnp.sum(jnp.exp(logits - peak), axis=1, keepdims=True))
    )


def dlogits_kernel(
    inv_count, place_ref, logits_ref, log_ref, labels_ref, words_ref, dlogits_ref, mine_ref, other_ref, sums_ref
):
    @pl.when(pl.program_id(0) == 0)
    def _():
        sums_ref[...] = jnp.zeros_like(sums_ref)

    logits = logits_ref[...]
    ids = lax.broadcasted_iota(jnp.int32, logits.shape, 1) + place_ref[1]
    is_label = ids.astype(jnp.float32) == turn_row(labels_ref[...])
    grads = jnp.exp(logits - turn_row(log_ref[...])) - jnp.where(is_label, 1.0, 0.0)
    grads = (grads * inv_count).astype(LOW)
    dlogits_ref[...] = grads
    words_mine, words_other = core_rows(words_ref, place_ref[0])
    other_ref[...] = product_nt(grads, words_other).astype(LOW)
    mine_ref[...] = product_nt(grads, words_mine).astype(LOW)
    sums_ref[0:1, :] += jnp.sum(grads.astype(jnp.float32), axis=0, keepdims=True)
    sums_ref[1:2, :] += jnp.sum(jnp.where(is_label, logits, 0.0), axis=0, keepdims=True)


def words_grad_kernel(place_ref, mine_ref, other_ref, dlogits_ref, grad_ref):
    half = mine_ref.shape[1]
    core = place_ref[0]
    grads = dlogits_ref[...]
    for spot, rows_ref in ((core, mine_ref), (1 - core, other_ref)):
        lanes = pl.ds(pl.multiple_of(spot * half, 128), half)
        grad_ref[lanes, :] = product_tn(rows_ref[...], grads).astype(LOW)


def row_blocks(slots):
    rows = min(256, slots)
    return (
        slots // rows,
        lambda width: pl.BlockSpec((rows, width), lambda step: (step, 0)),
        pl.BlockSpec((1, rows), lambda step: (0, step)),
    )


def whole_block(*shape):
    return pl.BlockSpec(shape, lambda step: (0,) * len(shape))


def part_logits(place, mine, other, words, bias, vocab_size):
    slots, half = mine.shape
    width = words.shape[1]
    steps, rows_of, line = row_blocks(slots)
    return pl.pallas_call(
        functools.partial(logits_kernel, vocab_size),
        grid=(steps,),
        in_specs=[
            pl.BlockSpec(memory_space=pltpu.SMEM),
            rows_of(half),
            rows_of(half),
            whole_block(2 * half, width),
            whole_block(1, width),
        ],
        out_specs=[rows_of(width), line],
        out_shape=[
            jax.ShapeDtypeStruct((slots, width), jnp.float32),
            jax.ShapeDtypeStruct((1, slots), jnp.float32),
        ],
        compiler_params=pltpu.CompilerParams(vmem_limit_bytes=24 * 1024 * 1024),
        cost_estimate=pl.CostEstimate(
            flops=4 * slots * half * width,
            bytes_accessed=4 * slots * width + 4 * half * (slots + width),
            transcendentals=slots * width,
        ),
    )(place, mine, other, words, bias)


def part_dlogits(place, logits, log_total, labels, words, inv_count):
    slots, width = logits.shape
    half = words.shape[0] // 2
    steps, rows_of, line = row_blocks(slots)
    return pl.pallas_call(
        functools.partial(dlogits_kernel, inv_count),
        grid=(steps,),
        in_specs=[
            pl.BlockSpec(memory_space=pltpu.SMEM),
            rows_of(width),
            line,
            line,
            whole_block(2 * half, width),
        ],
        out_specs=[rows_of(width), rows_of(half), rows_of(half), whole_block(8, width)],
        out_shape=[
            jax.ShapeDtypeStruct((slots, width), LOW),
            jax.ShapeDtypeStruct((slots, half), LOW),
            jax.ShapeDtypeStruct((slots, half), LOW),
            jax.ShapeDtypeStruct((8, width), jnp.float32),
        ],
        compiler_params=pltpu.CompilerParams(vmem_limit_bytes=24 * 1024 * 1024),
        cost_estimate=pl.CostEstimate(
            flops=4 * slots * half * width,
            bytes_accessed=6 * slots * width + 4 * half * (slots + width),
            transcendentals=slots * width,
        ),
    )(place, logits, log_total, labels, words)


def part_words_grad(place, mine, other, dlogits):
    slots, half = mine.shape
    width = dlogits.shape[1]
    return pl.pallas_call(
        words_grad_kernel,
        in_specs=[pl.BlockSpec(memory_space=pltpu.SMEM)] + [pl.BlockSpec(memory_space=pltpu.VMEM)] * 3,
        out_shape=jax.ShapeDtypeStruct((2 * half, width), LOW),
        compiler_params=pltpu.CompilerParams(vmem_limit_bytes=32 * 1024 * 1024),
        cost_estimate=pl.CostEstimate(
            flops=4 * slots * half * width,
            bytes_accessed=2 * slots * width + 4 * half * (slots + width),
            transcendentals=0,
        ),
    )(place, mine, other, dlogits)


def heads_of(rows):
    return rows.reshape(rows.shape[0], rows.shape[1] // HDIM, HDIM)


def attention_probs(queries, key_rows, query_seg, key_seg):
    scores = jnp.einsum(
        "qhd,khd->hqk", queries, key_rows, preferred_element_type=jnp.float32
    ) * HDIM ** (-0.5)
    same_seg = query_seg[:, None] == key_seg[None, :]
    masked = jnp.where(same_seg[None], scores, MASK_FILL)
    row_peak = jnp.max(masked, axis=-1, keepdims=True)
    exp_scores = jnp.exp(masked - row_peak)
    return exp_scores / jnp.sum(exp_scores, axis=-1, keepdims=True)


def per_device(
    tokens,
    segment_ids,
    mlm_labels,
    mask_order,
    mask_count,
    qkv_weight,
    query_bias,
    value_bias,
    out_weight,
    out_bias,
    attn_gain,
    attn_shift,
    up_weight,
    up_bias,
    down_weight,
    down_bias,
    ffn_gain,
    ffn_shift,
    head_weight,
    head_bias,
    head_gain,
    head_shift,
    decoder,
    decoder_bias,
):
    model_width = tokens.shape[1]
    tok_rows = tokens.shape[0]
    vocab_size = decoder.shape[1]
    bal_size = lax.axis_size("bal")
    dp_size = lax.axis_size("dp")
    bal_place = lax.axis_index("bal")
    dp_place = lax.axis_index("dp")
    grid = Grid(dp_size, bal_size)
    device_count = dp_size * bal_size
    my_place = dp_place * bal_size + bal_place
    slot_count = HEAD_DEV * device_count
    inv_count = 1.0 / slot_count
    part_vocab = -(-(-(-vocab_size // device_count)) // 128) * 128

    listed = mask_order[0, :MASK_DEV]
    pick_mat = listed[:, None] == jnp.arange(tok_rows)[None, :]
    pick_low = pick_mat.astype(LOW)

    def pick(rows):
        return product(pick_low, rows).astype(LOW)

    listed_ids = jnp.sum(jnp.where(pick_mat, mlm_labels[None, :], 0), axis=1)

    shard_rows = qkv_weight.shape[0]
    my_units = down_weight.shape[0]
    units = my_units * device_count
    ratio = my_units // shard_rows
    half = model_width // 2

    def unit_order(rows):
        split = rows.reshape(rows.shape[0], device_count, ratio, shard_rows)
        return split.transpose(0, 2, 1, 3).reshape(rows.shape[0], units)

    down_wide = down_weight.reshape(ratio, shard_rows, model_width).transpose(1, 0, 2)
    down_wide = down_wide.reshape(shard_rows, ratio * model_width)
    packed = lax.all_gather(
        jnp.concatenate([unit_order(up_weight), down_wide], axis=1), AXES, axis=0, tiled=True
    )
    up_offsets = unit_order(up_bias[None])[0]
    my_offsets = lax.dynamic_slice_in_dim(up_bias, my_place * my_units, my_units)

    def by_heads(rows):
        split = rows.reshape(rows.shape[0], 3, 2, half)
        return grid.halves(
            split[:, :, 0].reshape(rows.shape[0], 3 * half),
            split[:, :, 1].reshape(rows.shape[0], 3 * half),
        )

    info = jnp.concatenate([listed_ids, mask_count, jnp.zeros((63,), jnp.int32)])
    info = grid.gather_group(info[None])
    weights_run = Transfer(by_heads(qkv_weight), grid.gather_steps(shard_rows))
    both_run = Transfer(grid.halves(out_weight, head_weight), grid.gather_steps(shard_rows))
    qkv_width = 3 * half
    weights_run.step()
    weights_run.step()
    weights_run.step()
    all_mine, all_other = weights_run.finish()
    both_run.step()

    info = jnp.concatenate(info)
    group = jnp.stack(grid.group())
    counts = info[:, MASK_DEV]
    before = group[None, :] < group[:, None]
    starts = jnp.sum(jnp.where(before, counts[None, :], 0), axis=1)
    steps = jnp.arange(MASK_DEV)
    slot_of = jnp.where(steps[None] < counts[:, None], starts[:, None] + steps[None], -1)
    my_slots = bal_place * HEAD_DEV + jnp.arange(HEAD_DEV)
    is_mine = slot_of[None] == my_slots[:, None, None]
    my_labels = jnp.sum(jnp.where(is_mine, info[None, :, :MASK_DEV], 0), axis=(1, 2))
    to_head = is_mine.astype(LOW)
    group_slots = group[:, None] * HEAD_DEV + jnp.arange(HEAD_DEV)[None, :]
    from_head = (slot_of[0][:, None, None] == group_slots[None]).astype(LOW)

    def choose(choice, parts):
        total = product(choice[:, 0], parts[0])
        for index, part in enumerate(parts[1:], 1):
            total = total + product(choice[:, index], part)
        return total.astype(LOW)

    tokens_s = pick(tokens)

    bias_mine, bias_other = by_heads(
        jnp.concatenate([query_bias, jnp.zeros_like(query_bias), value_bias])[None]
    )
    parts_mine, context_mine = attention(
        tokens, all_mine, bias_mine, segment_ids, []
    )
    padded = lax.pad(
        decoder,
        nothing(context_mine).astype(LOW),
        ((0, 0, 0), (0, part_vocab * device_count - vocab_size, 0)),
    )
    padded = padded.reshape(decoder.shape[0], device_count, part_vocab).transpose(1, 0, 2)
    parts_other, context_other = attention(tokens, all_other, bias_other, segment_ids, [context_mine])
    both_run.step(context_mine)
    both_run.step()
    both_run.step(context_other)
    out_full, head_full = grid.halves(*both_run.finish())
    context = jnp.concatenate(grid.halves(context_mine, context_other), axis=1)
    words = lax.all_to_all(padded, AXES, split_axis=0, concat_axis=0, tiled=True)

    picked = [tokens_s, *grid.halves(pick(context_mine), pick(context_other))]
    group_rows = grid.gather_group(jnp.concatenate(picked, axis=1))
    listed_queries = jnp.concatenate(
        [pick(parts_mine[:, :half]), pick(parts_other[:, :half])], axis=1
    )
    slot_rows = choose(to_head, group_rows)
    tokens_own, context_own = slot_rows[:, :model_width], slot_rows[:, model_width:]
    vectors = jnp.stack(
        [out_bias, attn_gain, attn_shift, down_bias, ffn_gain, ffn_shift, out_bias, out_bias]
    )
    window = min(256, model_width)
    begin = jnp.minimum(my_place * shard_rows // 128 * 128, model_width - window)
    lanes = jnp.arange(window)[:, None] + begin - my_place * shard_rows
    unit_ids = np.arange(my_units)
    my_columns = jnp.zeros((model_width, my_units), jnp.float32)
    for block in range(ratio):
        piece = lax.dynamic_slice_in_dim(packed, block * model_width + begin, window, 1)
        wanted = np.where(unit_ids // shard_rows == block, unit_ids % shard_rows, -model_width)
        is_unit = lanes == jnp.asarray(wanted, jnp.int32)[None, :]
        my_columns = my_columns + product(piece, is_unit.astype(LOW))
    my_columns = my_columns.astype(LOW)


    def layer_part(part, others, room, into=None):
        return feed_forward(
            context, tokens, out_full, vectors, packed, up_offsets, others, room, part, 2, into
        )[0]

    head_in, normed_own, resid_one, resid_two = feed_forward(
        context_own, tokens_own, out_full, vectors, packed, up_offsets, [listed_queries], 24
    )

    rows_all = lax.all_gather(normed_own, AXES, axis=0, tiled=True)
    up_all = product(rows_all, my_columns) + my_offsets

    inner_rows = product(head_in, head_full) + head_bias
    head_act, act_back = jax.vjp(gelu_exact, inner_rows)
    head_normal, head_inv = norm_parts(head_act)
    head_normed = (head_normal * head_gain + head_shift).astype(LOW)
    head_run = Transfer(
        grid.halves(head_normed[:, :half], head_normed[:, half:]), grid.gather_steps(HEAD_DEV)
    )
    head_run.step(lax.dynamic_slice(words, (nothing(head_in), 0, 0), (1, 1, 1)))
    head_run.step()
    head_run.step()
    head_run.step()
    normed_mine, normed_other = head_run.finish()
    words = words.reshape(model_width, part_vocab)
    padded_bias = jnp.pad(decoder_bias, (0, part_vocab * device_count - vocab_size))
    words_bias = lax.dynamic_slice_in_dim(padded_bias, my_place * part_vocab, part_vocab)
    place = jnp.stack([grid.place[3], my_place * part_vocab]).astype(jnp.int32)
    logits, part_log = part_logits(
        place, normed_mine, normed_other, words, words_bias[None], vocab_size
    )
    spread = jnp.concatenate(
        [part_log[0], my_labels.astype(jnp.float32), jnp.zeros((128 - HEAD_DEV,), jnp.float32)]
    )
    spread = jnp.broadcast_to(spread[None, None], (device_count, 1, slot_count + 128))
    spread = lax.all_to_all(spread, AXES, split_axis=0, concat_axis=0, tiled=True)
    spread = spread[:, 0]
    all_logs = spread[:, :slot_count]
    labels = spread[:, slot_count : slot_count + HEAD_DEV].reshape(1, slot_count)
    peak = jnp.max(all_logs, axis=0)
    log_total = peak + jnp.log(jnp.sum(jnp.exp(all_logs - peak), axis=0))
    dlogits, dhead_mine, dhead_other, logit_sums = part_dlogits(
        place, logits, log_total[None], labels, words, inv_count
    )
    head_run = Transfer((dhead_mine, dhead_other), grid.scatter_steps(HEAD_DEV))
    words_grad = part_words_grad(place, normed_mine, normed_other, dlogits)
    head_run.step()
    head_run.step()
    head_run.step()
    head_run.step()
    words_bias_grad = logit_sums[0]
    target_part = jnp.sum(logit_sums[1])
    loss_part = jnp.where(my_place == 0, jnp.sum(log_total), 0.0) - target_part
    dhead_normed = jnp.concatenate(grid.halves(*head_run.finish()), axis=1).astype(jnp.float32)
    dhead_act, head_gain_part, head_shift_part = norm_back(
        head_normal, head_inv, head_gain, dhead_normed
    )
    dinner = act_back(dhead_act)[0].astype(LOW)
    head_bias_part = jnp.sum(dinner, axis=0, dtype=jnp.float32)
    dhead_in = product_nt(dinner, head_full).astype(LOW)

    words_back = lax.all_to_all(
        words_grad.reshape(device_count, decoder.shape[0], part_vocab),
        AXES,
        split_axis=0,
        concat_axis=0,
        tiled=True,
    )

    loss_high = loss_part.astype(LOW).astype(jnp.float32)
    vocab_rows = jnp.pad(words_bias_grad, (0, 2 * model_width - part_vocab))
    more = jnp.stack(
        [
            head_bias_part,
            head_gain_part,
            head_shift_part,
            jnp.where(jnp.arange(model_width) < half, loss_high, loss_part - loss_high),
            vocab_rows[:model_width],
            vocab_rows[model_width:],
            head_bias_part,
            head_bias_part,
        ]
    )
    send, dresid_own = feed_back(
        dhead_in, resid_one, resid_two, normed_own, vectors, more, packed, up_offsets, [up_all, words_grad]
    )
    group_grads = grid.gather_group(dresid_own)
    factors = lax.all_gather(send, AXES, axis=0, tiled=True)

    def two_parts(rows):
        high = rows.astype(LOW)
        return jnp.concatenate([high, (rows - high.astype(jnp.float32)).astype(LOW)])

    out_term = product_tn(context_own, dresid_own).astype(LOW)
    head_term = product_tn(head_in, dinner).astype(LOW)
    beside = jnp.concatenate(grid.halves(out_term, head_term), axis=1)
    dresid_one = choose(from_head, group_grads)
    dcontext = product_nt(dresid_one, out_full).astype(LOW)
    dcontext = jnp.concatenate(grid.halves(dcontext[:, :half], dcontext[:, half:]), axis=1)
    dqkv_mine, mine_term, dqkv_other, other_term, qkv_sums = attention_back(
        listed_queries,
        parts_mine,
        parts_other,
        dcontext,
        segment_ids,
        pick_low,
        tokens.T,
        beside,
        [],
    )
    other_taken = grid.shift(other_term, (3, 3), 1)
    weights_run = Transfer((mine_term, None), grid.scatter_steps(shard_rows, other_taken))
    weights_run.step(words_back)
    first_part = layer_part(0, [grid.sent], 24)
    weights_run.step(first_part)
    second_part = layer_part(1, [grid.sent], 24, first_part)
    qkv_sums = grid.halves(qkv_sums[:2, :half], qkv_sums[:2, half:])
    qkv_sums = two_parts(jnp.concatenate(qkv_sums, axis=1))

    ddown_all = factors[:, :model_width]
    hidden, act_back = jax.vjp(gelu_exact, up_all)
    dup_all = act_back(product_nt(ddown_all, down_weight))[0].astype(LOW)
    up_term = product_tn(rows_all, dup_all).astype(LOW).reshape(device_count, shard_rows, my_units)
    weights_run.step(second_part)
    words_back = once(words_back, grid.sent)
    qkv_sums = qkv_sums.reshape(-1, my_units)
    qkv_sums = jnp.broadcast_to(qkv_sums[None], (device_count, *qkv_sums.shape))
    up_back = lax.all_to_all(
        jnp.concatenate([up_term, qkv_sums], axis=1), AXES, split_axis=0, concat_axis=0, tiled=True
    )
    down_grad = product_tn(hidden.astype(LOW), ddown_all)
    up_grad = up_back[:, :shard_rows].transpose(1, 0, 2).reshape(shard_rows, units)
    up_grad = up_grad.astype(jnp.float32)
    qkv_sums = jnp.sum(up_back[:, shard_rows:].astype(jnp.float32), axis=0)
    qkv_sums = jnp.sum(qkv_sums.reshape(2, 2, model_width), axis=0)

    tokens_grad = product_tn(pick_low, once(dresid_one, weights_run.part[0][-1]))
    tokens_grad = tokens_grad + product_nt(dqkv_other, all_other)
    tokens_grad = tokens_grad + product_nt(dqkv_mine, all_mine)
    weights_run.step()
    mine, other = weights_run.finish()
    sums = factors[:, model_width:].astype(jnp.float32).reshape(device_count, 2, 16, half)
    sums = jnp.concatenate([sums[:, 0], sums[:, 1]], axis=2)
    decoder_bias_grad = sums[:, 4:6].reshape(device_count, 2 * model_width)[:, :part_vocab]
    decoder_bias_grad = decoder_bias_grad.reshape(-1)[:vocab_size]
    sums = jnp.sum(sums, axis=0)
    up_sums = sums[12:].reshape(ratio, device_count, shard_rows).transpose(1, 0, 2).reshape(-1)
    first, second = grid.halves(mine[:, :qkv_width], other[:, :qkv_width])
    qkv_grad = jnp.stack(
        [first.reshape(shard_rows, 3, half), second.reshape(shard_rows, 3, half)], axis=2
    )
    qkv_grad = qkv_grad.reshape(shard_rows, 3 * model_width).astype(jnp.float32)
    out_grad, head_grad = grid.halves(mine[:, qkv_width:], other[:, qkv_width:])
    decoder_grad = words_back.transpose(1, 0, 2).reshape(decoder.shape[0], -1)
    decoder_grad = decoder_grad[:, :vocab_size].astype(jnp.float32)
    return (
        second_part,
        (sums[3, 0] + sums[3, half]) * inv_count,
        tokens_grad,
        qkv_grad,
        qkv_sums[0],
        qkv_sums[1],
        out_grad.astype(jnp.float32),
        sums[11],
        sums[9],
        sums[10],
        up_grad,
        up_sums,
        down_grad,
        sums[8],
        sums[6],
        sums[7],
        head_grad.astype(jnp.float32),
        sums[0],
        sums[1],
        sums[2],
        decoder_grad,
        decoder_bias_grad,
    )


def solution(mesh):
    cut, rows = P(("dp", "bal"), None), P(("dp", "bal"))
    whole = P()
    return jax.shard_map(
        per_device,
        mesh=mesh,
        in_specs=(
            cut, cut, rows, cut, rows, cut, whole, whole, cut, whole, whole, whole,
            cut, whole, cut, whole, whole, whole, cut, whole, whole, whole, cut, whole,
        ),
        out_specs=(
            cut, whole, cut, cut, whole, whole, cut, whole, whole, whole, cut,
            whole, cut, whole, whole, whole, cut, whole, whole, whole, cut, whole,
        ),
        check_vma=False,
    )
```

```python
import functools

import jax
import jax.numpy as jnp
import numpy as np
from jax import lax
from jax.experimental import pallas as pl
from jax.experimental.pallas import tpu as pltpu
from jax.sharding import PartitionSpec as P

HDIM = 64
HEAD_DEV = 32
MASK_DEV = 64


EPSILON = 1e-06
MASK_FILL = -1e30
AXES = ("dp", "bal")
LOW = jnp.bfloat16


def gelu_exact(values):
    return jax.nn.gelu(values, approximate=False)


def product(left_mat, right_mat):
    return jnp.dot(left_mat, right_mat, preferred_element_type=jnp.float32)


def product_tn(left_mat, right_mat):
    return lax.dot_general(
        left_mat, right_mat, (((0,), (0,)), ((), ())), preferred_element_type=jnp.float32
    )


def product_nt(left_mat, right_mat):
    return lax.dot_general(
        left_mat, right_mat, (((1,), (1,)), ((), ())), preferred_element_type=jnp.float32
    )


def norm_parts(hidden):
    average = jnp.mean(hidden, axis=-1, keepdims=True)
    centered = hidden - average
    inv_std = lax.rsqrt(jnp.mean(centered * centered, axis=-1, keepdims=True) + EPSILON)
    return centered * inv_std, inv_std


def norm_back(normal, inv_std, gain_vec, grad):
    scaled = grad * gain_vec
    first = jnp.mean(scaled, axis=-1, keepdims=True)
    second = jnp.mean(scaled * normal, axis=-1, keepdims=True)
    return (
        inv_std * (scaled - first - normal * second),
        jnp.sum(grad * normal, axis=0),
        jnp.sum(grad, axis=0),
    )


class Grid:
    def __init__(self, dp_size, bal_size):
        self.high = 4 if dp_size % 4 == 0 else 1
        self.low = dp_size // self.high
        self.wide = bal_size // 2
        self.sizes = (self.high, self.low, self.wide, 2)
        self.count = dp_size * bal_size
        dp_place, bal_place = lax.axis_index("dp"), lax.axis_index("bal")
        self.place = (
            dp_place // self.low,
            dp_place % self.low,
            bal_place // 2,
            bal_place % 2,
        )
        self.crossed = self.low == self.wide

    def index(self, spot):
        high, low, wide, core = spot
        return ((high * self.low + low) * self.wide + wide) * 2 + core

    def spots(self):
        for high in range(self.high):
            for low in range(self.low):
                for wide in range(self.wide):
                    for core in range(2):
                        yield (high, low, wide, core)

    def shift(self, value, axis_of, step):
        pairs = []
        for spot in self.spots():
            axis = axis_of[spot[3]]
            target = list(spot)
            target[axis] = (spot[axis] + step) % self.sizes[axis]
            pairs.append((self.index(spot), self.index(target)))
        self.sent = value
        return lax.ppermute(value, AXES, pairs)

    def own(self, axis_of):
        first, second = self.place[axis_of[0]], self.place[axis_of[1]]
        return first if axis_of[0] == axis_of[1] else jnp.where(self.place[3] == 0, first, second)

    def orders(self):
        return ((1, 2), (2, 1)) if self.crossed else ((1, 1), (2, 2))

    def gather_stage(self, value, axis_of):
        size = self.sizes[axis_of[0]]
        me = self.own(axis_of)
        parts = [value] + [self.shift(value, axis_of, step) for step in range(1, size)]

        def join(hold):
            rel = (me + hold - jnp.arange(size)) % size
            rel = rel.reshape((size,) + (1,) * value.ndim)
            out = parts[-1][None]
            for step in range(size - 2, -1, -1):
                out = jnp.where(rel == step, parts[step][None], out)
            return out

        return join

    def halves(self, first, second, hold=0):
        is_first = self.place[3] + hold == 0
        return lax.select(is_first, first, second), lax.select(is_first, second, first)

    def gather_steps(self, height):
        core = self.place[3]
        first, second = self.orders()

        def start(pair):
            keep, give = pair
            taken = self.shift(give, (3, 3), 1)

            def join(hold):
                is_own = (jnp.arange(2) == core + hold)[:, None, None]
                return jnp.where(is_own, keep[None], taken[None])

            return join

        def third(part):
            other = self.gather_stage(part, second)

            def straight(hold):
                joined = other(hold)
                out = joined.transpose(2, 1, 0, 3, 4, 5)
                if self.crossed:
                    turned = joined.transpose(2, 0, 1, 3, 4, 5)
                    out = lax.select(core == 0, out, turned)
                out = lax.optimization_barrier(out)
                return out.reshape(self.count * height, part.shape[-1])

            return straight

        def last(mine):
            other = self.shift(mine, (3, 3), 1)
            return lambda hold: (mine, other)

        return [
            start,
            lambda part: self.gather_stage(part, (0, 0)),
            lambda part: self.gather_stage(part, first),
            third,
            last,
        ]

    def scatter_steps(self, height, taken=None):
        core = self.place[3]
        first, second = self.orders()

        def total(pieces, hold=0):
            out = jnp.asarray(hold).astype(jnp.float32)
            for piece in pieces:
                out = out + piece.astype(jnp.float32)
            return out.astype(LOW)

        def start(pair):
            keep, give = pair
            came = self.shift(give, (3, 3), 1) if taken is None else taken
            shape = (self.high, self.low, self.wide, 2, height, keep.shape[1])
            return lambda hold: ([keep.reshape(shape), came.reshape(shape)], hold)

        def stage(axis_of, piece, hold):
            size = self.sizes[axis_of[0]]
            moved = [self.shift(total(piece(step), hold), axis_of, step) for step in range(1, size)]
            return lambda hold: (piece(0) + moved, hold)

        def cut(given, axis_of, axis):
            parts, hold = given
            size, me = self.sizes[axis_of[0]], self.own(axis_of)

            def piece(step):
                spot = (me + step) % size
                return [lax.dynamic_index_in_dim(part, spot, axis, keepdims=False) for part in parts]

            return stage(axis_of, piece, hold)

        def one(given):
            parts, hold = given
            if not self.crossed:
                return cut(given, second, 2)
            size, me = self.wide, self.own(second)
            flat = [part.reshape(self.high, size * size, *part.shape[3:]) for part in parts]

            def piece(step, along):
                spot = (me + step) % size
                spot = jnp.where(core == 0, along * size + spot, spot * size + along)
                return [lax.dynamic_index_in_dim(part, spot, 1, keepdims=False) for part in flat]

            moved = [
                [self.shift(total(piece(step, along), hold), second, step) for step in range(1, size)]
                for along in range(size)
            ]
            return lambda hold: ([piece(0, along) + moved[along] for along in range(size)], hold)

        def two(given):
            if not self.crossed:
                return cut(given, first, 1)
            columns, hold = given
            size, me = self.low, self.own(first)

            def piece(step):
                spot = (me + step) % size
                out = columns[-1]
                for along in range(size - 2, -1, -1):
                    out = [lax.select(spot == along, *pair) for pair in zip(columns[along], out)]
                return out

            return stage(first, piece, hold)

        def last(given):
            parts, hold = given
            mine = total([lax.dynamic_index_in_dim(part, core, 0, keepdims=False) for part in parts])
            away = total(
                [lax.dynamic_index_in_dim(part, 1 - core, 0, keepdims=False) for part in parts], hold
            )
            other = self.shift(away, (3, 3), 1)
            return lambda hold: (mine, other)

        return [
            start,
            one,
            two,
            lambda given: cut(given, (0, 0), 0),
            last,
        ]

    def group(self):
        return [
            (self.place[2] - wide) % self.wide * 2 + (self.place[3] - core) % 2
            for wide in range(self.wide)
            for core in range(2)
        ]

    def gather_group(self, rows):
        parts = []
        for wide in range(self.wide):
            for core in range(2):
                if wide == 0 and core == 0:
                    parts.append(rows)
                    continue
                pairs = []
                for spot in self.spots():
                    target = (spot[0], spot[1], (spot[2] + wide) % self.wide, (spot[3] + core) % 2)
                    pairs.append((self.index(spot), self.index(target)))
                parts.append(lax.ppermute(rows, AXES, pairs))
        return parts


class Transfer:
    def __init__(self, part, steps):
        self.part = part
        self.steps = list(steps)
        self.join = self.steps.pop(0)(part)

    def step(self, *others):
        self.part = self.join(sum((nothing(other) for other in others), 0))
        self.join = self.steps.pop(0)(self.part)

    def finish(self, *others):
        while self.steps:
            self.step(*others)
            others = ()
        self.part = self.join(sum((nothing(other) for other in others), 0))
        return self.part


def nothing(value):
    hold = 0
    for piece in jax.tree.leaves(value):
        if piece.ndim:
            spot = piece[(0,) * piece.ndim]
            is_float = jnp.issubdtype(spot.dtype, jnp.floating)
            hold = hold + (spot != spot if is_float else spot < -1).astype(jnp.int32)
    return hold


def once(value, *others):
    for other in others:
        value = value + nothing(other).astype(value.dtype)
    return value


def erf_fast(value):
    value = jnp.clip(value, -3.832506856900711, 3.832506856900711)
    square = value * value
    top = jnp.float32(0.00022905065861350646)
    for number in (0.0034082910107109506, 0.050955695062380861, 0.18520832239976145, 1.128379143519084):
        top = top * square + number
    low = jnp.float32(-1.1791602954361697e-7)
    for number in (
        0.000023547966471313185,
        0.0010179625278914885,
        0.014070470171167667,
        0.11098505178285362,
        0.49746925110067538,
        1.0,
    ):
        low = low * square + number
    return value * top / low


def gelu_fast(value):
    return 0.5 * value * (1.0 + erf_fast(value * 0.7071067811865476))


def gelu_slope(value):
    bell = jnp.exp(value * value * -0.5) * 0.3989422804014327
    return 0.5 * (1.0 + erf_fast(value * 0.7071067811865476)) + value * bell


def call_after(kernel, others, in_specs, **settings):
    others = jax.tree.leaves(others)

    def run(*refs):
        kernel(*refs[len(others) :])

    call = pl.pallas_call(
        run, in_specs=[pl.BlockSpec(memory_space=pl.ANY)] * len(others) + in_specs, **settings
    )
    return lambda *operands: call(*others, *operands)


def load_weights(packed_ref, weights_ref, sems):
    count, _, width = weights_ref.shape
    copies = []
    order = [part * (count // 2) + block for block in range(count // 2) for part in range(2)]
    for block in order:
        source = packed_ref.at[:, block * width : (block + 1) * width]
        copies.append((block, pltpu.make_async_copy(source, weights_ref.at[block], sems.at[block])))
        copies[-1][1].start()
    return dict(copies)


def feed_forward_kernel(
    spot_out,
    context_ref,
    tokens_ref,
    out_ref,
    vectors_ref,
    up_bias_ref,
    packed_ref,
    layer_ref,
    normed_ref,
    one_ref,
    total_ref,
):
    width = tokens_ref.shape[1]
    blocks = packed_ref.shape[1] // (2 * width)
    resid = tokens_ref[spot_out, :].astype(jnp.float32)
    resid = resid + product(context_ref[spot_out, :], out_ref[...])
    resid = resid + vectors_ref[0:1, :]
    one_ref[...] = resid
    normed = norm_parts(resid)[0] * vectors_ref[1:2, :] + vectors_ref[2:3, :]
    normed = normed.astype(LOW)
    normed_ref[...] = normed
    total_ref[...] = normed.astype(jnp.float32) + vectors_ref[3:4, :]
    rows = total_ref.shape[0]
    parts = max(1, rows // 128)
    for block in range(blocks):
        lanes = slice(block * width, (block + 1) * width)
        down_lanes = slice((blocks + block) * width, (blocks + block + 1) * width)
        bias = up_bias_ref[:, lanes]
        for part in range(parts):
            spot = slice(part * (rows // parts), (part + 1) * (rows // parts))
            up = product(normed_ref[spot, :], packed_ref[:, lanes])
            hidden = gelu_fast(up + bias).astype(LOW)
            total_ref[spot, :] += product(hidden, packed_ref[:, down_lanes])
    layer = norm_parts(total_ref[...])[0] * vectors_ref[4:5, :] + vectors_ref[5:6, :]
    layer_ref[spot_out, :] = layer.astype(LOW)


def square_scratch(packed, width):
    count = packed.shape[1] // width
    return [pltpu.VMEM((count, width, width), LOW), pltpu.SemaphoreType.DMA((count,))]


def feed_forward_more_kernel(spot, into_ref, *refs):
    layer_ref = refs[6]
    layer_ref[: spot.start, :] = into_ref[: spot.start, :]
    feed_forward_kernel(spot, *refs)


def feed_forward(context, tokens, out_full, vectors, packed, up_bias, others, room, part=0, parts=1, into=None):
    rows, width = tokens.shape[0] // parts, tokens.shape[1]
    units = packed.shape[1] // 2
    spot = slice(part * rows, (part + 1) * rows)
    more = () if into is None else (into,)
    kernel = functools.partial(feed_forward_kernel, spot)
    if more:
        kernel = functools.partial(feed_forward_more_kernel, spot)
    others = jax.tree.leaves(others)
    return call_after(
        kernel,
        others,
        [pl.BlockSpec(memory_space=pltpu.VMEM)] * (6 + len(more)),
        out_shape=[
            jax.ShapeDtypeStruct((parts * rows, width), LOW),
            jax.ShapeDtypeStruct((rows, width), LOW),
            jax.ShapeDtypeStruct((rows, width), jnp.float32),
            jax.ShapeDtypeStruct((rows, width), jnp.float32),
        ],
        compiler_params=pltpu.CompilerParams(vmem_limit_bytes=room * 1024 * 1024),
        cost_estimate=pl.CostEstimate(
            flops=4 * rows * width * units,
            bytes_accessed=4 * width * units,
            transcendentals=rows * units,
        ),
    )(*more, context, tokens, out_full, vectors, up_bias[None, :], packed)


def feed_back_kernel(
    grad_ref,
    one_ref,
    two_ref,
    normed_ref,
    vectors_ref,
    more_ref,
    up_bias_ref,
    packed_ref,
    send_ref,
    done_ref,
    total_ref,
    sums_ref,
    weights_ref,
    sems,
):
    copies = load_weights(packed_ref, weights_ref, sems)
    blocks = len(copies) // 2
    width = normed_ref.shape[1]
    sums_ref[...] = jnp.zeros_like(sums_ref)
    sums_ref[0:6, :] = more_ref[0:6, :]

    def norm_grad(resid, gain, grad, row):
        normal, inv_std = norm_parts(resid)
        dresid, gain_part, shift_part = norm_back(normal, inv_std, gain, grad)
        sums_ref[row : row + 1, :] = gain_part[None]
        sums_ref[row + 1 : row + 2, :] = shift_part[None]
        sums_ref[row + 2 : row + 3, :] = jnp.sum(
            dresid.astype(LOW).astype(jnp.float32), axis=0, keepdims=True
        )
        return dresid

    dtwo = norm_grad(two_ref[...], vectors_ref[4:5, :], grad_ref[...].astype(jnp.float32), 6)
    total_ref[...] = dtwo
    ddown = dtwo.astype(LOW)
    send_ref[:, :width] = ddown
    for block in range(blocks):
        copies[block].wait()
        copies[blocks + block].wait()
        spot = slice(block * width, (block + 1) * width)
        up = product(normed_ref[...], weights_ref[block]) + up_bias_ref[:, spot]
        dup = (gelu_slope(up) * product_nt(ddown, weights_ref[blocks + block])).astype(LOW)
        sums_ref[12 + block : 13 + block, :] = jnp.sum(
            dup.astype(jnp.float32), axis=0, keepdims=True
        )
        total_ref[...] += product_nt(dup, weights_ref[block])
    done_ref[...] = norm_grad(one_ref[...], vectors_ref[1:2, :], total_ref[...], 9).astype(LOW)
    half = width // 2
    send_ref[:16, width:] = sums_ref[:, :half].astype(LOW)
    send_ref[16:, width:] = sums_ref[:, half:].astype(LOW)


def feed_back(grad, resid_one, resid_two, normed, vectors, more, packed, up_bias, others):
    rows, width = normed.shape
    units = packed.shape[1] // 2
    return call_after(
        feed_back_kernel,
        others,
        [pl.BlockSpec(memory_space=pltpu.VMEM)] * 7
        + [pl.BlockSpec(memory_space=pltpu.HBM)],
        out_shape=[
            jax.ShapeDtypeStruct((rows, width + width // 2), LOW),
            jax.ShapeDtypeStruct((rows, width), LOW),
        ],
        scratch_shapes=[
            pltpu.VMEM((rows, width), jnp.float32),
            pltpu.VMEM((16, width), jnp.float32),
        ]
        + square_scratch(packed, width),
        compiler_params=pltpu.CompilerParams(vmem_limit_bytes=24 * 1024 * 1024),
        cost_estimate=pl.CostEstimate(
            flops=6 * rows * width * units,
            bytes_accessed=4 * width * units,
            transcendentals=rows * units,
        ),
    )(grad, resid_one, resid_two, normed, vectors, more, up_bias[None, :], packed)


def segment_rows(seg_ref):
    rows = lax.broadcasted_iota(jnp.int32, (8, seg_ref.shape[1]), 0)
    return (rows == seg_ref[...]).astype(jnp.float32).astype(LOW)


def attention_kernel(tokens_ref, weight_ref, bias_ref, seg_ref, qkv_ref, context_ref):
    width = context_ref.shape[1]
    rows = tokens_ref.shape[0]
    qkv = product(tokens_ref[...], weight_ref[:, : 3 * width])
    qkv_ref[...] = (qkv + bias_ref[...]).astype(LOW)
    block = rows // 2
    segments = segment_rows(seg_ref)
    same_seg = product_tn(segments, segments) > 0.5
    for head in range(width // HDIM):
        lanes = [slice(i * width + head * HDIM, i * width + (head + 1) * HDIM) for i in range(3)]
        key, value = qkv_ref[:, lanes[1]], qkv_ref[:, lanes[2]]
        for part in range(2):
            spot = slice(part * block, (part + 1) * block)
            query = qkv_ref[spot, lanes[0]] * jnp.asarray(HDIM ** (-0.5), LOW)
            scores = lax.dot_general(
                query, key, (((1,), (1,)), ((), ())), preferred_element_type=jnp.float32
            )
            scores = jnp.where(same_seg[spot, :], scores, MASK_FILL)
            exp_scores = jnp.exp(scores - jnp.max(scores, axis=-1, keepdims=True))
            probs = exp_scores * (1.0 / jnp.sum(exp_scores, axis=-1, keepdims=True))
            context_ref[spot, lanes[0]] = jnp.dot(
                probs.astype(LOW), value, preferred_element_type=jnp.float32
            ).astype(LOW)


def attention(tokens, weight, bias, segment_ids, others=()):
    rows = tokens.shape[0]
    width = bias.shape[1] // 3
    return call_after(
        attention_kernel,
        others,
        [pl.BlockSpec(memory_space=pltpu.VMEM)] * 4,
        out_shape=[
            jax.ShapeDtypeStruct((rows, 3 * width), LOW),
            jax.ShapeDtypeStruct((rows, width), LOW),
        ],
        compiler_params=pltpu.CompilerParams(vmem_limit_bytes=24 * 1024 * 1024),
        cost_estimate=pl.CostEstimate(
            flops=2 * rows * width * (3 * tokens.shape[1] + 2 * rows),
            bytes_accessed=2 * rows * tokens.shape[1] + 2 * weight.size,
            transcendentals=rows * rows * width // HDIM,
        ),
    )(tokens, weight, bias, segment_ids)


def attention_back_kernel(
    scale, queries_ref, first_ref, second_ref, grad_ref, seg_ref, pick_ref, turned_ref,
    beside_ref, first_grad_ref, first_term_ref, second_grad_ref, second_term_ref, sums_ref, dqueries_ref,
):
    segments = segment_rows(seg_ref)
    listed_segments = product_nt(segments, pick_ref[...]).astype(LOW)
    same_seg = product_tn(listed_segments, segments) > 0.5
    width = first_ref.shape[1] // 3
    sums_ref[...] = jnp.zeros_like(sums_ref)

    def dot(left, right, left_dim, right_dim):
        return lax.dot_general(
            left,
            right,
            (((left_dim,), (right_dim,)), ((), ())),
            preferred_element_type=jnp.float32,
        )

    halves = (
        (0, first_ref, first_grad_ref, first_term_ref),
        (1, second_ref, second_grad_ref, second_term_ref),
    )
    for half, qkv_ref, dqkv_ref, term_ref in halves:
        for head in range(width // HDIM):
            lanes = slice(half * width + head * HDIM, half * width + (head + 1) * HDIM)
            keys = slice(width + head * HDIM, width + (head + 1) * HDIM)
            values = slice(2 * width + head * HDIM, 2 * width + (head + 1) * HDIM)
            query, grad = queries_ref[:, lanes], grad_ref[:, lanes]
            key, value = qkv_ref[:, keys], qkv_ref[:, values]
            listed = query.shape[0]
            zeros = jnp.zeros_like(query)
            left = jnp.concatenate(
                [jnp.concatenate([query, zeros], axis=1), jnp.concatenate([zeros, grad], axis=1)]
            )
            scores_dprobs = dot(left, jnp.concatenate([key, value], axis=1), 1, 1)
            scores = jnp.where(same_seg, scores_dprobs[:listed] * scale, MASK_FILL)
            exp_scores = jnp.exp(scores - jnp.max(scores, axis=-1, keepdims=True))
            probs = exp_scores / jnp.sum(exp_scores, axis=-1, keepdims=True)
            dprobs = scores_dprobs[listed:]
            dscores = probs * (dprobs - jnp.sum(probs * dprobs, axis=-1, keepdims=True))
            dscores = dscores.astype(LOW)
            dqueries_ref[:, lanes] = (dot(dscores, key, 1, 0) * scale).astype(LOW)
            dkeys_dvalues = dot(jnp.concatenate([dscores, probs.astype(LOW)]), left, 0, 0)
            dqkv_ref[:, keys] = (dkeys_dvalues[:, :HDIM] * scale).astype(LOW)
            dqkv_ref[:, values] = dkeys_dvalues[:, HDIM:].astype(LOW)
        lanes = slice(half * width, (half + 1) * width)
        dqkv_ref[:, :width] = dot(pick_ref[...], dqueries_ref[:, lanes], 0, 0).astype(LOW)
        term_ref[:, : 3 * width] = product(turned_ref[...], dqkv_ref[...]).astype(LOW)
        term_ref[:, 3 * width :] = beside_ref[:, 2 * half * width : 2 * (half + 1) * width]
        sums_ref[0:1, lanes] = jnp.sum(
            dqueries_ref[:, lanes].astype(jnp.float32), axis=0, keepdims=True
        )
        sums_ref[1:2, lanes] = jnp.sum(
            dqkv_ref[:, 2 * width :].astype(jnp.float32), axis=0, keepdims=True
        )


def attention_back(queries, first, second, grad, segment_ids, pick, turned, beside, others):
    listed = queries.shape[0]
    rows, width = first.shape
    term = (turned.shape[0], width + beside.shape[1] // 2)
    return call_after(
        functools.partial(attention_back_kernel, HDIM ** (-0.5)),
        others,
        [pl.BlockSpec(memory_space=pltpu.VMEM)] * 8,
        out_shape=[
            jax.ShapeDtypeStruct((rows, width), LOW),
            jax.ShapeDtypeStruct(term, LOW),
            jax.ShapeDtypeStruct((rows, width), LOW),
            jax.ShapeDtypeStruct(term, LOW),
            jax.ShapeDtypeStruct((8, queries.shape[1]), jnp.float32),
        ],
        scratch_shapes=[pltpu.VMEM(queries.shape, LOW)],
        compiler_params=pltpu.CompilerParams(vmem_limit_bytes=32 * 1024 * 1024),
        cost_estimate=pl.CostEstimate(
            flops=20 * listed * rows * width // 3 + 4 * turned.size * width,
            bytes_accessed=20 * rows * width // 3,
            transcendentals=2 * listed * rows * width // (3 * HDIM),
        ),
    )(queries, first, second, grad, segment_ids, pick, turned, beside)


def turn_row(row):
    return jnp.transpose(jnp.broadcast_to(row, (128, row.shape[1])))[:, 0:1]


def turn_column(column):
    return jnp.transpose(jnp.broadcast_to(column, (column.shape[0], 128)))[0:1, :]


def core_rows(words_ref, core):
    half = words_ref.shape[0] // 2
    mine = words_ref[pl.ds(pl.multiple_of(core * half, 128), half), :]
    other = words_ref[pl.ds(pl.multiple_of((1 - core) * half, 128), half), :]
    return mine, other


def logits_kernel(vocab_size, place_ref, mine_ref, other_ref, words_ref, bias_ref, logits_ref, log_ref):
    words_mine, words_other = core_rows(words_ref, place_ref[0])
    logits = product(mine_ref[...], words_mine) + product(other_ref[...], words_other) + bias_ref[...]
    ids = lax.broadcasted_iota(jnp.int32, logits.shape, 1) + place_ref[1]
    logits = jnp.where(ids < vocab_size, logits, MASK_FILL)
    logits_ref[...] = logits
    peak = jnp.max(logits, axis=1, keepdims=True)
    log_ref[...] = turn_column(
        peak + jnp.log(jnp.sum(jnp.exp(logits - peak), axis=1, keepdims=True))
    )


def dlogits_kernel(
    inv_count, place_ref, logits_ref, log_ref, labels_ref, words_ref, dlogits_ref, mine_ref, other_ref, sums_ref
):
    @pl.when(pl.program_id(0) == 0)
    def _():
        sums_ref[...] = jnp.zeros_like(sums_ref)

    logits = logits_ref[...]
    ids = lax.broadcasted_iota(jnp.int32, logits.shape, 1) + place_ref[1]
    is_label = ids.astype(jnp.float32) == turn_row(labels_ref[...])
    grads = jnp.exp(logits - turn_row(log_ref[...])) - jnp.where(is_label, 1.0, 0.0)
    grads = (grads * inv_count).astype(LOW)
    dlogits_ref[...] = grads
    words_mine, words_other = core_rows(words_ref, place_ref[0])
    other_ref[...] = product_nt(grads, words_other).astype(LOW)
    mine_ref[...] = product_nt(grads, words_mine).astype(LOW)
    sums_ref[0:1, :] += jnp.sum(grads.astype(jnp.float32), axis=0, keepdims=True)
    sums_ref[1:2, :] += jnp.sum(jnp.where(is_label, logits, 0.0), axis=0, keepdims=True)


def words_grad_kernel(place_ref, mine_ref, other_ref, dlogits_ref, grad_ref):
    half = mine_ref.shape[1]
    core = place_ref[0]
    grads = dlogits_ref[...]
    for spot, rows_ref in ((core, mine_ref), (1 - core, other_ref)):
        lanes = pl.ds(pl.multiple_of(spot * half, 128), half)
        grad_ref[lanes, :] = product_tn(rows_ref[...], grads).astype(LOW)


def row_blocks(slots):
    rows = min(256, slots)
    return (
        slots // rows,
        lambda width: pl.BlockSpec((rows, width), lambda step: (step, 0)),
        pl.BlockSpec((1, rows), lambda step: (0, step)),
    )


def whole_block(*shape):
    return pl.BlockSpec(shape, lambda step: (0,) * len(shape))


def part_logits(place, mine, other, words, bias, vocab_size):
    slots, half = mine.shape
    width = words.shape[1]
    steps, rows_of, line = row_blocks(slots)
    return pl.pallas_call(
        functools.partial(logits_kernel, vocab_size),
        grid=(steps,),
        in_specs=[
            pl.BlockSpec(memory_space=pltpu.SMEM),
            rows_of(half),
            rows_of(half),
            whole_block(2 * half, width),
            whole_block(1, width),
        ],
        out_specs=[rows_of(width), line],
        out_shape=[
            jax.ShapeDtypeStruct((slots, width), jnp.float32),
            jax.ShapeDtypeStruct((1, slots), jnp.float32),
        ],
        compiler_params=pltpu.CompilerParams(vmem_limit_bytes=24 * 1024 * 1024),
        cost_estimate=pl.CostEstimate(
            flops=4 * slots * half * width,
            bytes_accessed=4 * slots * width + 4 * half * (slots + width),
            transcendentals=slots * width,
        ),
    )(place, mine, other, words, bias)


def part_dlogits(place, logits, log_total, labels, words, inv_count):
    slots, width = logits.shape
    half = words.shape[0] // 2
    steps, rows_of, line = row_blocks(slots)
    return pl.pallas_call(
        functools.partial(dlogits_kernel, inv_count),
        grid=(steps,),
        in_specs=[
            pl.BlockSpec(memory_space=pltpu.SMEM),
            rows_of(width),
            line,
            line,
            whole_block(2 * half, width),
        ],
        out_specs=[rows_of(width), rows_of(half), rows_of(half), whole_block(8, width)],
        out_shape=[
            jax.ShapeDtypeStruct((slots, width), LOW),
            jax.ShapeDtypeStruct((slots, half), LOW),
            jax.ShapeDtypeStruct((slots, half), LOW),
            jax.ShapeDtypeStruct((8, width), jnp.float32),
        ],
        compiler_params=pltpu.CompilerParams(vmem_limit_bytes=24 * 1024 * 1024),
        cost_estimate=pl.CostEstimate(
            flops=4 * slots * half * width,
            bytes_accessed=6 * slots * width + 4 * half * (slots + width),
            transcendentals=slots * width,
        ),
    )(place, logits, log_total, labels, words)


def part_words_grad(place, mine, other, dlogits):
    slots, half = mine.shape
    width = dlogits.shape[1]
    return pl.pallas_call(
        words_grad_kernel,
        in_specs=[pl.BlockSpec(memory_space=pltpu.SMEM)] + [pl.BlockSpec(memory_space=pltpu.VMEM)] * 3,
        out_shape=jax.ShapeDtypeStruct((2 * half, width), LOW),
        compiler_params=pltpu.CompilerParams(vmem_limit_bytes=32 * 1024 * 1024),
        cost_estimate=pl.CostEstimate(
            flops=4 * slots * half * width,
            bytes_accessed=2 * slots * width + 4 * half * (slots + width),
            transcendentals=0,
        ),
    )(place, mine, other, dlogits)


def heads_of(rows):
    return rows.reshape(rows.shape[0], rows.shape[1] // HDIM, HDIM)


def attention_probs(queries, key_rows, query_seg, key_seg):
    scores = jnp.einsum(
        "qhd,khd->hqk", queries, key_rows, preferred_element_type=jnp.float32
    ) * HDIM ** (-0.5)
    same_seg = query_seg[:, None] == key_seg[None, :]
    masked = jnp.where(same_seg[None], scores, MASK_FILL)
    row_peak = jnp.max(masked, axis=-1, keepdims=True)
    exp_scores = jnp.exp(masked - row_peak)
    return exp_scores / jnp.sum(exp_scores, axis=-1, keepdims=True)


def per_device(
    tokens,
    segment_ids,
    mlm_labels,
    mask_order,
    mask_count,
    qkv_weight,
    query_bias,
    value_bias,
    out_weight,
    out_bias,
    attn_gain,
    attn_shift,
    up_weight,
    up_bias,
    down_weight,
    down_bias,
    ffn_gain,
    ffn_shift,
    head_weight,
    head_bias,
    head_gain,
    head_shift,
    decoder,
    decoder_bias,
):
    model_width = tokens.shape[1]
    tok_rows = tokens.shape[0]
    vocab_size = decoder.shape[1]
    bal_size = lax.axis_size("bal")
    dp_size = lax.axis_size("dp")
    bal_place = lax.axis_index("bal")
    dp_place = lax.axis_index("dp")
    grid = Grid(dp_size, bal_size)
    device_count = dp_size * bal_size
    my_place = dp_place * bal_size + bal_place
    slot_count = HEAD_DEV * device_count
    inv_count = 1.0 / slot_count
    part_vocab = -(-(-(-vocab_size // device_count)) // 128) * 128

    listed = mask_order[0, :MASK_DEV]
    pick_mat = listed[:, None] == jnp.arange(tok_rows)[None, :]
    pick_low = pick_mat.astype(LOW)

    def pick(rows):
        return product(pick_low, rows).astype(LOW)

    listed_ids = jnp.sum(jnp.where(pick_mat, mlm_labels[None, :], 0), axis=1)

    shard_rows = qkv_weight.shape[0]
    my_units = down_weight.shape[0]
    units = my_units * device_count
    ratio = my_units // shard_rows
    half = model_width // 2

    def unit_order(rows):
        split = rows.reshape(rows.shape[0], device_count, ratio, shard_rows)
        return split.transpose(0, 2, 1, 3).reshape(rows.shape[0], units)

    down_wide = down_weight.reshape(ratio, shard_rows, model_width).transpose(1, 0, 2)
    down_wide = down_wide.reshape(shard_rows, ratio * model_width)
    packed = lax.all_gather(
        jnp.concatenate([unit_order(up_weight), down_wide], axis=1), AXES, axis=0, tiled=True
    )
    up_offsets = unit_order(up_bias[None])[0]
    my_offsets = lax.dynamic_slice_in_dim(up_bias, my_place * my_units, my_units)

    def by_heads(rows):
        split = rows.reshape(rows.shape[0], 3, 2, half)
        return grid.halves(
            split[:, :, 0].reshape(rows.shape[0], 3 * half),
            split[:, :, 1].reshape(rows.shape[0], 3 * half),
        )

    info = jnp.concatenate([listed_ids, mask_count, jnp.zeros((63,), jnp.int32)])
    info = grid.gather_group(info[None])
    weights_run = Transfer(by_heads(qkv_weight), grid.gather_steps(shard_rows))
    both_run = Transfer(grid.halves(out_weight, head_weight), grid.gather_steps(shard_rows))
    qkv_width = 3 * half
    weights_run.step()
    weights_run.step()
    weights_run.step()
    all_mine, all_other = weights_run.finish()
    both_run.step()

    info = jnp.concatenate(info)
    group = jnp.stack(grid.group())
    counts = info[:, MASK_DEV]
    before = group[None, :] < group[:, None]
    starts = jnp.sum(jnp.where(before, counts[None, :], 0), axis=1)
    steps = jnp.arange(MASK_DEV)
    slot_of = jnp.where(steps[None] < counts[:, None], starts[:, None] + steps[None], -1)
    my_slots = bal_place * HEAD_DEV + jnp.arange(HEAD_DEV)
    is_mine = slot_of[None] == my_slots[:, None, None]
    my_labels = jnp.sum(jnp.where(is_mine, info[None, :, :MASK_DEV], 0), axis=(1, 2))
    to_head = is_mine.astype(LOW)
    group_slots = group[:, None] * HEAD_DEV + jnp.arange(HEAD_DEV)[None, :]
    from_head = (slot_of[0][:, None, None] == group_slots[None]).astype(LOW)

    def choose(choice, parts):
        total = product(choice[:, 0], parts[0])
        for index, part in enumerate(parts[1:], 1):
            total = total + product(choice[:, index], part)
        return total.astype(LOW)

    tokens_s = pick(tokens)

    bias_mine, bias_other = by_heads(
        jnp.concatenate([query_bias, jnp.zeros_like(query_bias), value_bias])[None]
    )
    parts_mine, context_mine = attention(
        tokens, all_mine, bias_mine, segment_ids, []
    )
    padded = lax.pad(
        decoder,
        nothing(context_mine).astype(LOW),
        ((0, 0, 0), (0, part_vocab * device_count - vocab_size, 0)),
    )
    padded = padded.reshape(decoder.shape[0], device_count, part_vocab).transpose(1, 0, 2)
    parts_other, context_other = attention(tokens, all_other, bias_other, segment_ids, [context_mine])
    both_run.step(context_mine)
    both_run.step()
    both_run.step(context_other)
    out_full, head_full = grid.halves(*both_run.finish())
    context = jnp.concatenate(grid.halves(context_mine, context_other), axis=1)
    words = lax.all_to_all(padded, AXES, split_axis=0, concat_axis=0, tiled=True)

    picked = [tokens_s, *grid.halves(pick(context_mine), pick(context_other))]
    group_rows = grid.gather_group(jnp.concatenate(picked, axis=1))
    listed_queries = jnp.concatenate(
        [pick(parts_mine[:, :half]), pick(parts_other[:, :half])], axis=1
    )
    slot_rows = choose(to_head, group_rows)
    tokens_own, context_own = slot_rows[:, :model_width], slot_rows[:, model_width:]
    vectors = jnp.stack(
        [out_bias, attn_gain, attn_shift, down_bias, ffn_gain, ffn_shift, out_bias, out_bias]
    )
    window = min(256, model_width)
    begin = jnp.minimum(my_place * shard_rows // 128 * 128, model_width - window)
    lanes = jnp.arange(window)[:, None] + begin - my_place * shard_rows
    unit_ids = np.arange(my_units)
    my_columns = jnp.zeros((model_width, my_units), jnp.float32)
    for block in range(ratio):
        piece = lax.dynamic_slice_in_dim(packed, block * model_width + begin, window, 1)
        wanted = np.where(unit_ids // shard_rows == block, unit_ids % shard_rows, -model_width)
        is_unit = lanes == jnp.asarray(wanted, jnp.int32)[None, :]
        my_columns = my_columns + product(piece, is_unit.astype(LOW))
    my_columns = my_columns.astype(LOW)


    def layer_part(part, others, room, into=None):
        return feed_forward(
            context, tokens, out_full, vectors, packed, up_offsets, others, room, part, 2, into
        )[0]

    head_in, normed_own, resid_one, resid_two = feed_forward(
        context_own, tokens_own, out_full, vectors, packed, up_offsets, [listed_queries], 24
    )

    rows_all = lax.all_gather(normed_own, AXES, axis=0, tiled=True)
    up_all = product(rows_all, my_columns) + my_offsets

    inner_rows = product(head_in, head_full) + head_bias
    head_act, act_back = jax.vjp(gelu_exact, inner_rows)
    head_normal, head_inv = norm_parts(head_act)
    head_normed = (head_normal * head_gain + head_shift).astype(LOW)
    head_run = Transfer(
        grid.halves(head_normed[:, :half], head_normed[:, half:]), grid.gather_steps(HEAD_DEV)
    )
    head_run.step(lax.dynamic_slice(words, (nothing(head_in), 0, 0), (1, 1, 1)))
    head_run.step()
    head_run.step()
    head_run.step()
    normed_mine, normed_other = head_run.finish()
    words = words.reshape(model_width, part_vocab)
    padded_bias = jnp.pad(decoder_bias, (0, part_vocab * device_count - vocab_size))
    words_bias = lax.dynamic_slice_in_dim(padded_bias, my_place * part_vocab, part_vocab)
    place = jnp.stack([grid.place[3], my_place * part_vocab]).astype(jnp.int32)
    logits, part_log = part_logits(
        place, normed_mine, normed_other, words, words_bias[None], vocab_size
    )
    spread = jnp.concatenate(
        [part_log[0], my_labels.astype(jnp.float32), jnp.zeros((128 - HEAD_DEV,), jnp.float32)]
    )
    spread = jnp.broadcast_to(spread[None, None], (device_count, 1, slot_count + 128))
    spread = lax.all_to_all(spread, AXES, split_axis=0, concat_axis=0, tiled=True)
    spread = spread[:, 0]
    all_logs = spread[:, :slot_count]
    labels = spread[:, slot_count : slot_count + HEAD_DEV].reshape(1, slot_count)
    peak = jnp.max(all_logs, axis=0)
    log_total = peak + jnp.log(jnp.sum(jnp.exp(all_logs - peak), axis=0))
    dlogits, dhead_mine, dhead_other, logit_sums = part_dlogits(
        place, logits, log_total[None], labels, words, inv_count
    )
    head_run = Transfer((dhead_mine, dhead_other), grid.scatter_steps(HEAD_DEV))
    words_grad = part_words_grad(place, normed_mine, normed_other, dlogits)
    head_run.step()
    head_run.step()
    head_run.step()
    head_run.step()
    words_bias_grad = logit_sums[0]
    target_part = jnp.sum(logit_sums[1])
    loss_part = jnp.where(my_place == 0, jnp.sum(log_total), 0.0) - target_part
    dhead_normed = jnp.concatenate(grid.halves(*head_run.finish()), axis=1).astype(jnp.float32)
    dhead_act, head_gain_part, head_shift_part = norm_back(
        head_normal, head_inv, head_gain, dhead_normed
    )
    dinner = act_back(dhead_act)[0].astype(LOW)
    head_bias_part = jnp.sum(dinner, axis=0, dtype=jnp.float32)
    dhead_in = product_nt(dinner, head_full).astype(LOW)

    words_back = lax.all_to_all(
        words_grad.reshape(device_count, decoder.shape[0], part_vocab),
        AXES,
        split_axis=0,
        concat_axis=0,
        tiled=True,
    )

    loss_high = loss_part.astype(LOW).astype(jnp.float32)
    vocab_rows = jnp.pad(words_bias_grad, (0, 2 * model_width - part_vocab))
    more = jnp.stack(
        [
            head_bias_part,
            head_gain_part,
            head_shift_part,
            jnp.where(jnp.arange(model_width) < half, loss_high, loss_part - loss_high),
            vocab_rows[:model_width],
            vocab_rows[model_width:],
            head_bias_part,
            head_bias_part,
        ]
    )
    send, dresid_own = feed_back(
        dhead_in, resid_one, resid_two, normed_own, vectors, more, packed, up_offsets, [up_all, words_grad]
    )
    group_grads = grid.gather_group(dresid_own)
    factors = lax.all_gather(send, AXES, axis=0, tiled=True)

    def two_parts(rows):
        high = rows.astype(LOW)
        return jnp.concatenate([high, (rows - high.astype(jnp.float32)).astype(LOW)])

    out_term = product_tn(context_own, dresid_own).astype(LOW)
    head_term = product_tn(head_in, dinner).astype(LOW)
    beside = jnp.concatenate(grid.halves(out_term, head_term), axis=1)
    dresid_one = choose(from_head, group_grads)
    dcontext = product_nt(dresid_one, out_full).astype(LOW)
    dcontext = jnp.concatenate(grid.halves(dcontext[:, :half], dcontext[:, half:]), axis=1)
    dqkv_mine, mine_term, dqkv_other, other_term, qkv_sums = attention_back(
        listed_queries,
        parts_mine,
        parts_other,
        dcontext,
        segment_ids,
        pick_low,
        tokens.T,
        beside,
        [],
    )
    other_taken = grid.shift(other_term, (3, 3), 1)
    weights_run = Transfer((mine_term, None), grid.scatter_steps(shard_rows, other_taken))
    weights_run.step(words_back)
    first_part = layer_part(0, [grid.sent], 24)
    weights_run.step(first_part)
    second_part = layer_part(1, [grid.sent], 24, first_part)
    qkv_sums = grid.halves(qkv_sums[:2, :half], qkv_sums[:2, half:])
    qkv_sums = two_parts(jnp.concatenate(qkv_sums, axis=1))

    ddown_all = factors[:, :model_width]
    hidden, act_back = jax.vjp(gelu_exact, up_all)
    dup_all = act_back(product_nt(ddown_all, down_weight))[0].astype(LOW)
    up_term = product_tn(rows_all, dup_all).astype(LOW).reshape(device_count, shard_rows, my_units)
    weights_run.step(second_part)
    words_back = once(words_back, grid.sent)
    qkv_sums = qkv_sums.reshape(-1, my_units)
    qkv_sums = jnp.broadcast_to(qkv_sums[None], (device_count, *qkv_sums.shape))
    up_back = lax.all_to_all(
        jnp.concatenate([up_term, qkv_sums], axis=1), AXES, split_axis=0, concat_axis=0, tiled=True
    )
    down_grad = product_tn(hidden.astype(LOW), ddown_all)
    up_grad = up_back[:, :shard_rows].transpose(1, 0, 2).reshape(shard_rows, units)
    up_grad = up_grad.astype(jnp.float32)
    qkv_sums = jnp.sum(up_back[:, shard_rows:].astype(jnp.float32), axis=0)
    qkv_sums = jnp.sum(qkv_sums.reshape(2, 2, model_width), axis=0)

    tokens_grad = product_tn(pick_low, once(dresid_one, weights_run.part[0][-1]))
    tokens_grad = tokens_grad + product_nt(dqkv_other, all_other)
    tokens_grad = tokens_grad + product_nt(dqkv_mine, all_mine)
    weights_run.step()
    mine, other = weights_run.finish()
    sums = factors[:, model_width:].astype(jnp.float32).reshape(device_count, 2, 16, half)
    sums = jnp.concatenate([sums[:, 0], sums[:, 1]], axis=2)
    decoder_bias_grad = sums[:, 4:6].reshape(device_count, 2 * model_width)[:, :part_vocab]
    decoder_bias_grad = decoder_bias_grad.reshape(-1)[:vocab_size]
    sums = jnp.sum(sums, axis=0)
    up_sums = sums[12:].reshape(ratio, device_count, shard_rows).transpose(1, 0, 2).reshape(-1)
    first, second = grid.halves(mine[:, :qkv_width], other[:, :qkv_width])
    qkv_grad = jnp.stack(
        [first.reshape(shard_rows, 3, half), second.reshape(shard_rows, 3, half)], axis=2
    )
    qkv_grad = qkv_grad.reshape(shard_rows, 3 * model_width).astype(jnp.float32)
    out_grad, head_grad = grid.halves(mine[:, qkv_width:], other[:, qkv_width:])
    decoder_grad = words_back.transpose(1, 0, 2).reshape(decoder.shape[0], -1)
    decoder_grad = decoder_grad[:, :vocab_size].astype(jnp.float32)
    return (
        second_part,
        (sums[3, 0] + sums[3, half]) * inv_count,
        tokens_grad,
        qkv_grad,
        qkv_sums[0],
        qkv_sums[1],
        out_grad.astype(jnp.float32),
        sums[11],
        sums[9],
        sums[10],
        up_grad,
        up_sums,
        down_grad,
        sums[8],
        sums[6],
        sums[7],
        head_grad.astype(jnp.float32),
        sums[0],
        sums[1],
        sums[2],
        decoder_grad,
        decoder_bias_grad,
    )


def solution(mesh):
    cut, rows = P(("dp", "bal"), None), P(("dp", "bal"))
    whole = P()
    return jax.shard_map(
        per_device,
        mesh=mesh,
        in_specs=(
            cut, cut, rows, cut, rows, cut, whole, whole, cut, whole, whole, whole,
            cut, whole, cut, whole, whole, whole, cut, whole, whole, whole, cut, whole,
        ),
        out_specs=(
            cut, whole, cut, cut, whole, whole, cut, whole, whole, whole, cut,
            whole, cut, whole, whole, whole, cut, whole, whole, whole, cut, whole,
        ),
        check_vma=False,
    )
```
